128 devices in a mesh: section: 2 (over x_hi), batch: 64 (over x_lo, z, y, core).
Axes of the slice: x: 4 (x_hi: 2, x_lo: 2; x = x_hi * 2 + x_lo), y: 4, z: 4, core: 2. Of those that a mesh axis runs over, the one named last changes fastest.
Arguments:
- inputs: bfloat16 [65536, 384], P('batch'), may hold values from -6 to 6
- cotangent: bfloat16 [65536, 384], P('batch'), may hold values from -6 to 6
- text: bfloat16 [16384, 384], P('batch'), may hold values from -6 to 6
- text_mask: int32 [16384], P('batch'), may hold values from 0 to 1, as said below
- segments: int32 [65536], P('batch'), may hold values from 0 to 1, as said below
- time_index: int32 [256], P('batch'), may hold values from 0 to 999
- time_table: bfloat16 [1000, 384], replicated, may hold values from -6 to 6
- w_qkv: bfloat16 [2, 384, 1152], P('section'), may hold values from -0.3125 to 0.3125
- w_out: bfloat16 [2, 384, 384], P('section'), may hold values from -0.625 to 0.625
- w_query: bfloat16 [2, 384, 384], P('section'), may hold values from -0.3125 to 0.3125
- w_keyval: bfloat16 [2, 384, 768], P('section'), may hold values from -0.3125 to 0.3125
- w_cross: bfloat16 [2, 384, 384], P('section'), may hold values from -0.625 to 0.625
- w_up: bfloat16 [2, 384, 1536], P('section'), may hold values from -0.3125 to 0.3125
- w_down: bfloat16 [2, 1536, 384], P('section'), may hold values from -0.15625 to 0.15625
- w_ada: bfloat16 [2, 384, 2304], P('section'), may hold values from -0.3125 to 0.3125
- b_ada: float32 [2, 2304], P('section'), may hold values from -1 to 1
Outputs:
- activations: bfloat16 [2, 65536, 384], P('section', 'batch')
- input_grads: float32 [2, 65536, 384], P('section', 'batch')
- text_grad: float32 [16384, 384], P('batch')
- table_grad: float32 [1000, 384], replicated
- g_qkv: float32 [2, 384, 1152], P('section')
- g_out: float32 [2, 384, 384], P('section')
- g_query: float32 [2, 384, 384], P('section')
- g_keyval: float32 [2, 384, 768], P('section')
- g_cross: float32 [2, 384, 384], P('section')
- g_up: float32 [2, 384, 1536], P('section')
- g_down: float32 [2, 1536, 384], P('section')
- g_ada: float32 [2, 384, 2304], P('section')
- g_bias: float32 [2, 2304], P('section')
The draws below stay inside these ranges and needn't reach their ends.
Inputs may be any that keep to these rules, and one draw needn't show every extreme that they name: `segments`: each clip of 512 tokens holds exactly 2 videos, numbered 0 to 1 in order, each made of whole consecutive frames; the number is constant over a frame's 128 tokens. `text_mask`: each video's 64 text rows are 1 up to its caption length, 1 to 64, and 0 after it.
All inputs are finite; a program needn't handle non-finite values.
Results may differ from the reference program's by a relative error of at most 0.024.
Values may be sent and summed in bfloat16 or wider, within the bound.
No kernel may reach another device: no remote copies, remote signals or barrier semaphores. Data moves between devices by JAX's collectives and lax.ppermute only.
A program may use at most 192 MiB of HBM per device.

```python
import jax
import jax.numpy as jnp
from jax import lax

D = 384
HEADS = 6
HEAD = 64
FF = 1536
PATCHES = 128
FRAMES = 4
VIDS = 2
TXT = 64
STEPS = 1000
LAYERS = 2
CLIPS = 128
TOKENS = 65536
VIDEOS = 256
TEXTROWS = 16384


def draw_segments(key, part):
    key = jax.random.fold_in(key, 11)
    clip_keys = jax.random.split(key, CLIPS)

    def clip_segments(clip_key):
        boundaries = jax.random.permutation(clip_key, FRAMES - 1)[:VIDS - 1] + 1
        frame_ids = jnp.arange(FRAMES)
        frame_owner = jnp.sum((boundaries[None, :] <= frame_ids[:, None]).astype(jnp.int32), axis=1)
        return jnp.repeat(frame_owner, PATCHES, total_repeat_length=FRAMES * PATCHES)
    return jax.vmap(clip_segments)(clip_keys).reshape(-1).astype(jnp.int32)


def draw_text_mask(key, part):
    key = jax.random.fold_in(key, 12)
    lengths = jax.random.randint(key, (VIDEOS,), 1, TXT + 1)
    positions = jnp.arange(TXT)
    return (positions[None, :] < lengths[:, None]).astype(jnp.int32).reshape(-1)


def touch_ends(drawn, own_key, least, high):
    spot = [jax.random.randint(jax.random.fold_in(own_key, axis), (), 0, length) for axis, length in enumerate(drawn.shape)]
    longest = drawn.shape.index(max(drawn.shape))
    neighbour = spot[:longest] + [(spot[longest] + 1) % drawn.shape[longest]] + spot[longest + 1:]
    return drawn.at[tuple(spot)].set(least).at[tuple(neighbour)].set(high)


def level_of(own_key, dims, shards, smallest, high):
    def one(dim, shards_of):
        steps = jax.random.uniform(jax.random.fold_in(jax.random.fold_in(own_key, 6), dim), (shards_of,), jnp.float32, smallest / len(shards), high / len(shards))
        return jnp.repeat(jnp.exp(steps), dims[dim] // shards_of).reshape((-1,) + (1,) * (len(dims) - dim - 1))

    level = one(*shards[0])
    for cut in shards[1:]:
        level = level * one(*cut)
    return level


def centred(own_key, extent, deviation, bound, cuts=(), dtype=jnp.bfloat16):
    entries = deviation * jax.random.normal(own_key, extent, jnp.float32)
    if cuts:
        entries = entries * level_of(own_key, extent, cuts, -0.22, 0.18)
    return jnp.clip(entries, -bound, bound).astype(dtype)


def setup_inputs(seed: int = 0) -> dict:
    streams_of = jax.random.split(jax.random.key(seed), 17)
    inputs = centred(streams_of[0], (TOKENS, D), 1.0, 6.0, ((0, 64),))
    cotangent = centred(streams_of[1], (TOKENS, D), 1.0, 6.0, ((0, 64),))
    text = centred(streams_of[2], (TEXTROWS, D), 1.0, 6.0, ((0, 64),))
    text_mask = draw_text_mask(jax.random.fold_in(streams_of[16], 71), 0)
    segments = draw_segments(jax.random.fold_in(streams_of[16], 71), 0)
    time_index = touch_ends(jax.random.randint(streams_of[5], (VIDEOS,), 0, STEPS), jax.random.fold_in(streams_of[5], 1), 0, STEPS - 1).astype(jnp.int32)
    time_table = centred(streams_of[6], (STEPS, D), 1.0, 6.0)
    w_qkv = centred(streams_of[7], (LAYERS, D, 3 * D), D ** -0.5, 0.3125, ((0, 2),))
    w_out = centred(streams_of[8], (LAYERS, D, D), (D // 4) ** -0.5, 0.625, ((0, 2),))
    w_query = centred(streams_of[9], (LAYERS, D, D), D ** -0.5, 0.3125, ((0, 2),))
    w_keyval = centred(streams_of[10], (LAYERS, D, 2 * D), D ** -0.5, 0.3125, ((0, 2),))
    w_cross = centred(streams_of[11], (LAYERS, D, D), (D // 4) ** -0.5, 0.625, ((0, 2),))
    w_up = centred(streams_of[12], (LAYERS, D, FF), D ** -0.5, 0.3125, ((0, 2),))
    w_down = centred(streams_of[13], (LAYERS, FF, D), FF ** -0.5, 0.15625, ((0, 2),))
    w_ada = centred(streams_of[14], (LAYERS, D, 6 * D), D ** -0.5, 0.3125, ((0, 2),))
    b_ada = jnp.clip(jax.random.uniform(streams_of[15], (LAYERS, 6 * D), jnp.float32, -1.0, 1.0) * level_of(streams_of[15], (LAYERS, 6 * D), ((0, 2),), -0.4, 0.0), -1.0, 1.0)
    return dict(inputs=inputs, cotangent=cotangent, text=text, text_mask=text_mask, segments=segments, time_index=time_index, time_table=time_table, w_qkv=w_qkv, w_out=w_out, w_query=w_query, w_keyval=w_keyval, w_cross=w_cross, w_up=w_up, w_down=w_down, w_ada=w_ada, b_ada=b_ada)


SCORE_SCALE = 0.125
NEGATIVE = -1000000000.0
EPSILON = 1e-06

@jax.custom_vjp
def low(v):
    return lax.optimization_barrier(v.astype(jnp.bfloat16)).astype(jnp.float32)

@jax.custom_vjp
def low_back(v):
    return v

def low_keep(v):
    return (low(v), None)

def low_pass(kept, grad):
    return (grad,)

def back_keep(v):
    return (v, None)

def back_low(kept, grad):
    return (low(grad),)
low.defvjp(low_keep, low_pass)
low_back.defvjp(back_keep, back_low)

def exact_dot(left, right):
    return jnp.dot(left, right, precision=lax.Precision.HIGHEST)

def layer_norm(tensor):
    centre = tensor - lax.optimization_barrier(jnp.mean(tensor, axis=-1, keepdims=True))
    return centre * lax.rsqrt(lax.optimization_barrier(jnp.mean(centre * centre, axis=-1, keepdims=True)) + EPSILON)

def modulate(tensor, shift_by, scale_by):
    return layer_norm(tensor) * (1.0 + scale_by) + shift_by

def lookups(segment_rows, time_slots, text_marks, temporal):
    length = segment_rows.shape[0]
    position = jnp.arange(length)
    frame_of = position // PATCHES
    patch_of = position % PATCHES
    if temporal:
        self_mask = (patch_of[:, None] == patch_of[None, :]) & (segment_rows[:, None] == segment_rows[None, :])
    else:
        self_mask = frame_of[:, None] == frame_of[None, :]
    text_owner = jnp.arange(text_marks.shape[0]) // TXT
    cross_mask = (segment_rows[:, None] == text_owner[None, :]) & (text_marks[None, :] == 1)
    tok_onehot = (segment_rows[:, None] == jnp.arange(VIDS)[None, :]).astype(jnp.float32)
    time_onehot = (time_slots[:, None] == jnp.arange(STEPS)[None, :]).astype(jnp.float32)
    return (self_mask, cross_mask, tok_onehot, time_onehot)

def attend(query_heads, key_heads, value_heads, allowed):
    scores = low_back(jnp.einsum('qhe,khe->hqk', query_heads, key_heads, precision=lax.Precision.HIGHEST))
    logits = jnp.where(allowed[None], scores * SCORE_SCALE, NEGATIVE)
    probs_low = low(jax.nn.softmax(logits, axis=-1))
    return low_back(low(jnp.einsum('hqk,khe->qhe', probs_low, value_heads, precision=lax.Precision.HIGHEST)))

def latte_block(block_input, segment_rows, time_slots, text_rows, text_marks, table, weights, temporal):
    w_qkv, w_out, w_query, w_keyval, w_cross, w_up, w_down, w_ada, b_ada = weights
    length, features = block_input.shape
    self_mask, cross_mask, tok_onehot, time_onehot = lookups(segment_rows, time_slots, text_marks, temporal)
    time_rows = exact_dot(time_onehot, table)
    act_time = low(jax.nn.silu(time_rows))
    mod_video = low_back(exact_dot(act_time, w_ada)) + b_ada
    modulation = exact_dot(tok_onehot, mod_video)
    shift_attend, scale_attend, gate_attend, shift_feed, scale_feed, gate_feed = jnp.split(modulation, 6, axis=1)
    normed_one = low(modulate(block_input, shift_attend, scale_attend))
    qkv = low_back(low(exact_dot(normed_one, w_qkv))).reshape(length, 3, HEADS, HEAD)
    self_mixed = attend(qkv[:, 0], qkv[:, 1], qkv[:, 2], self_mask).reshape(length, features)
    after_attend = block_input + gate_attend * low_back(exact_dot(self_mixed, w_out))
    normed_two = low(layer_norm(after_attend))
    cross_query = low_back(low(exact_dot(normed_two, w_query))).reshape(length, HEADS, HEAD)
    text_kv = low_back(low(exact_dot(text_rows, w_keyval))).reshape(-1, 2, HEADS, HEAD)
    cross_mixed = attend(cross_query, text_kv[:, 0], text_kv[:, 1], cross_mask).reshape(length, features)
    after_cross = after_attend + low_back(exact_dot(cross_mixed, w_cross))
    normed_three = low(modulate(after_cross, shift_feed, scale_feed))
    hidden = low_back(exact_dot(normed_three, w_up))
    activated = low(jax.nn.gelu(hidden, approximate=True))
    return after_cross + gate_feed * low_back(exact_dot(activated, w_down))

def reference(inputs, cotangent, text, text_mask, segments, time_index, time_table, w_qkv, w_out, w_query, w_keyval, w_cross, w_up, w_down, w_ada, b_ada):
    clip_rows = FRAMES * PATCHES
    clip_count = inputs.shape[0] // clip_rows
    features = inputs.shape[1]
    params = tuple((member.astype(jnp.float32) for member in (w_qkv, w_out, w_query, w_keyval, w_cross, w_up, w_down, w_ada, b_ada)))
    segment_blocks = segments.reshape(clip_count, clip_rows)
    time_blocks = time_index.reshape(clip_count, VIDS)
    mark_blocks = text_mask.reshape(clip_count, VIDS * TXT)

    def forward_all(x_in, text_in, table_in, weights, probes):
        text_blocks = text_in.reshape(clip_count, VIDS * TXT, features)
        current = x_in
        between = []
        for layer_index in range(LAYERS):
            layer_weights = tuple((member[layer_index] for member in weights))
            temporal = layer_index % 2 == 1

            def run_clip(pieces, layer_weights=layer_weights, temporal=temporal):
                x_clip, seg_clip, time_clip, text_clip, mark_clip = pieces
                return latte_block(x_clip, seg_clip, time_clip, text_clip, mark_clip, table_in, layer_weights, temporal)
            layer_out = lax.map(jax.checkpoint(run_clip), (current.reshape(clip_count, clip_rows, features), segment_blocks, time_blocks, text_blocks, mark_blocks)).reshape(-1, features)
            if layer_index < LAYERS - 1:
                layer_out = low_back(low(layer_out) + probes[layer_index])
                between.append(layer_out)
            current = layer_out
        return (current, jnp.stack(between))
    probes = jnp.zeros((LAYERS - 1, inputs.shape[0], features), jnp.float32)
    (last_out, between), pullback = jax.vjp(forward_all, inputs.astype(jnp.float32), text.astype(jnp.float32), time_table.astype(jnp.float32), params, probes)
    d_inputs, d_text, d_table, d_params, d_probes = pullback((cotangent.astype(jnp.float32), jnp.zeros_like(between)))
    activations = jnp.concatenate([between, last_out[None]], axis=0).astype(jnp.bfloat16)
    input_grads = jnp.concatenate([d_inputs[None], d_probes], axis=0)
    return (activations, input_grads, d_text, d_table, d_params[0], d_params[1], d_params[2], d_params[3], d_params[4], d_params[5], d_params[6], d_params[7], d_params[8])
```

```python
from types import SimpleNamespace

import jax
import jax.numpy as jnp
from jax import lax
from jax.sharding import PartitionSpec as P

HEADS = 6
HEAD = 64
PATCHES = 128
FRAMES = 4
VIDS = 2
TXT = 64
MICRO = 2
STEPS = 1000


SCORE_SCALE = 0.125
NEGATIVE = -1000000000.0
EPSILON = 1e-06


def shifted(value, axis, steps):
    count = lax.axis_size(axis)
    first, last = (max(0, -steps), min(count, count - steps))
    return lax.ppermute(value, axis, [(source, source + steps) for source in range(first, last)])


def layer_norm(tensor):
    centre = tensor - jnp.mean(tensor, axis=-1, keepdims=True)
    return centre * lax.rsqrt(jnp.mean(centre * centre, axis=-1, keepdims=True) + EPSILON)


def modulate(tensor, shift_by, scale_by):
    return layer_norm(tensor) * (1.0 + scale_by) + shift_by


def gelu_tanh(tensor):
    return jax.nn.gelu(tensor, approximate=True)


def lookups(segment_rows, time_slots, text_marks, temporal):
    length = segment_rows.shape[0]
    position = jnp.arange(length)
    frame_of = position // PATCHES
    patch_of = position % PATCHES
    same_frame = frame_of[:, None] == frame_of[None, :]
    same_video = (patch_of[:, None] == patch_of[None, :]) & (
        segment_rows[:, None] == segment_rows[None, :]
    )
    self_mask = jnp.where(temporal, same_video, same_frame)
    text_owner = jnp.arange(text_marks.shape[0]) // TXT
    cross_mask = (segment_rows[:, None] == text_owner[None, :]) & (text_marks[None, :] == 1)
    tok_onehot = (segment_rows[:, None] == jnp.arange(VIDS)[None, :]).astype(jnp.float32)
    time_onehot = (time_slots[:, None] == jnp.arange(STEPS)[None, :]).astype(jnp.float32)
    return (self_mask, cross_mask, tok_onehot, time_onehot)


def attend(query_heads, key_heads, value_heads, allowed):
    scores = jnp.einsum("qhe,khe->hqk", query_heads, key_heads, preferred_element_type=jnp.float32)
    logits = jnp.where(allowed[None], scores * SCORE_SCALE, NEGATIVE)
    probs = jax.nn.softmax(logits, axis=-1)
    mixed_heads = jnp.einsum(
        "hqk,khe->qhe", probs.astype(jnp.bfloat16), value_heads, preferred_element_type=jnp.float32
    )
    return (probs, mixed_heads.astype(jnp.bfloat16))


def attend_back(query_heads, key_heads, value_heads, probs, d_mixed):
    d_values = jnp.einsum(
        "hqk,qhe->khe", probs.astype(jnp.bfloat16), d_mixed, preferred_element_type=jnp.float32
    ).astype(jnp.bfloat16)
    d_probs = jnp.einsum("qhe,khe->hqk", d_mixed, value_heads, preferred_element_type=jnp.float32)
    d_scores = (
        SCORE_SCALE * probs * (d_probs - jnp.sum(probs * d_probs, axis=-1, keepdims=True))
    ).astype(jnp.bfloat16)
    d_queries = jnp.einsum(
        "hqk,khe->qhe", d_scores, key_heads, preferred_element_type=jnp.float32
    ).astype(jnp.bfloat16)
    d_keys = jnp.einsum(
        "hqk,qhe->khe", d_scores, query_heads, preferred_element_type=jnp.float32
    ).astype(jnp.bfloat16)
    return (d_queries, d_keys, d_values)


def forward_block(
    block_input, segment_rows, time_slots, text_rows, text_marks, table, weights, temporal
):
    w_qkv, w_out, w_query, w_keyval, w_cross, w_up, w_down, w_ada, b_ada = weights
    length, features = block_input.shape
    self_mask, cross_mask, tok_onehot, time_onehot = lookups(
        segment_rows, time_slots, text_marks, temporal
    )
    time_rows = jnp.dot(time_onehot.astype(jnp.bfloat16), table, preferred_element_type=jnp.float32)
    act_time = jax.nn.silu(time_rows).astype(jnp.bfloat16)
    mod_video = jnp.dot(act_time, w_ada, preferred_element_type=jnp.float32) + b_ada
    modulation = jnp.dot(tok_onehot, mod_video, precision=lax.Precision.HIGHEST)
    shift_attend, scale_attend, gate_attend, shift_feed, scale_feed, gate_feed = jnp.split(
        modulation, 6, axis=1
    )
    normed_one = modulate(block_input, shift_attend, scale_attend).astype(jnp.bfloat16)
    qkv = (
        jnp.dot(normed_one, w_qkv, preferred_element_type=jnp.float32)
        .astype(jnp.bfloat16)
        .reshape(length, 3, HEADS, HEAD)
    )
    self_query, self_keys, self_values = (qkv[:, 0], qkv[:, 1], qkv[:, 2])
    self_probs, self_mixed = attend(self_query, self_keys, self_values, self_mask)
    self_mixed = self_mixed.reshape(length, features)
    attended = jnp.dot(self_mixed, w_out, preferred_element_type=jnp.float32)
    after_attend = block_input + gate_attend * attended
    normed_two = layer_norm(after_attend).astype(jnp.bfloat16)
    cross_query = (
        jnp.dot(normed_two, w_query, preferred_element_type=jnp.float32)
        .astype(jnp.bfloat16)
        .reshape(length, HEADS, HEAD)
    )
    text_kv = (
        jnp.dot(text_rows, w_keyval, preferred_element_type=jnp.float32)
        .astype(jnp.bfloat16)
        .reshape(-1, 2, HEADS, HEAD)
    )
    cross_keys, cross_values = (text_kv[:, 0], text_kv[:, 1])
    cross_probs, cross_mixed = attend(cross_query, cross_keys, cross_values, cross_mask)
    cross_mixed = cross_mixed.reshape(length, features)
    after_cross = after_attend + jnp.dot(cross_mixed, w_cross, preferred_element_type=jnp.float32)
    normed_three = modulate(after_cross, shift_feed, scale_feed).astype(jnp.bfloat16)
    hidden = jnp.dot(normed_three, w_up, preferred_element_type=jnp.float32)
    activated = gelu_tanh(hidden).astype(jnp.bfloat16)
    projected = jnp.dot(activated, w_down, preferred_element_type=jnp.float32)
    result = after_cross + gate_feed * projected
    kept_state = SimpleNamespace(
        block_input=block_input,
        tok_onehot=tok_onehot,
        time_onehot=time_onehot,
        time_rows=time_rows,
        act_time=act_time,
        shift_attend=shift_attend,
        scale_attend=scale_attend,
        gate_attend=gate_attend,
        shift_feed=shift_feed,
        scale_feed=scale_feed,
        gate_feed=gate_feed,
        normed_one=normed_one,
        self_query=self_query,
        self_keys=self_keys,
        self_values=self_values,
        self_probs=self_probs,
        self_mixed=self_mixed,
        attended=attended,
        after_attend=after_attend,
        normed_two=normed_two,
        cross_query=cross_query,
        cross_keys=cross_keys,
        cross_values=cross_values,
        cross_probs=cross_probs,
        cross_mixed=cross_mixed,
        after_cross=after_cross,
        normed_three=normed_three,
        hidden=hidden,
        activated=activated,
        projected=projected,
    )
    return (result, kept_state)


def backward_block(kept_state, grad_in, weights, text_rows):
    w_qkv, w_out, w_query, w_keyval, w_cross, w_up, w_down, w_ada, b_ada = weights
    length, features = grad_in.shape
    d_projected = (grad_in * kept_state.gate_feed).astype(jnp.bfloat16)
    d_gate_feed = grad_in * kept_state.projected
    g_down = jnp.einsum(
        "nf,nd->fd", kept_state.activated, d_projected, preferred_element_type=jnp.float32
    )
    d_activated = jnp.einsum("nd,fd->nf", d_projected, w_down, preferred_element_type=jnp.float32)
    unused, gelu_back = jax.vjp(gelu_tanh, kept_state.hidden)
    d_hidden = gelu_back(d_activated)[0].astype(jnp.bfloat16)
    g_up = jnp.einsum(
        "nd,nf->df", kept_state.normed_three, d_hidden, preferred_element_type=jnp.float32
    )
    d_normed_three = jnp.einsum("nf,df->nd", d_hidden, w_up, preferred_element_type=jnp.float32)
    unused, feed_back = jax.vjp(
        modulate, kept_state.after_cross, kept_state.shift_feed, kept_state.scale_feed
    )
    d_after_cross, d_shift_feed, d_scale_feed = feed_back(d_normed_three)
    d_after_cross = d_after_cross + grad_in
    d_crossed = d_after_cross.astype(jnp.bfloat16)
    g_cross = jnp.einsum(
        "nc,nd->cd", kept_state.cross_mixed, d_crossed, preferred_element_type=jnp.float32
    )
    d_cross_mixed = (
        jnp.einsum("nd,cd->nc", d_crossed, w_cross, preferred_element_type=jnp.float32)
        .astype(jnp.bfloat16)
        .reshape(length, HEADS, HEAD)
    )
    d_cross_query, d_cross_keys, d_cross_values = attend_back(
        kept_state.cross_query,
        kept_state.cross_keys,
        kept_state.cross_values,
        kept_state.cross_probs,
        d_cross_mixed,
    )
    d_text_kv = jnp.stack([d_cross_keys, d_cross_values], axis=1).reshape(-1, 2 * features)
    d_cross_query = d_cross_query.reshape(length, features)
    g_query = jnp.einsum(
        "nc,nd->cd", kept_state.normed_two, d_cross_query, preferred_element_type=jnp.float32
    )
    g_keyval = jnp.einsum("tc,td->cd", text_rows, d_text_kv, preferred_element_type=jnp.float32)
    d_text_rows = jnp.einsum("td,cd->tc", d_text_kv, w_keyval, preferred_element_type=jnp.float32)
    d_normed_two = jnp.einsum(
        "nd,cd->nc", d_cross_query, w_query, preferred_element_type=jnp.float32
    )
    unused, norm_back = jax.vjp(layer_norm, kept_state.after_attend)
    d_after_attend = d_after_cross + norm_back(d_normed_two)[0]
    d_attended = (d_after_attend * kept_state.gate_attend).astype(jnp.bfloat16)
    d_gate_attend = d_after_attend * kept_state.attended
    g_out = jnp.einsum(
        "nc,nd->cd", kept_state.self_mixed, d_attended, preferred_element_type=jnp.float32
    )
    d_self_mixed = (
        jnp.einsum("nd,cd->nc", d_attended, w_out, preferred_element_type=jnp.float32)
        .astype(jnp.bfloat16)
        .reshape(length, HEADS, HEAD)
    )
    d_queries, d_keys, d_values = attend_back(
        kept_state.self_query,
        kept_state.self_keys,
        kept_state.self_values,
        kept_state.self_probs,
        d_self_mixed,
    )
    d_qkv = jnp.stack([d_queries, d_keys, d_values], axis=1).reshape(length, 3 * features)
    g_qkv = jnp.einsum(
        "nc,nd->cd", kept_state.normed_one, d_qkv, preferred_element_type=jnp.float32
    )
    d_normed_one = jnp.einsum("nd,cd->nc", d_qkv, w_qkv, preferred_element_type=jnp.float32)
    unused, attend_mod_back = jax.vjp(
        modulate, kept_state.block_input, kept_state.shift_attend, kept_state.scale_attend
    )
    d_block_input, d_shift_attend, d_scale_attend = attend_mod_back(d_normed_one)
    d_block_input = d_block_input + d_after_attend
    d_modulation = jnp.concatenate(
        [d_shift_attend, d_scale_attend, d_gate_attend, d_shift_feed, d_scale_feed, d_gate_feed],
        axis=1,
    )
    d_mod_video = jnp.einsum(
        "nv,nc->vc", kept_state.tok_onehot, d_modulation, precision=lax.Precision.HIGHEST
    )
    layer_terms = (g_qkv, g_out, g_query, g_keyval, g_cross, g_up, g_down)
    return (d_block_input, layer_terms, d_text_rows, d_mod_video)


def batch_groups():
    return [[2 * chip + core for chip in range(32)] for core in range(2)]


def core_swap(value):
    count = lax.axis_size("batch")
    return lax.ppermute(value, "batch", [(i, i ^ 1) for i in range(count)])


def section_swap(value):
    return lax.ppermute(value, "section", [(0, 1), (1, 0)])


def across_chips(value):
    return lax.all_to_all(value, "batch", 0, 0, axis_index_groups=batch_groups(), tiled=True)


def join_halves(mine, core, axis):
    other = core_swap(mine)
    first = jnp.where(core == 0, mine, other)
    second = jnp.where(core == 0, other, mine)
    return jnp.concatenate([first, second], axis=axis)


def pack(members):
    blocks = []
    for member in members:
        rows, columns = member.shape
        blocks.append(
            member.astype(jnp.bfloat16)
            .reshape(rows // 384, 384, columns // 128, 128)
            .transpose(0, 2, 1, 3)
            .reshape(-1, 384, 128)
        )
    return jnp.concatenate(blocks, axis=0)


def unpack(blocks, shapes):
    members, at = [], 0
    for rows, columns in shapes:
        count = rows * columns // (384 * 128)
        piece = blocks[at : at + count].reshape(rows // 384, columns // 128, 384, 128)
        members.append(piece.transpose(0, 2, 1, 3).reshape(rows, columns).astype(jnp.float32))
        at += count
    return members


def summed_over_batch(blocks, core):
    count = blocks.shape[0]
    halves = blocks.reshape(2, count // 2 * 384, 128)
    keep = lax.dynamic_index_in_dim(halves, core, 0, keepdims=False)
    send = lax.dynamic_index_in_dim(halves, 1 - core, 0, keepdims=False)
    both = (keep.astype(jnp.float32) + core_swap(send).astype(jnp.float32)).astype(jnp.bfloat16)
    parts = across_chips(both).reshape(32, -1, 128)
    shard = jnp.sum(parts.astype(jnp.float32), axis=0).astype(jnp.bfloat16)
    full = across_chips(jnp.broadcast_to(shard[None], parts.shape).reshape(-1, 128))
    return join_halves(full, core, 0).reshape(count, 384, 128)


def gathered_modulation(d_mod_low, core):
    rows, columns = d_mod_low.shape
    halves = d_mod_low.reshape(rows, 2, columns // 2)
    keep = lax.dynamic_index_in_dim(halves, core, 1, keepdims=False)
    other = core_swap(lax.dynamic_index_in_dim(halves, 1 - core, 1, keepdims=False))
    first = jnp.where(core == 0, keep, other)
    second = jnp.where(core == 0, other, keep)
    chip = jnp.concatenate([first, second], axis=0)
    spread = jnp.broadcast_to(chip[None], (32,) + chip.shape).reshape(-1, columns // 2)
    return join_halves(across_chips(spread), core, 1)


def put_slot(stacked, member, slot_index, active):
    updated = lax.dynamic_update_index_in_dim(stacked, member, slot_index, 0)
    return jnp.where(active, updated, stacked)


def body(
    inputs,
    cotangent,
    text,
    text_mask,
    segments,
    time_index,
    time_table,
    w_qkv,
    w_out,
    w_query,
    w_keyval,
    w_cross,
    w_up,
    w_down,
    w_ada,
    b_ada,
):
    weights = tuple(
        (
            member[0]
            for member in (w_qkv, w_out, w_query, w_keyval, w_cross, w_up, w_down, w_ada, b_ada)
        )
    )
    section_index = lax.axis_index("section")
    section_count = lax.axis_size("section")
    last_section = section_count - 1
    temporal = section_index % 2 == 1
    clip_rows = FRAMES * PATCHES
    text_span = VIDS * TXT
    features = inputs.shape[1]
    moments = MICRO + section_count - 1

    def clip_data(slot_index):
        return (
            lax.dynamic_slice_in_dim(segments, slot_index * clip_rows, clip_rows, 0),
            lax.dynamic_slice_in_dim(time_index, slot_index * VIDS, VIDS, 0),
            lax.dynamic_slice_in_dim(text, slot_index * text_span, text_span, 0),
            lax.dynamic_slice_in_dim(text_mask, slot_index * text_span, text_span, 0),
        )

    def run_forward(block_input, slot_index):
        segment_rows, time_slots, text_rows, text_marks = clip_data(slot_index)
        return forward_block(
            block_input,
            segment_rows,
            time_slots,
            text_rows,
            text_marks,
            time_table,
            weights,
            temporal,
        )

    core = lax.axis_index("batch") % 2
    other_index = core_swap(time_index)
    chip_index = jnp.where(
        core == 0,
        jnp.concatenate([time_index, other_index]),
        jnp.concatenate([other_index, time_index]),
    )
    every_index = across_chips(jnp.broadcast_to(chip_index[None], (32, 2 * MICRO * VIDS)))
    every_index = every_index.reshape(-1)
    received = jnp.zeros((clip_rows, features), jnp.bfloat16)
    outputs = jnp.zeros((MICRO, clip_rows, features), jnp.bfloat16)
    kept_states = []
    for moment in range(moments):
        micro_batch = moment - section_index
        active = (micro_batch >= 0) & (micro_batch < MICRO)
        slot_index = jnp.clip(micro_batch, 0, MICRO - 1)
        own_rows = lax.dynamic_slice_in_dim(inputs, slot_index * clip_rows, clip_rows, 0).astype(
            jnp.float32
        )
        block_input = jnp.where(section_index == 0, own_rows, received.astype(jnp.float32))
        result, kept_state = run_forward(block_input, slot_index)
        kept_states.append(kept_state)
        outgoing = result.astype(jnp.bfloat16)
        outputs = put_slot(outputs, outgoing, slot_index, active)
        if moment < moments - 1:
            received = shifted(outgoing, "section", 1)
    grad_received = jnp.zeros((clip_rows, features), jnp.bfloat16)
    d_text_all = jnp.zeros((MICRO, text_span, features), jnp.float32)
    d_mod_all = jnp.zeros((MICRO, VIDS, 6 * features), jnp.float32)
    d_inputs = jnp.zeros((MICRO, clip_rows, features), jnp.float32)
    totals = ()
    for moment in range(moments):
        micro_batch = MICRO - 1 - moment + last_section - section_index
        active = (micro_batch >= 0) & (micro_batch < MICRO)
        active_float = active.astype(jnp.float32)
        slot_index = jnp.clip(micro_batch, 0, MICRO - 1)
        given_grad = lax.dynamic_slice_in_dim(
            cotangent, slot_index * clip_rows, clip_rows, 0
        ).astype(jnp.float32)
        grad_in = jnp.where(
            section_index == last_section, given_grad, grad_received.astype(jnp.float32)
        )
        kept_state = kept_states[moments - 1 - moment]
        text_rows = clip_data(slot_index)[2]
        d_block_input, layer_terms, d_text_rows, d_mod_video = backward_block(
            kept_state, grad_in, weights, text_rows
        )
        layer_terms = tuple((member * active_float for member in layer_terms))
        if moment == 0:
            totals = layer_terms
        else:
            totals = tuple((left + right for left, right in zip(totals, layer_terms)))
        d_text_all = put_slot(d_text_all, d_text_rows, slot_index, active)
        d_mod_all = put_slot(d_mod_all, d_mod_video, slot_index, active)
        outgoing = d_block_input.astype(jnp.bfloat16)
        section_grad = jnp.where(section_index == 0, d_block_input, outgoing.astype(jnp.float32))
        d_inputs = put_slot(d_inputs, section_grad, slot_index, active)
        if moment < moments - 1:
            grad_received = shifted(outgoing, "section", -1)
    g_qkv, g_out, g_query, g_keyval, g_cross, g_up, g_down = totals
    d_mod_low = gathered_modulation(
        d_mod_all.reshape(MICRO * VIDS, 6 * features).astype(jnp.bfloat16), core
    )
    feed = summed_over_batch(pack((g_up, g_down)), core)
    g_up, g_down = unpack(feed, (g_up.shape, g_down.shape))
    mixing = (g_qkv, g_out, g_query, g_keyval, g_cross)
    mixed = summed_over_batch(pack(mixing), core)
    g_qkv, g_out, g_query, g_keyval, g_cross = unpack(mixed, [member.shape for member in mixing])
    w_ada = weights[7]
    time_onehot = (every_index[:, None] == jnp.arange(STEPS)[None, :]).astype(jnp.bfloat16)
    time_rows = jnp.dot(time_onehot, time_table, preferred_element_type=jnp.float32)
    act_time = jax.nn.silu(time_rows).astype(jnp.bfloat16)
    g_bias = jnp.sum(d_mod_low.astype(jnp.float32), axis=0)
    g_ada = jnp.einsum("vd,vc->dc", act_time, d_mod_low, preferred_element_type=jnp.float32)
    d_act_time = jnp.einsum("vc,dc->vd", d_mod_low, w_ada, preferred_element_type=jnp.float32)
    unused, silu_back = jax.vjp(jax.nn.silu, time_rows)
    d_time_low = silu_back(d_act_time)[0].astype(jnp.bfloat16)
    d_time_rows = d_time_low.astype(jnp.float32) + section_swap(d_time_low).astype(jnp.float32)
    table_grad = jnp.einsum(
        "vs,vd->sd", time_onehot.astype(jnp.float32), d_time_rows, precision=lax.Precision.HIGHEST
    )
    d_text_low = d_text_all.reshape(-1, features).astype(jnp.bfloat16)
    text_grad = d_text_low.astype(jnp.float32) + section_swap(d_text_low).astype(jnp.float32)
    return (
        outputs.reshape(1, -1, features),
        d_inputs.reshape(1, -1, features),
        text_grad,
        table_grad,
        g_qkv[None],
        g_out[None],
        g_query[None],
        g_keyval[None],
        g_cross[None],
        g_up[None],
        g_down[None],
        g_ada[None],
        g_bias[None],
    )


def solution(mesh):
    return jax.shard_map(
        body,
        mesh=mesh,
        in_specs=(
            P("batch", None),
            P("batch", None),
            P("batch", None),
            P("batch"),
            P("batch"),
            P("batch"),
            P(),
            P("section", None, None),
            P("section", None, None),
            P("section", None, None),
            P("section", None, None),
            P("section", None, None),
            P("section", None, None),
            P("section", None, None),
            P("section", None, None),
            P("section", None),
        ),
        out_specs=(
            P("section", "batch", None),
            P("section", "batch", None),
            P("batch", None),
            P(),
            P("section", None, None),
            P("section", None, None),
            P("section", None, None),
            P("section", None, None),
            P("section", None, None),
            P("section", None, None),
            P("section", None, None),
            P("section", None, None),
            P("section", None),
        ),
        check_vma=False,
    )
```

```python
import functools
import jax
import jax.numpy as jnp
from jax import lax
from jax.experimental import pallas as pl
from jax.experimental.pallas import tpu as pltpu
from jax.sharding import PartitionSpec as P

D = 384
HEADS = 6
HEAD = 64
FF = 1536
PATCHES = 128
FRAMES = 4
VIDS = 2
TXT = 64
MICRO = 2
STEPS = 1000
ROWS = FRAMES * PATCHES
PAIRS = HEADS // 2
SCORE_SCALE = 0.125
NEGATIVE = -1000000000.0
EPSILON = 1e-06
F32 = jnp.float32
BF = jnp.bfloat16
VMEM_LIMIT = 56 * 1024 * 1024


def mm(left, right):
    return lax.dot_general(left, right, (((1,), (0,)), ((), ())), preferred_element_type=F32)


def mm_nt(left, right):
    return lax.dot_general(left, right, (((1,), (1,)), ((), ())), preferred_element_type=F32)


def mm_tn(left, right):
    return lax.dot_general(left, right, (((0,), (0,)), ((), ())), preferred_element_type=F32)


def frame(index):
    return pl.ds(index * PATCHES, PATCHES)


def normed(tensor):
    centre = tensor - jnp.sum(tensor, axis=-1, keepdims=True) * (1.0 / D)
    inverse = lax.rsqrt(jnp.sum(centre * centre, axis=-1, keepdims=True) * (1.0 / D) + EPSILON)
    return centre * inverse, inverse


def norm_back(hat, inverse, d_hat):
    first = jnp.sum(d_hat, axis=-1, keepdims=True) * (1.0 / D)
    second = jnp.sum(d_hat * hat, axis=-1, keepdims=True) * (1.0 / D)
    return inverse * (d_hat - first - hat * second)


def gelu_parts(hidden):
    square = hidden * hidden
    inner = hidden * (0.7978845608028654 + 0.035677408136300125 * square)
    tanh = jnp.tanh(inner)
    half = 0.5 * (1.0 + tanh)
    slope = half + 0.5 * hidden * (1.0 - tanh * tanh) * (
        0.7978845608028654 + 0.10703222440890037 * square
    )
    return hidden * half, slope


def gelu(hidden):
    inner = hidden * (0.7978845608028654 + 0.035677408136300125 * (hidden * hidden))
    return hidden * (0.5 + 0.5 * jnp.tanh(inner))


def half_masks():
    lane = lax.broadcasted_iota(jnp.int32, (1, 128), 1)
    low = (lane < HEAD).astype(F32)
    return low.astype(BF), (1.0 - low).astype(BF)


def stacked(pair, masks):
    return jnp.concatenate([pair * masks[0], pair * masks[1]], axis=0)


def folded(both):
    lane = lax.broadcasted_iota(jnp.int32, (PATCHES, 128), 1)
    return jnp.where(lane < HEAD, both[:PATCHES], both[PATCHES:])


def pair_attend(query, keys, values, allowed, masks):
    logits = mm_nt(stacked(query, masks), keys) * SCORE_SCALE
    if allowed is not None:
        logits = jnp.where(allowed, logits, NEGATIVE)
    raised = jnp.exp(logits - jnp.max(logits, axis=-1, keepdims=True))
    probs = raised * (1.0 / jnp.sum(raised, axis=-1, keepdims=True))
    return folded(mm(probs.astype(BF), values)).astype(BF)


def pair_back(query, keys, values, d_mixed, allowed, masks):
    both_query = stacked(query, masks)
    both_d = stacked(d_mixed, masks)
    logits = mm_nt(keys, both_query) * SCORE_SCALE
    if allowed is not None:
        logits = jnp.where(allowed, logits, NEGATIVE)
    raised = jnp.exp(logits - jnp.max(logits, axis=0, keepdims=True))
    probs = raised * (1.0 / jnp.sum(raised, axis=0, keepdims=True))
    d_probs = mm_nt(values, both_d)
    weighed = probs * d_probs
    d_scores = (
        SCORE_SCALE * (weighed - probs * jnp.sum(weighed, axis=0, keepdims=True))
    ).astype(BF)
    d_query = folded(mm_tn(d_scores, keys))
    d_keys = mm(d_scores, both_query)
    d_values = mm(probs.astype(BF), both_d)
    return d_query, d_keys, d_values


def head_maps():
    feature = lax.broadcasted_iota(jnp.int32, (D, 128), 0) // HEAD
    lane = lax.broadcasted_iota(jnp.int32, (D, 128), 1)
    gather = (feature == lane).astype(F32).astype(BF)
    feature = lax.broadcasted_iota(jnp.int32, (128, D), 1) // HEAD
    lane = lax.broadcasted_iota(jnp.int32, (128, D), 0)
    return gather, (feature == lane).astype(F32).astype(BF)


def temporal_probs(query, keys, same, gather):
    products = jnp.concatenate([(query * key).astype(BF) for key in keys], axis=0)
    scores = mm(products, gather) * SCORE_SCALE
    logits = [
        jnp.where(same[other], scores[other * PATCHES : (other + 1) * PATCHES], NEGATIVE)
        for other in range(FRAMES)
    ]
    top = functools.reduce(jnp.maximum, logits)
    raised = [jnp.exp(member - top) for member in logits]
    scale = 1.0 / functools.reduce(jnp.add, raised)
    return [member * scale for member in raised]


def spread(members, expand):
    wide = mm(jnp.concatenate([member.astype(BF) for member in members], axis=0), expand)
    return [wide[other * PATCHES : (other + 1) * PATCHES] for other in range(FRAMES)]


def forward_kernel(
    info, own, given, mod, text, mask_row, w_qkv, w_out, w_query, w_keyval, w_cross, w_up, w_down,
    result, x_kept, qkv, mixed, attended, after_attend, cross_query, text_kv, cross_mixed,
    after_cross, hidden, projected,
    normed_rows, activated,
):
    section, clip = info[0], info[1]
    masks = half_masks()
    video = [clip * VIDS + info[2 + index] for index in range(FRAMES)]
    text_rows = text[pl.ds(clip * VIDS * TXT, VIDS * TXT), :]
    text_kv[...] = mm(text_rows, w_keyval[...]).astype(BF)

    def group(index, which):
        return mod[pl.ds(video[index], 1), which * D : (which + 1) * D]

    for index in range(FRAMES):
        rows = frame(index)
        x = jnp.where(section == 0, own[pl.ds(clip * ROWS + index * PATCHES, PATCHES), :], given[rows, :])
        x_kept[rows, :] = x
        hat, unused = normed(x.astype(F32))
        normed_rows[rows, :] = (hat * (1.0 + group(index, 1)) + group(index, 0)).astype(BF)
    for part in range(3):
        columns = pl.ds(part * D, D)
        qkv[:, columns] = mm(normed_rows[...], w_qkv[:, columns]).astype(BF)

    @pl.when(section == 0)
    def spatial():
        def one(index, carry):
            rows = frame(index)
            for pair in range(PAIRS):
                mixed[rows, pair * 128 : (pair + 1) * 128] = pair_attend(
                    qkv[rows, pair * 128 : (pair + 1) * 128],
                    qkv[rows, D + pair * 128 : D + (pair + 1) * 128],
                    qkv[rows, 2 * D + pair * 128 : 2 * D + (pair + 1) * 128],
                    None,
                    masks,
                )
            return carry

        lax.fori_loop(0, FRAMES, one, 0)

    @pl.when(section != 0)
    def temporal():
        gather, expand = head_maps()

        def one(index, carry):
            rows = frame(index)
            query = qkv[rows, :D].astype(F32)
            keys = [qkv[frame(other), D : 2 * D].astype(F32) for other in range(FRAMES)]
            same = [info[2 + other] == info[2 + index] for other in range(FRAMES)]
            wide = spread(temporal_probs(query, keys, same, gather), expand)
            total = sum(
                wide[other] * qkv[frame(other), 2 * D :].astype(F32) for other in range(FRAMES)
            )
            mixed[rows, :] = total.astype(BF)
            return carry

        lax.fori_loop(0, FRAMES, one, 0)

    projection = mm(mixed[...], w_out[...])
    for index in range(FRAMES):
        rows = frame(index)
        piece = projection[index * PATCHES : (index + 1) * PATCHES]
        attended[rows, :] = piece.astype(BF)
        state = x_kept[rows, :].astype(F32) + group(index, 2) * piece
        after_attend[rows, :] = state
        normed_rows[rows, :] = normed(state)[0].astype(BF)
    cross_query[...] = mm(normed_rows[...], w_query[...]).astype(BF)
    owner = lax.broadcasted_iota(jnp.int32, (1, VIDS * TXT), 1) // TXT
    real = mask_row[pl.ds(clip, 1), :] == 1

    def cross(index, carry):
        rows = frame(index)
        allowed = real & (owner == info[2 + index])
        for pair in range(PAIRS):
            cross_mixed[rows, pair * 128 : (pair + 1) * 128] = pair_attend(
                cross_query[rows, pair * 128 : (pair + 1) * 128],
                text_kv[:, pair * 128 : (pair + 1) * 128],
                text_kv[:, D + pair * 128 : D + (pair + 1) * 128],
                allowed,
                masks,
            )
        return carry

    lax.fori_loop(0, FRAMES, cross, 0)
    projection = mm(cross_mixed[...], w_cross[...])
    for index in range(FRAMES):
        rows = frame(index)
        state = after_attend[rows, :] + projection[index * PATCHES : (index + 1) * PATCHES]
        after_cross[rows, :] = state
        hat, unused = normed(state)
        normed_rows[rows, :] = (hat * (1.0 + group(index, 4)) + group(index, 3)).astype(BF)

    def feed(chunk, carry):
        columns = pl.ds(pl.multiple_of(chunk * 256, 256), 256)
        for half in range(2):
            rows = pl.ds(half * 256, 256)
            raw = mm(normed_rows[rows, :], w_up[:, columns])
            hidden[rows, columns] = raw.astype(BF)
            activated[rows, columns] = gelu(raw).astype(BF)
        return carry

    lax.fori_loop(0, FF // 256, feed, 0)
    projection = mm(activated[...], w_down[...])
    for index in range(FRAMES):
        rows = frame(index)
        piece = projection[index * PATCHES : (index + 1) * PATCHES]
        projected[rows, :] = piece.astype(BF)
        result[rows, :] = (after_cross[rows, :] + group(index, 5) * piece).astype(BF)


def vmem_specs(count):
    return [pl.BlockSpec(memory_space=pltpu.VMEM)] * count


def forward_call(info, own, given, mod, text, mask_row, weights):
    bf = lambda *shape: jax.ShapeDtypeStruct(shape, BF)
    f32 = lambda *shape: jax.ShapeDtypeStruct(shape, F32)
    return pl.pallas_call(
        forward_kernel,
        out_shape=(
            bf(ROWS, D), bf(ROWS, D), bf(ROWS, 3 * D), bf(ROWS, D), bf(ROWS, D), f32(ROWS, D),
            bf(ROWS, D), bf(VIDS * TXT, 2 * D), bf(ROWS, D), f32(ROWS, D), bf(ROWS, FF), bf(ROWS, D),
        ),
        in_specs=[pl.BlockSpec(memory_space=pltpu.SMEM)] + vmem_specs(12),
        out_specs=tuple(vmem_specs(12)),
        scratch_shapes=[pltpu.VMEM((ROWS, D), BF), pltpu.VMEM((ROWS, FF), BF)],
        compiler_params=pltpu.CompilerParams(vmem_limit_bytes=VMEM_LIMIT),
        name="forward",
    )(info, own, given, mod, text, mask_row, *weights)


def put_blocks(target, at, fresh, prior, info):
    for offset in range(fresh.shape[1] // 128):
        piece = fresh[:, offset * 128 : (offset + 1) * 128]
        if prior is not None:
            piece = jnp.where(info[6] == 1, piece, 0.0) + jnp.where(
                info[7] == 1, prior[at + offset].astype(F32), 0.0
            )
        target[at + offset] = piece.astype(BF)


def column_sum(tensor):
    return jnp.sum(tensor, axis=0, keepdims=True)


def add_by_video(totals, info, index, terms):
    for video in range(VIDS):
        for slot, term in enumerate(terms):
            totals[video][slot] = totals[video][slot] + jnp.where(
                info[2 + index] == video, term, 0.0
            )


def feed_back_kernel(has_prior, info, own, given, mod, after_cross, hidden, projected, w_up, w_down, *rest):
    if has_prior:
        prior, d_after_cross, grads, d_mod, normed_turned, d_turned, d_low, d_active, d_hidden = rest
    else:
        prior = None
        d_after_cross, grads, d_mod, normed_turned, d_turned, d_low, d_active, d_hidden = rest
    section, clip = info[0], info[1]
    video = [clip * VIDS + info[2 + index] for index in range(FRAMES)]
    totals = [[jnp.zeros((1, D), F32) for unused in range(3)] for unused in range(VIDS)]

    def group(index, which):
        return mod[pl.ds(video[index], 1), which * D : (which + 1) * D]

    def incoming(index):
        return jnp.where(
            section == 1, own[pl.ds(clip * ROWS + index * PATCHES, PATCHES), :], given[frame(index), :]
        ).astype(F32)

    for index in range(FRAMES):
        rows = frame(index)
        grad = incoming(index)
        low = (grad * group(index, 5)).astype(BF)
        d_low[rows, :] = low
        d_turned[:, rows] = jnp.swapaxes(low, 0, 1)
        d_gate = column_sum(grad * projected[rows, :].astype(F32))
        zero = jnp.zeros((1, D), F32)
        add_by_video(totals, info, index, (zero, zero, d_gate))
        hat, unused = normed(after_cross[rows, :])
        normed_turned[:, rows] = jnp.swapaxes(
            (hat * (1.0 + group(index, 4)) + group(index, 3)).astype(BF), 0, 1
        )

    def feed(chunk, carry):
        columns = pl.ds(pl.multiple_of(chunk * 256, 256), 256)
        d_active[...] = mm_nt(d_low[...], w_down[columns, :])
        for piece in range(8):
            rows = pl.ds(piece * 64, 64)
            active, slope = gelu_parts(hidden[rows, columns].astype(F32))
            d_hidden[rows, columns] = (d_active[rows, :] * slope).astype(BF)
            d_active[rows, :] = active
        put_blocks(grads, 2 * chunk, mm(normed_turned[...], d_hidden[:, columns]), prior, info)
        put_blocks(grads, 12 + 2 * chunk, mm(d_turned[...], d_active[...].astype(BF)), prior, info)
        return carry

    lax.fori_loop(0, FF // 256, feed, 0)
    d_normed = mm_nt(d_hidden[...], w_up[...])
    for index in range(FRAMES):
        rows = frame(index)
        grad = incoming(index)
        piece = d_normed[index * PATCHES : (index + 1) * PATCHES]
        hat, inverse = normed(after_cross[rows, :])
        add_by_video(
            totals, info, index, (column_sum(piece), column_sum(piece * hat), jnp.zeros((1, D), F32))
        )
        d_after_cross[rows, :] = grad + norm_back(hat, inverse, piece * (1.0 + group(index, 4)))
    for member in range(VIDS):
        for slot in range(3):
            d_mod[member : member + 1, slot * D : (slot + 1) * D] = totals[member][slot]


def feed_back_call(info, own, given, mod, after_cross, hidden, projected, w_up, w_down, prior):
    args = [info, own, given, mod, after_cross, hidden, projected, w_up, w_down]
    if prior is not None:
        args.append(prior)
    return pl.pallas_call(
        functools.partial(feed_back_kernel, prior is not None),
        out_shape=(
            jax.ShapeDtypeStruct((ROWS, D), F32),
            jax.ShapeDtypeStruct((24, D, 128), BF),
            jax.ShapeDtypeStruct((VIDS, 3 * D), F32),
        ),
        in_specs=[pl.BlockSpec(memory_space=pltpu.SMEM)] + vmem_specs(len(args) - 1),
        out_specs=tuple(vmem_specs(3)),
        scratch_shapes=[
            pltpu.VMEM((D, ROWS), BF),
            pltpu.VMEM((D, ROWS), BF),
            pltpu.VMEM((ROWS, D), BF),
            pltpu.VMEM((ROWS, 256), F32),
            pltpu.VMEM((ROWS, FF), BF),
        ],
        compiler_params=pltpu.CompilerParams(vmem_limit_bytes=VMEM_LIMIT),
        name="feed_back",
    )(*args)


def mixing_back_kernel(
    has_prior, info, mod, text, mask_column, d_after_cross, x_kept, qkv, mixed, attended,
    after_attend, cross_query, text_kv, cross_mixed, w_qkv, w_out, w_query, w_keyval, w_cross, *rest
):
    if has_prior:
        prior, rest = rest[0], rest[1:]
    else:
        prior = None
    (
        d_input, d_sent, grads, d_text, d_mod,
        low, turned, d_heads, d_query, d_text_kv, d_qkv, d_attend, d_keys, d_values,
    ) = rest
    section, clip = info[0], info[1]
    video = [clip * VIDS + info[2 + index] for index in range(FRAMES)]
    totals = [[jnp.zeros((1, D), F32) for unused in range(3)] for unused in range(VIDS)]
    masks = half_masks()
    zero = jnp.zeros((1, D), F32)

    def group(index, which):
        return mod[pl.ds(video[index], 1), which * D : (which + 1) * D]

    for index in range(FRAMES):
        rows = frame(index)
        low[rows, :] = d_after_cross[rows, :].astype(BF)
        turned[:, rows] = jnp.swapaxes(cross_mixed[rows, :], 0, 1)
    put_blocks(grads, 12, mm(turned[...], low[...]), prior, info)
    d_heads[...] = mm_nt(low[...], w_cross[...]).astype(BF)
    owner = lax.broadcasted_iota(jnp.int32, (VIDS * TXT, 1), 0) // TXT
    real = mask_column[pl.ds(clip * VIDS * TXT, VIDS * TXT), :] == 1
    d_keys[...] = jnp.zeros_like(d_keys)
    d_values[...] = jnp.zeros_like(d_values)

    def cross(index, carry):
        rows = frame(index)
        allowed = real & (owner == info[2 + index])
        for pair in range(PAIRS):
            columns = slice(pair * 128, (pair + 1) * 128)
            late = slice(D + pair * 128, D + (pair + 1) * 128)
            one, two, three = pair_back(
                cross_query[rows, columns], text_kv[:, columns], text_kv[:, late],
                d_heads[rows, columns], allowed, masks,
            )
            d_query[rows, columns] = one.astype(BF)
            d_keys[: VIDS * TXT, columns] += two
            d_values[: VIDS * TXT, columns] += three
        return carry

    lax.fori_loop(0, FRAMES, cross, 0)
    d_text_kv[:, :D] = d_keys[: VIDS * TXT, :].astype(BF)
    d_text_kv[:, D:] = d_values[: VIDS * TXT, :].astype(BF)
    text_turned = jnp.swapaxes(text[pl.ds(clip * VIDS * TXT, VIDS * TXT), :], 0, 1)
    put_blocks(grads, 18, mm(text_turned, d_text_kv[...]), prior, info)
    d_text[...] = mm_nt(d_text_kv[...], w_keyval[...])
    for index in range(FRAMES):
        rows = frame(index)
        hat, unused = normed(after_attend[rows, :])
        turned[:, rows] = jnp.swapaxes(hat.astype(BF), 0, 1)
    put_blocks(grads, 15, mm(turned[...], d_query[...]), prior, info)
    d_normed = mm_nt(d_query[...], w_query[...])
    for index in range(FRAMES):
        rows = frame(index)
        piece = d_normed[index * PATCHES : (index + 1) * PATCHES]
        hat, inverse = normed(after_attend[rows, :])
        total = d_after_cross[rows, :] + norm_back(hat, inverse, piece)
        d_attend[rows, :] = total
        low[rows, :] = (total * group(index, 2)).astype(BF)
        add_by_video(
            totals, info, index, (zero, zero, column_sum(total * attended[rows, :].astype(F32)))
        )
        turned[:, rows] = jnp.swapaxes(mixed[rows, :], 0, 1)
    put_blocks(grads, 9, mm(turned[...], low[...]), prior, info)
    d_heads[...] = mm_nt(low[...], w_out[...]).astype(BF)

    @pl.when(section == 0)
    def spatial():
        def one_frame(index, carry):
            rows = frame(index)
            for pair in range(PAIRS):
                columns = slice(pair * 128, (pair + 1) * 128)
                second = slice(D + pair * 128, D + (pair + 1) * 128)
                third = slice(2 * D + pair * 128, 2 * D + (pair + 1) * 128)
                one, two, three = pair_back(
                    qkv[rows, columns], qkv[rows, second], qkv[rows, third],
                    d_heads[rows, columns], None, masks,
                )
                d_qkv[rows, columns] = one.astype(BF)
                d_qkv[rows, second] = two.astype(BF)
                d_qkv[rows, third] = three.astype(BF)
            return carry

        lax.fori_loop(0, FRAMES, one_frame, 0)

    @pl.when(section != 0)
    def temporal():
        gather, expand = head_maps()
        d_keys[...] = jnp.zeros_like(d_keys)
        d_values[...] = jnp.zeros_like(d_values)

        def one_frame(index, carry):
            rows = frame(index)
            query = qkv[rows, :D].astype(F32)
            d_mixed = d_heads[rows, :].astype(F32)
            keys = [qkv[frame(other), D : 2 * D].astype(F32) for other in range(FRAMES)]
            same = [info[2 + other] == info[2 + index] for other in range(FRAMES)]
            probs = temporal_probs(query, keys, same, gather)
            products = jnp.concatenate(
                [
                    (d_mixed * qkv[frame(other), 2 * D :].astype(F32)).astype(BF)
                    for other in range(FRAMES)
                ],
                axis=0,
            )
            d_probs = mm(products, gather)
            weighed = [
                probs[other] * d_probs[other * PATCHES : (other + 1) * PATCHES]
                for other in range(FRAMES)
            ]
            total = functools.reduce(jnp.add, weighed)
            d_scores = [
                SCORE_SCALE * (weighed[other] - probs[other] * total) for other in range(FRAMES)
            ]
            wide_probs = spread(probs, expand)
            wide_scores = spread(d_scores, expand)
            d_one = jnp.zeros((PATCHES, D), F32)
            for other in range(FRAMES):
                d_one = d_one + wide_scores[other] * keys[other]
                d_keys[frame(other), :] += wide_scores[other] * query
                d_values[frame(other), :] += wide_probs[other] * d_mixed
            d_qkv[rows, :D] = d_one.astype(BF)
            return carry

        lax.fori_loop(0, FRAMES, one_frame, 0)
        d_qkv[:, D : 2 * D] = d_keys[...].astype(BF)
        d_qkv[:, 2 * D :] = d_values[...].astype(BF)

    for index in range(FRAMES):
        rows = frame(index)
        hat, unused = normed(x_kept[rows, :].astype(F32))
        turned[:, rows] = jnp.swapaxes(
            (hat * (1.0 + group(index, 1)) + group(index, 0)).astype(BF), 0, 1
        )
    for part in range(3):
        put_blocks(
            grads, 3 * part, mm(turned[...], d_qkv[:, part * D : (part + 1) * D]), prior, info
        )
    d_normed = mm_nt(d_qkv[...], w_qkv[...])
    for index in range(FRAMES):
        rows = frame(index)
        piece = d_normed[index * PATCHES : (index + 1) * PATCHES]
        hat, inverse = normed(x_kept[rows, :].astype(F32))
        add_by_video(totals, info, index, (column_sum(piece), column_sum(piece * hat), zero))
        total = d_attend[rows, :] + norm_back(hat, inverse, piece * (1.0 + group(index, 1)))
        d_sent[rows, :] = total.astype(BF)
        d_input[rows, :] = total
    for member in range(VIDS):
        for slot in range(3):
            d_mod[member : member + 1, slot * D : (slot + 1) * D] = totals[member][slot]


def mixing_back_call(info, mod, text, mask_column, d_after_cross, kept, weights, prior):
    (
        x_kept, qkv, mixed, attended, after_attend, cross_query, text_kv, cross_mixed
    ) = kept
    args = [
        info, mod, text, mask_column, d_after_cross, x_kept, qkv, mixed, attended, after_attend,
        cross_query, text_kv, cross_mixed, *weights,
    ]
    if prior is not None:
        args.append(prior)
    return pl.pallas_call(
        functools.partial(mixing_back_kernel, prior is not None),
        out_shape=(
            jax.ShapeDtypeStruct((ROWS, D), F32),
            jax.ShapeDtypeStruct((ROWS, D), BF),
            jax.ShapeDtypeStruct((24, D, 128), BF),
            jax.ShapeDtypeStruct((VIDS * TXT, D), F32),
            jax.ShapeDtypeStruct((VIDS, 3 * D), F32),
        ),
        in_specs=[pl.BlockSpec(memory_space=pltpu.SMEM)] + vmem_specs(len(args) - 1),
        out_specs=tuple(vmem_specs(5)),
        scratch_shapes=[
            pltpu.VMEM((ROWS, D), BF),
            pltpu.VMEM((D, ROWS), BF),
            pltpu.VMEM((ROWS, D), BF),
            pltpu.VMEM((ROWS, D), BF),
            pltpu.VMEM((VIDS * TXT, 2 * D), BF),
            pltpu.VMEM((ROWS, 3 * D), BF),
            pltpu.VMEM((ROWS, D), F32),
            pltpu.VMEM((ROWS, D), F32),
            pltpu.VMEM((ROWS, D), F32),
        ],
        compiler_params=pltpu.CompilerParams(vmem_limit_bytes=VMEM_LIMIT),
        name="mixing_back",
    )(*args)


def spread_kernel(info, mine, other, up, down):
    def write(core):
        for block in range(24):
            source = mine if block // 12 == core else other
            at = (block % 12) * D
            piece = source[at : at + D, :].astype(F32)
            if block < 12:
                up[:, block * 128 : (block + 1) * 128] = piece
            else:
                down[(block - 12) * 128 : (block - 11) * 128, :] = jnp.swapaxes(piece, 0, 1)

    for core in range(2):
        pl.when(info[0] == core)(functools.partial(write, core))


def spread_mixing_kernel(info, mine, other, qkv, out, cross, query, keyval):
    def write(core):
        at = 0
        for target, count in ((qkv, 9), (out, 3), (cross, 3), (query, 3), (keyval, 6)):
            for block in range(count):
                source = mine if at // 12 == core else other
                start = (at % 12) * D
                target[:, block * 128 : (block + 1) * 128] = source[start : start + D, :].astype(F32)
                at += 1

    for core in range(2):
        pl.when(info[0] == core)(functools.partial(write, core))


def spread_call(kernel, core, mine, other, shapes):
    return pl.pallas_call(
        kernel,
        out_shape=tuple(jax.ShapeDtypeStruct(shape, F32) for shape in shapes),
        in_specs=[pl.BlockSpec(memory_space=pltpu.SMEM)] + vmem_specs(2),
        out_specs=tuple(vmem_specs(len(shapes))),
        compiler_params=pltpu.CompilerParams(vmem_limit_bytes=VMEM_LIMIT),
        name="spread",
    )(core.reshape(1), mine, other)


def batch_groups():
    return [[2 * chip + core for chip in range(32)] for core in range(2)]


def core_swap(value):
    count = lax.axis_size("batch")
    return lax.ppermute(value, "batch", [(i, i ^ 1) for i in range(count)])


def section_swap(value):
    return lax.ppermute(value, "section", [(0, 1), (1, 0)])


def across_chips(value):
    return lax.all_to_all(value, "batch", 0, 0, axis_index_groups=batch_groups(), tiled=True)


def join_halves(mine, core, axis):
    other = core_swap(mine)
    first = jnp.where(core == 0, mine, other)
    second = jnp.where(core == 0, other, mine)
    return jnp.concatenate([first, second], axis=axis)


def summed_over_batch(blocks, core):
    count = blocks.shape[0]
    halves = blocks.reshape(2, count // 2 * D, 128)
    keep = lax.dynamic_index_in_dim(halves, core, 0, keepdims=False)
    send = lax.dynamic_index_in_dim(halves, 1 - core, 0, keepdims=False)
    both = (keep.astype(F32) + core_swap(send).astype(F32)).astype(BF)
    parts = across_chips(both).reshape(32, -1, 128)
    shard = jnp.sum(parts.astype(F32), axis=0).astype(BF)
    full = across_chips(jnp.broadcast_to(shard[None], parts.shape).reshape(-1, 128))
    return full, core_swap(full)


def gathered_modulation(d_mod_low, core):
    rows, columns = d_mod_low.shape
    halves = d_mod_low.reshape(rows, 2, columns // 2)
    keep = lax.dynamic_index_in_dim(halves, core, 1, keepdims=False)
    other = core_swap(lax.dynamic_index_in_dim(halves, 1 - core, 1, keepdims=False))
    first = jnp.where(core == 0, keep, other)
    second = jnp.where(core == 0, other, keep)
    chip = jnp.concatenate([first, second], axis=0)
    spread_rows = jnp.broadcast_to(chip[None], (32,) + chip.shape).reshape(-1, columns // 2)
    return join_halves(across_chips(spread_rows), core, 1)


def body(
    inputs, cotangent, text, text_mask, segments, time_index, time_table,
    w_qkv, w_out, w_query, w_keyval, w_cross, w_up, w_down, w_ada, b_ada,
):
    section = lax.axis_index("section")
    core = lax.axis_index("batch") % 2
    mixing_weights = (w_qkv[0], w_out[0], w_query[0], w_keyval[0], w_cross[0])
    feed_weights = (w_up[0], w_down[0])
    frames = segments.reshape(MICRO, FRAMES, PATCHES)[:, :, 0]
    mask_row = text_mask.reshape(MICRO, VIDS * TXT)
    mask_column = text_mask.reshape(-1, 1)

    other_index = core_swap(time_index)
    chip_index = jnp.where(
        core == 0,
        jnp.concatenate([time_index, other_index]),
        jnp.concatenate([other_index, time_index]),
    )
    every_index = across_chips(jnp.broadcast_to(chip_index[None], (32, 2 * MICRO * VIDS)))
    every_index = every_index.reshape(-1)

    def time_lookup(slots):
        onehot = (slots[:, None] == jnp.arange(STEPS)[None, :]).astype(BF)
        rows = mm(onehot, time_table)
        return onehot, rows, jax.nn.silu(rows).astype(BF)

    mod = mm(time_lookup(time_index)[2], w_ada[0]) + b_ada

    def moment_info(clip, fresh, prior):
        clip = jnp.clip(clip, 0, MICRO - 1)
        head = jnp.stack([section, clip])
        tail = jnp.stack([fresh, prior])
        return jnp.concatenate(
            [head, lax.dynamic_index_in_dim(frames, clip, 0, keepdims=False), tail]
        ).astype(jnp.int32)

    none = jnp.zeros((), jnp.int32)
    given = jnp.zeros((ROWS, D), BF)
    results, states = [], []
    for moment in range(MICRO + 1):
        info = moment_info(moment - section, none, none)
        made = forward_call(
            info, inputs, given, mod, text, mask_row, mixing_weights + feed_weights
        )
        results.append(made[0])
        states.append(made[1:])
        if moment < MICRO:
            given = lax.ppermute(made[0], "section", [(0, 1)])
    given = jnp.zeros((ROWS, D), BF)
    feed_sum = mixing_sum = None
    backs = []
    on_first = (section == 0).astype(jnp.int32)
    for moment in range(MICRO + 1):
        fresh = (jnp.ones((), jnp.int32), jnp.ones((), jnp.int32), on_first)[moment]
        prior = (none, 1 - on_first, jnp.ones((), jnp.int32))[moment]
        info = moment_info(MICRO - moment - section, fresh, prior)
        state = states[MICRO - moment]
        d_after_cross, feed_sum, d_mod_feed = feed_back_call(
            info, cotangent, given, mod, state[8], state[9], state[10], *feed_weights, feed_sum
        )
        d_input, d_sent, mixing_sum, d_text, d_mod_mixing = mixing_back_call(
            info, mod, text, mask_column, d_after_cross, state[:8], mixing_weights, mixing_sum
        )
        backs.append((d_input, d_sent, d_text, jnp.concatenate([d_mod_mixing, d_mod_feed], axis=1)))
        if moment < MICRO:
            given = lax.ppermute(d_sent, "section", [(1, 0)])

    first = section == 0
    outputs = jnp.concatenate(
        [jnp.where(first, results[0], results[1]), jnp.where(first, results[1], results[2])]
    )
    d_inputs = jnp.concatenate(
        [
            jnp.where(first, backs[2][0], backs[1][1].astype(F32)),
            jnp.where(first, backs[1][0], backs[0][1].astype(F32)),
        ]
    )

    def by_clip(slot):
        return jnp.concatenate(
            [
                jnp.where(first, backs[2][slot], backs[1][slot]),
                jnp.where(first, backs[1][slot], backs[0][slot]),
            ]
        ).astype(BF)

    feed_full, feed_other = summed_over_batch(feed_sum, core)
    d_mod_low = gathered_modulation(by_clip(3), core)
    mixing_full, mixing_other = summed_over_batch(mixing_sum, core)
    g_up, g_down = spread_call(spread_kernel, core, feed_full, feed_other, ((D, FF), (FF, D)))
    g_qkv, g_out, g_cross, g_query, g_keyval = spread_call(
        spread_mixing_kernel, core, mixing_full, mixing_other,
        ((D, 3 * D), (D, D), (D, D), (D, D), (D, 2 * D)),
    )
    time_onehot, time_rows, act_time = time_lookup(every_index)
    g_bias = jnp.sum(d_mod_low.astype(F32), axis=0)
    g_ada = mm_tn(act_time, d_mod_low)
    d_act_time = mm_nt(d_mod_low, w_ada[0])
    unused, silu_back = jax.vjp(jax.nn.silu, time_rows)
    d_time_low = silu_back(d_act_time)[0].astype(BF)
    d_time_rows = d_time_low.astype(F32) + section_swap(d_time_low).astype(F32)
    table_grad = jnp.einsum(
        "vs,vd->sd", time_onehot.astype(F32), d_time_rows, precision=lax.Precision.HIGHEST
    )
    d_text_low = by_clip(2)
    text_grad = d_text_low.astype(F32) + section_swap(d_text_low).astype(F32)
    return (
        outputs[None], d_inputs[None], text_grad, table_grad, g_qkv[None], g_out[None],
        g_query[None], g_keyval[None], g_cross[None], g_up[None], g_down[None], g_ada[None],
        g_bias[None],
    )


def solution(mesh):
    return jax.shard_map(
        body,
        mesh=mesh,
        in_specs=(
            P("batch", None),
            P("batch", None),
            P("batch", None),
            P("batch"),
            P("batch"),
            P("batch"),
            P(),
            P("section", None, None),
            P("section", None, None),
            P("section", None, None),
            P("section", None, None),
            P("section", None, None),
            P("section", None, None),
            P("section", None, None),
            P("section", None, None),
            P("section", None),
        ),
        out_specs=(
            P("section", "batch", None),
            P("section", "batch", None),
            P("batch", None),
            P(),
            P("section", None, None),
            P("section", None, None),
            P("section", None, None),
            P("section", None, None),
            P("section", None, None),
            P("section", None, None),
            P("section", None, None),
            P("section", None, None),
            P("section", None),
        ),
        check_vma=False,
    )
```

```python
import functools
import jax
import jax.numpy as jnp
from jax import lax
from jax.experimental import pallas as pl
from jax.experimental.pallas import tpu as pltpu
from jax.sharding import PartitionSpec as P

D = 384
HEADS = 6
HEAD = 64
FF = 1536
PATCHES = 128
FRAMES = 4
VIDS = 2
TXT = 64
MICRO = 2
STEPS = 1000
ROWS = FRAMES * PATCHES
TEXT = VIDS * TXT
BLOCKS = 24
PACKED = BLOCKS * D
HALF = PACKED // 2
SHARE = PACKED // 32
EXTRA = 88
TIMES = 24
PAIRS = HEADS // 2
SCORE_SCALE = 0.125
NEGATIVE = -1000000000.0
EPSILON = 1e-06
F32 = jnp.float32
BF = jnp.bfloat16
VMEM_LIMIT = 56 * 1024 * 1024


def mm(left, right):
    return lax.dot_general(left, right, (((1,), (0,)), ((), ())), preferred_element_type=F32)


def mm_nt(left, right):
    return lax.dot_general(left, right, (((1,), (1,)), ((), ())), preferred_element_type=F32)


def mm_tn(left, right):
    return lax.dot_general(left, right, (((0,), (0,)), ((), ())), preferred_element_type=F32)


def frame(index):
    return pl.ds(index * PATCHES, PATCHES)


def normed(tensor):
    centre = tensor - jnp.sum(tensor, axis=-1, keepdims=True) * (1.0 / D)
    inverse = lax.rsqrt(jnp.sum(centre * centre, axis=-1, keepdims=True) * (1.0 / D) + EPSILON)
    return centre * inverse, inverse


def norm_back(hat, inverse, d_hat):
    first = jnp.sum(d_hat, axis=-1, keepdims=True) * (1.0 / D)
    second = jnp.sum(d_hat * hat, axis=-1, keepdims=True) * (1.0 / D)
    return inverse * (d_hat - first - hat * second)


def gelu_parts(hidden):
    square = hidden * hidden
    inner = hidden * (0.7978845608028654 + 0.035677408136300125 * square)
    tanh = jnp.tanh(inner)
    half = 0.5 * (1.0 + tanh)
    slope = half + 0.5 * hidden * (1.0 - tanh * tanh) * (
        0.7978845608028654 + 0.10703222440890037 * square
    )
    return hidden * half, slope


def gelu(hidden):
    inner = hidden * (0.7978845608028654 + 0.035677408136300125 * (hidden * hidden))
    return hidden * (0.5 + 0.5 * jnp.tanh(inner))


def half_masks():
    lane = lax.broadcasted_iota(jnp.int32, (1, 128), 1)
    low = (lane < HEAD).astype(F32)
    return low.astype(BF), (1.0 - low).astype(BF)


def stacked(pair, masks):
    return jnp.concatenate([pair * masks[0], pair * masks[1]], axis=0)


def folded(both):
    lane = lax.broadcasted_iota(jnp.int32, (PATCHES, 128), 1)
    return jnp.where(lane < HEAD, both[:PATCHES], both[PATCHES:])


def pair_attend(query, keys, values, allowed, masks):
    logits = mm_nt(stacked(query, masks), keys) * SCORE_SCALE
    if allowed is not None:
        logits = jnp.where(allowed, logits, NEGATIVE)
    raised = jnp.exp(logits - jnp.max(logits, axis=-1, keepdims=True))
    probs = raised * (1.0 / jnp.sum(raised, axis=-1, keepdims=True))
    return folded(mm(probs.astype(BF), values)).astype(BF)


def pair_back(query, keys, values, d_mixed, allowed, masks):
    both_query = stacked(query, masks)
    both_d = stacked(d_mixed, masks)
    logits = mm_nt(keys, both_query) * SCORE_SCALE
    if allowed is not None:
        logits = jnp.where(allowed, logits, NEGATIVE)
    raised = jnp.exp(logits - jnp.max(logits, axis=0, keepdims=True))
    probs = raised * (1.0 / jnp.sum(raised, axis=0, keepdims=True))
    d_probs = mm_nt(values, both_d)
    weighed = probs * d_probs
    d_scores = (
        SCORE_SCALE * (weighed - probs * jnp.sum(weighed, axis=0, keepdims=True))
    ).astype(BF)
    d_query = folded(mm_tn(d_scores, keys))
    d_keys = mm(d_scores, both_query)
    d_values = mm(probs.astype(BF), both_d)
    return d_query, d_keys, d_values


def head_maps():
    feature = lax.broadcasted_iota(jnp.int32, (D, 128), 0) // HEAD
    lane = lax.broadcasted_iota(jnp.int32, (D, 128), 1)
    gather = (feature == lane).astype(F32).astype(BF)
    feature = lax.broadcasted_iota(jnp.int32, (128, D), 1) // HEAD
    lane = lax.broadcasted_iota(jnp.int32, (128, D), 0)
    return gather, (feature == lane).astype(F32).astype(BF)


def temporal_probs(query, keys, same, gather):
    products = jnp.concatenate([(query * key).astype(BF) for key in keys], axis=0)
    scores = mm(products, gather) * SCORE_SCALE
    logits = [
        jnp.where(same[other], scores[other * PATCHES : (other + 1) * PATCHES], NEGATIVE)
        for other in range(FRAMES)
    ]
    top = functools.reduce(jnp.maximum, logits)
    raised = [jnp.exp(member - top) for member in logits]
    scale = 1.0 / functools.reduce(jnp.add, raised)
    return [member * scale for member in raised]


def spread(members, expand):
    wide = mm(jnp.concatenate([member.astype(BF) for member in members], axis=0), expand)
    return [wide[other * PATCHES : (other + 1) * PATCHES] for other in range(FRAMES)]


def vmem_specs(count):
    return [pl.BlockSpec(memory_space=pltpu.VMEM)] * count


def any_specs(count):
    return [pl.BlockSpec(memory_space=pl.ANY)] * count


def params():
    return pltpu.CompilerParams(vmem_limit_bytes=VMEM_LIMIT)


def cost(micros):
    return pl.CostEstimate(flops=int(micros * 1e9), bytes_accessed=1 << 20, transcendentals=0)


def shape_of(dtype, *shape):
    return jax.ShapeDtypeStruct(shape, dtype)


class Weights:
    def __init__(self, info, layer, sources, held, arrived, pieces, shift):
        self.own, self.mine, self.other = sources
        self.held, self.arrived, self.pieces = held, arrived, pieces
        is_own = info[0] == layer
        for slot, (start, count) in enumerate(pieces):
            half = start // HALF
            into = held.at[pl.ds(start, count), :]
            inside = start - half * HALF + shift

            def begin(source, at, into=into, slot=slot, count=count):
                pltpu.make_async_copy(
                    source.at[pl.ds(at, count), :], into, arrived.at[slot]
                ).start()

            pl.when(is_own)(functools.partial(begin, self.own, half * PACKED + inside))
            pl.when(jnp.logical_not(is_own) & (info[1] == half))(
                functools.partial(begin, self.mine, inside)
            )
            pl.when(jnp.logical_not(is_own) & (info[1] != half))(
                functools.partial(begin, self.other, inside)
            )

    def wait(self, slot):
        start, count = self.pieces[slot]
        rows = pl.ds(start, count)
        pltpu.make_async_copy(
            self.own.at[rows, :], self.held.at[rows, :], self.arrived.at[slot]
        ).wait()

    def columns(self, block, count):
        return jnp.concatenate(
            [self.held[(block + at) * D : (block + at + 1) * D, :] for at in range(count)], axis=1
        )


class Gradients:
    def __init__(self, info, kept, keep, send, left):
        self.info, self.kept, self.keep, self.send, self.left = info, kept, keep, send, left

    def put(self, block, fresh):
        for offset in range(fresh.shape[1] // 128):
            at = (block + offset) * D
            if not isinstance(at, int):
                at = pl.multiple_of(at, D)
            self.kept[pl.ds(at, D), :] = fresh[:, offset * 128 : (offset + 1) * 128].astype(BF)

    def copy(self, half, target):
        return pltpu.make_async_copy(
            self.kept.at[pl.ds(half * HALF, HALF), :], target, self.left.at[half]
        )

    def begin(self, half):
        pl.when(self.info[1] == half)(lambda: self.copy(half, self.keep).start())
        pl.when(self.info[1] != half)(lambda: self.copy(half, self.send).start())

    def finish(self):
        for half in range(2):
            self.copy(half, self.keep).wait()


MIXING_PIECES = ((0, 9 * D), (9 * D, 3 * D), (12 * D, 3 * D), (15 * D, 9 * D))
FEED_PIECES = ((0, 12 * D), (12 * D, 12 * D))
QKV, OUT, CROSS, QUERY, KEYVAL = 0, 9, 12, 15, 18


def weight_scratch(pieces):
    return [pltpu.VMEM((PACKED, 128), BF), pltpu.SemaphoreType.DMA((len(pieces),))]


def fill_packed(weights, held, after_part):
    w_qkv, w_out, w_query, w_keyval, w_cross, w_up, w_down = weights
    for half, members in enumerate(
        (((w_qkv, 9), (w_out, 3)), ((w_cross, 3), (w_query, 3), (w_keyval, 6)))
    ):
        at = half * PACKED
        for source, count in members:
            for block in range(count):
                held[at : at + D, :] = source[0, :, block * 128 : (block + 1) * 128]
                at += D
        after_part(half * PACKED)
    for block in range(12):
        at = HALF + block * D
        held[at : at + D, :] = w_up[0, :, block * 128 : (block + 1) * 128]
    after_part(HALF)
    for block in range(3):
        at = PACKED + HALF + block * FF
        held[at : at + FF, :] = w_down[0, :, block * 128 : (block + 1) * 128]
    after_part(PACKED + HALF)


def shard_kernel(place, *refs):
    weights, (shard, held) = refs[:7], refs[7:]
    fill_packed(weights, held, lambda start: None)
    start = (place[0] % 2) * PACKED + (place[0] // 2) * SHARE
    shard[...] = held[pl.ds(pl.multiple_of(start, SHARE), SHARE), :]


def shard_call(place, weights):
    return pl.pallas_call(
        shard_kernel,
        out_shape=shape_of(BF, SHARE, 128),
        in_specs=[pl.BlockSpec(memory_space=pltpu.SMEM)] + vmem_specs(len(weights)),
        out_specs=vmem_specs(1)[0],
        scratch_shapes=[pltpu.VMEM((2 * PACKED, 128), BF)],
        compiler_params=params(),
        name="shard",
    )(place, *weights)


def pack_kernel(*refs):
    weights, (after, packed, held, left) = refs[:7], refs[7:]
    copies = []

    def leave(start):
        rows = pl.ds(start, HALF)
        made = pltpu.make_async_copy(held.at[rows, :], packed.at[rows, :], left.at[len(copies)])
        made.start()
        copies.append(made)

    fill_packed(weights, held, leave)
    for made in copies:
        made.wait()


def pack_call(weights, after):
    return pl.pallas_call(
        pack_kernel,
        out_shape=shape_of(BF, 2 * PACKED, 128),
        in_specs=vmem_specs(len(weights)) + any_specs(1),
        out_specs=any_specs(1)[0],
        scratch_shapes=[pltpu.VMEM((2 * PACKED, 128), BF), pltpu.SemaphoreType.DMA((4,))],
        compiler_params=params(),
        name="pack",
    )(*weights, after)


def video_group(info, mod):
    def group(index, which):
        return mod[pl.ds(info[2 + index], 1), which * D : (which + 1) * D]

    return group


def mix_forward_kernel(
    layer, info, given, mod, text, mask_row, own, mine, other,
    x_kept, qkv, mixed, attended, after_attend, cross_query, text_kv, cross_mixed, after_cross,
    normed_rows, held, arrived,
):
    weights = Weights(info, layer, (own, mine, other), held, arrived, MIXING_PIECES, 0)
    clip = info[0]
    masks = half_masks()
    group = video_group(info, mod)
    for index in range(FRAMES):
        rows = frame(index)
        if layer == 0:
            x = given[pl.ds(clip * ROWS + index * PATCHES, PATCHES), :]
        else:
            x = given[rows, :]
        x_kept[rows, :] = x
        hat, unused = normed(x.astype(F32))
        normed_rows[rows, :] = (hat * (1.0 + group(index, 1)) + group(index, 0)).astype(BF)
    weights.wait(0)
    for part in range(3):
        qkv[:, part * D : (part + 1) * D] = mm(
            normed_rows[...], weights.columns(QKV + 3 * part, 3)
        ).astype(BF)

    def spatial(index, carry):
        rows = frame(index)
        for pair in range(PAIRS):
            mixed[rows, pair * 128 : (pair + 1) * 128] = pair_attend(
                qkv[rows, pair * 128 : (pair + 1) * 128],
                qkv[rows, D + pair * 128 : D + (pair + 1) * 128],
                qkv[rows, 2 * D + pair * 128 : 2 * D + (pair + 1) * 128],
                None,
                masks,
            )
        return carry

    def temporal(index, carry):
        gather, expand = head_maps()
        rows = frame(index)
        query = qkv[rows, :D].astype(F32)
        keys = [qkv[frame(at), D : 2 * D].astype(F32) for at in range(FRAMES)]
        same = [info[2 + at] == info[2 + index] for at in range(FRAMES)]
        wide = spread(temporal_probs(query, keys, same, gather), expand)
        total = sum(wide[at] * qkv[frame(at), 2 * D :].astype(F32) for at in range(FRAMES))
        mixed[rows, :] = total.astype(BF)
        return carry

    lax.fori_loop(0, FRAMES, spatial if layer == 0 else temporal, 0)
    weights.wait(1)
    projection = mm(mixed[...], weights.columns(OUT, 3))
    for index in range(FRAMES):
        rows = frame(index)
        piece = projection[index * PATCHES : (index + 1) * PATCHES]
        attended[rows, :] = piece.astype(BF)
        state = x_kept[rows, :].astype(F32) + group(index, 2) * piece
        after_attend[rows, :] = state
        normed_rows[rows, :] = normed(state)[0].astype(BF)
    weights.wait(2)
    weights.wait(3)
    cross_query[...] = mm(normed_rows[...], weights.columns(QUERY, 3)).astype(BF)
    text_rows = text[pl.ds(clip * TEXT, TEXT), :]
    text_kv[...] = mm(text_rows, weights.columns(KEYVAL, 6)).astype(BF)
    owner = lax.broadcasted_iota(jnp.int32, (1, TEXT), 1) // TXT
    real = mask_row[pl.ds(clip, 1), :] == 1

    def cross(index, carry):
        rows = frame(index)
        allowed = real & (owner == info[2 + index])
        for pair in range(PAIRS):
            cross_mixed[rows, pair * 128 : (pair + 1) * 128] = pair_attend(
                cross_query[rows, pair * 128 : (pair + 1) * 128],
                text_kv[:, pair * 128 : (pair + 1) * 128],
                text_kv[:, D + pair * 128 : D + (pair + 1) * 128],
                allowed,
                masks,
            )
        return carry

    lax.fori_loop(0, FRAMES, cross, 0)
    projection = mm(cross_mixed[...], weights.columns(CROSS, 3))
    for index in range(FRAMES):
        rows = frame(index)
        after_cross[rows, :] = (
            after_attend[rows, :] + projection[index * PATCHES : (index + 1) * PATCHES]
        )


def mix_forward_call(layer, info, given, mod, text, mask_row, sources):
    return pl.pallas_call(
        functools.partial(mix_forward_kernel, layer),
        out_shape=(
            shape_of(BF, ROWS, D), shape_of(BF, ROWS, 3 * D), shape_of(BF, ROWS, D),
            shape_of(BF, ROWS, D), shape_of(F32, ROWS, D), shape_of(BF, ROWS, D),
            shape_of(BF, TEXT, 2 * D), shape_of(BF, ROWS, D), shape_of(F32, ROWS, D),
        ),
        in_specs=[pl.BlockSpec(memory_space=pltpu.SMEM)] + vmem_specs(4) + any_specs(3),
        out_specs=tuple(vmem_specs(9)),
        scratch_shapes=[pltpu.VMEM((ROWS, D), BF)] + weight_scratch(MIXING_PIECES),
        compiler_params=params(),
        cost_estimate=cost(0.05),
        name="mix_forward",
    )(info, given, mod, text, mask_row, *sources)


def feed_forward_kernel(
    layer, info, mod, after_cross, own, mine, other, result, hidden, projected,
    normed_rows, activated, held, arrived,
):
    weights = Weights(info, layer, (own, mine, other), held, arrived, FEED_PIECES, HALF)
    group = video_group(info, mod)
    for index in range(FRAMES):
        rows = frame(index)
        hat, unused = normed(after_cross[rows, :])
        normed_rows[rows, :] = (hat * (1.0 + group(index, 4)) + group(index, 3)).astype(BF)
    weights.wait(0)
    for chunk in range(FF // 256):
        columns = slice(chunk * 256, (chunk + 1) * 256)
        raw = mm(normed_rows[...], weights.columns(2 * chunk, 2))
        hidden[:, columns] = raw.astype(BF)
        activated[:, columns] = gelu(raw).astype(BF)
    weights.wait(1)
    down = jnp.concatenate(
        [held[HALF + block * FF : HALF + (block + 1) * FF, :] for block in range(3)], axis=1
    )
    projection = mm(activated[...], down)
    for index in range(FRAMES):
        rows = frame(index)
        piece = projection[index * PATCHES : (index + 1) * PATCHES]
        projected[rows, :] = piece.astype(BF)
        result[rows, :] = (after_cross[rows, :] + group(index, 5) * piece).astype(BF)


def feed_forward_call(layer, info, mod, after_cross, sources):
    return pl.pallas_call(
        functools.partial(feed_forward_kernel, layer),
        out_shape=(shape_of(BF, ROWS, D), shape_of(BF, ROWS, FF), shape_of(BF, ROWS, D)),
        in_specs=[pl.BlockSpec(memory_space=pltpu.SMEM)] + vmem_specs(2) + any_specs(3),
        out_specs=tuple(vmem_specs(3)),
        scratch_shapes=[pltpu.VMEM((ROWS, D), BF), pltpu.VMEM((ROWS, FF), BF)]
        + weight_scratch(FEED_PIECES),
        compiler_params=params(),
        cost_estimate=cost(0.05),
        name="feed_forward",
    )(info, mod, after_cross, *sources)


def column_sum(tensor):
    return jnp.sum(tensor, axis=0, keepdims=True)


def add_by_video(totals, info, index, terms):
    for video in range(VIDS):
        for slot, term in enumerate(terms):
            if term is not None:
                totals[video][slot] = totals[video][slot] + jnp.where(
                    info[2 + index] == video, term, 0.0
                )


def no_totals():
    return [[jnp.zeros((1, D), F32) for unused in range(3)] for unused in range(VIDS)]


def put_totals(d_mod, totals):
    for member in range(VIDS):
        for slot in range(3):
            d_mod[member : member + 1, slot * D : (slot + 1) * D] = totals[member][slot]


def following(kernel, layer, count, unused):
    def call(*refs):
        kernel(layer, *refs[:count], *refs[count + unused :])

    return call


def feed_back_kernel(
    layer, info, given, mod, after_cross, hidden, projected, own, mine, other,
    d_after_cross, keep, send, d_mod,
    normed_turned, d_turned, d_low, d_active, d_hidden, held, arrived, kept_grads, left,
):
    grads = Gradients(info, kept_grads, keep, send, left)
    weights = Weights(info, layer, (own, mine, other), held, arrived, FEED_PIECES, HALF)
    clip = info[0]
    totals = no_totals()
    group = video_group(info, mod)

    def incoming(index):
        if layer == 1:
            return given[pl.ds(clip * ROWS + index * PATCHES, PATCHES), :].astype(F32)
        return given[frame(index), :].astype(F32)

    for index in range(FRAMES):
        rows = frame(index)
        grad = incoming(index)
        low = (grad * group(index, 5)).astype(BF)
        d_low[rows, :] = low
        d_turned[:, rows] = jnp.swapaxes(low, 0, 1)
        d_gate = column_sum(grad * projected[rows, :].astype(F32))
        add_by_video(totals, info, index, (None, None, d_gate))
        hat, unused = normed(after_cross[rows, :])
        normed_turned[:, rows] = jnp.swapaxes(
            (hat * (1.0 + group(index, 4)) + group(index, 3)).astype(BF), 0, 1
        )
    weights.wait(1)
    weights.wait(0)

    def feed(chunk, carry):
        columns = pl.ds(pl.multiple_of(chunk * 256, 256), 256)
        down = jnp.concatenate(
            [
                held[pl.ds(pl.multiple_of(HALF + block * FF + chunk * 256, 256), 256), :]
                for block in range(3)
            ],
            axis=1,
        )
        d_active[...] = mm_nt(d_low[...], down)
        for piece in range(8):
            rows = pl.ds(piece * 64, 64)
            active, slope = gelu_parts(hidden[rows, columns].astype(F32))
            d_hidden[rows, columns] = (d_active[rows, :] * slope).astype(BF)
            d_active[rows, :] = active
        grads.put(2 * chunk, mm(normed_turned[...], d_hidden[:, columns]))
        grads.put(12 + 2 * chunk, mm(d_turned[...], d_active[...].astype(BF)))
        return carry

    lax.fori_loop(0, FF // 256, feed, 0)
    grads.begin(0)
    grads.begin(1)
    d_normed = mm_nt(d_hidden[...], weights.columns(0, 12))
    for index in range(FRAMES):
        rows = frame(index)
        grad = incoming(index)
        piece = d_normed[index * PATCHES : (index + 1) * PATCHES]
        hat, inverse = normed(after_cross[rows, :])
        add_by_video(totals, info, index, (column_sum(piece), column_sum(piece * hat), None))
        d_after_cross[rows, :] = grad + norm_back(hat, inverse, piece * (1.0 + group(index, 4)))
    put_totals(d_mod, totals)
    grads.finish()


def feed_back_call(layer, info, given, mod, after_cross, hidden, projected, sources, *after):
    return pl.pallas_call(
        following(feed_back_kernel, layer, 9, len(after)),
        out_shape=(
            shape_of(F32, ROWS, D), shape_of(BF, HALF, 128), shape_of(BF, HALF, 128),
            shape_of(F32, VIDS, 3 * D),
        ),
        in_specs=[pl.BlockSpec(memory_space=pltpu.SMEM)] + vmem_specs(5) + any_specs(3 + len(after)),
        out_specs=tuple(vmem_specs(1) + any_specs(2) + vmem_specs(1)),
        scratch_shapes=[
            pltpu.VMEM((D, ROWS), BF),
            pltpu.VMEM((D, ROWS), BF),
            pltpu.VMEM((ROWS, D), BF),
            pltpu.VMEM((ROWS, 256), F32),
            pltpu.VMEM((ROWS, FF), BF),
        ]
        + weight_scratch(FEED_PIECES)
        + [pltpu.VMEM((PACKED, 128), BF), pltpu.SemaphoreType.DMA((2,))],
        compiler_params=params(),
        cost_estimate=cost(0.05),
        name="feed_back",
    )(info, given, mod, after_cross, hidden, projected, *sources, *after)


def mix_back_kernel(
    layer, info, mod, text, mask_column, d_after_cross, x_kept, qkv, mixed, attended,
    after_attend, cross_query, text_kv, cross_mixed, own, mine, other,
    d_input, d_sent, keep, send, d_text, d_mod,
    low, turned, d_heads, d_query, d_text_kv, d_qkv, d_attend, d_keys, d_values, held, arrived,
    kept_grads, left,
):
    grads = Gradients(info, kept_grads, keep, send, left)
    weights = Weights(info, layer, (own, mine, other), held, arrived, MIXING_PIECES, 0)
    clip = info[0]
    totals = no_totals()
    masks = half_masks()
    group = video_group(info, mod)

    for index in range(FRAMES):
        rows = frame(index)
        low[rows, :] = d_after_cross[rows, :].astype(BF)
        turned[:, rows] = jnp.swapaxes(cross_mixed[rows, :], 0, 1)
    grads.put(CROSS, mm(turned[...], low[...]))
    weights.wait(2)
    weights.wait(3)
    d_heads[...] = mm_nt(low[...], weights.columns(CROSS, 3)).astype(BF)
    owner = lax.broadcasted_iota(jnp.int32, (TEXT, 1), 0) // TXT
    real = mask_column[pl.ds(clip * TEXT, TEXT), :] == 1
    d_keys[...] = jnp.zeros_like(d_keys)
    d_values[...] = jnp.zeros_like(d_values)

    def cross(index, carry):
        rows = frame(index)
        allowed = real & (owner == info[2 + index])
        for pair in range(PAIRS):
            columns = slice(pair * 128, (pair + 1) * 128)
            late = slice(D + pair * 128, D + (pair + 1) * 128)
            one, two, three = pair_back(
                cross_query[rows, columns], text_kv[:, columns], text_kv[:, late],
                d_heads[rows, columns], allowed, masks,
            )
            d_query[rows, columns] = one.astype(BF)
            d_keys[: TEXT, columns] += two
            d_values[: TEXT, columns] += three
        return carry

    lax.fori_loop(0, FRAMES, cross, 0)
    d_text_kv[:, :D] = d_keys[: TEXT, :].astype(BF)
    d_text_kv[:, D:] = d_values[: TEXT, :].astype(BF)
    text_turned = jnp.swapaxes(text[pl.ds(clip * TEXT, TEXT), :], 0, 1)
    grads.put(KEYVAL, mm(text_turned, d_text_kv[...]))
    d_text[...] = mm_nt(d_text_kv[...], weights.columns(KEYVAL, 6))
    for index in range(FRAMES):
        rows = frame(index)
        hat, unused = normed(after_attend[rows, :])
        turned[:, rows] = jnp.swapaxes(hat.astype(BF), 0, 1)
    grads.put(QUERY, mm(turned[...], d_query[...]))
    grads.begin(1)
    d_normed = mm_nt(d_query[...], weights.columns(QUERY, 3))
    for index in range(FRAMES):
        rows = frame(index)
        piece = d_normed[index * PATCHES : (index + 1) * PATCHES]
        hat, inverse = normed(after_attend[rows, :])
        total = d_after_cross[rows, :] + norm_back(hat, inverse, piece)
        d_attend[rows, :] = total
        low[rows, :] = (total * group(index, 2)).astype(BF)
        add_by_video(
            totals, info, index, (None, None, column_sum(total * attended[rows, :].astype(F32)))
        )
        turned[:, rows] = jnp.swapaxes(mixed[rows, :], 0, 1)
    grads.put(OUT, mm(turned[...], low[...]))
    weights.wait(1)
    d_heads[...] = mm_nt(low[...], weights.columns(OUT, 3)).astype(BF)

    if layer == 0:
        def one_frame(index, carry):
            rows = frame(index)
            for pair in range(PAIRS):
                columns = slice(pair * 128, (pair + 1) * 128)
                second = slice(D + pair * 128, D + (pair + 1) * 128)
                third = slice(2 * D + pair * 128, 2 * D + (pair + 1) * 128)
                one, two, three = pair_back(
                    qkv[rows, columns], qkv[rows, second], qkv[rows, third],
                    d_heads[rows, columns], None, masks,
                )
                d_qkv[rows, columns] = one.astype(BF)
                d_qkv[rows, second] = two.astype(BF)
                d_qkv[rows, third] = three.astype(BF)
            return carry

        lax.fori_loop(0, FRAMES, one_frame, 0)

    else:
        gather, expand = head_maps()
        d_keys[...] = jnp.zeros_like(d_keys)
        d_values[...] = jnp.zeros_like(d_values)

        def one_frame(index, carry):
            rows = frame(index)
            query = qkv[rows, :D].astype(F32)
            d_mixed = d_heads[rows, :].astype(F32)
            keys = [qkv[frame(at), D : 2 * D].astype(F32) for at in range(FRAMES)]
            same = [info[2 + at] == info[2 + index] for at in range(FRAMES)]
            probs = temporal_probs(query, keys, same, gather)
            products = jnp.concatenate(
                [
                    (d_mixed * qkv[frame(at), 2 * D :].astype(F32)).astype(BF)
                    for at in range(FRAMES)
                ],
                axis=0,
            )
            d_probs = mm(products, gather)
            weighed = [
                probs[at] * d_probs[at * PATCHES : (at + 1) * PATCHES]
                for at in range(FRAMES)
            ]
            total = functools.reduce(jnp.add, weighed)
            d_scores = [
                SCORE_SCALE * (weighed[at] - probs[at] * total) for at in range(FRAMES)
            ]
            wide_probs = spread(probs, expand)
            wide_scores = spread(d_scores, expand)
            d_one = jnp.zeros((PATCHES, D), F32)
            for at in range(FRAMES):
                d_one = d_one + wide_scores[at] * keys[at]
                d_keys[frame(at), :] += wide_scores[at] * query
                d_values[frame(at), :] += wide_probs[at] * d_mixed
            d_qkv[rows, :D] = d_one.astype(BF)
            return carry

        lax.fori_loop(0, FRAMES, one_frame, 0)
        d_qkv[:, D : 2 * D] = d_keys[...].astype(BF)
        d_qkv[:, 2 * D :] = d_values[...].astype(BF)

    for index in range(FRAMES):
        rows = frame(index)
        hat, unused = normed(x_kept[rows, :].astype(F32))
        turned[:, rows] = jnp.swapaxes(
            (hat * (1.0 + group(index, 1)) + group(index, 0)).astype(BF), 0, 1
        )
    for part in range(3):
        grads.put(3 * part, mm(turned[...], d_qkv[:, part * D : (part + 1) * D]))
    grads.begin(0)
    weights.wait(0)
    d_normed = mm_nt(d_qkv[...], weights.columns(QKV, 9))
    for index in range(FRAMES):
        rows = frame(index)
        piece = d_normed[index * PATCHES : (index + 1) * PATCHES]
        hat, inverse = normed(x_kept[rows, :].astype(F32))
        add_by_video(totals, info, index, (column_sum(piece), column_sum(piece * hat), None))
        total = d_attend[rows, :] + norm_back(hat, inverse, piece * (1.0 + group(index, 1)))
        d_sent[rows, :] = total.astype(BF)
        d_input[rows, :] = total
    put_totals(d_mod, totals)
    grads.finish()


def mix_back_call(layer, info, mod, text, mask_column, d_after_cross, kept, sources, *after):
    return pl.pallas_call(
        following(mix_back_kernel, layer, 16, len(after)),
        out_shape=(
            shape_of(F32, ROWS, D), shape_of(BF, ROWS, D), shape_of(BF, HALF, 128), shape_of(BF, HALF, 128),
            shape_of(F32, TEXT, D), shape_of(F32, VIDS, 3 * D),
        ),
        in_specs=[pl.BlockSpec(memory_space=pltpu.SMEM)] + vmem_specs(12) + any_specs(3 + len(after)),
        out_specs=tuple(vmem_specs(2) + any_specs(2) + vmem_specs(2)),
        scratch_shapes=[
            pltpu.VMEM((ROWS, D), BF),
            pltpu.VMEM((D, ROWS), BF),
            pltpu.VMEM((ROWS, D), BF),
            pltpu.VMEM((ROWS, D), BF),
            pltpu.VMEM((TEXT, 2 * D), BF),
            pltpu.VMEM((ROWS, 3 * D), BF),
            pltpu.VMEM((ROWS, D), F32),
            pltpu.VMEM((ROWS, D), F32),
            pltpu.VMEM((ROWS, D), F32),
        ]
        + weight_scratch(MIXING_PIECES)
        + [pltpu.VMEM((PACKED, 128), BF), pltpu.SemaphoreType.DMA((2,))],
        compiler_params=params(),
        cost_estimate=cost(0.05),
        name="mix_back",
    )(info, mod, text, mask_column, d_after_cross, *kept, *sources, *after)


def unpack_kernel(
    info, mine, other, qkv, out, cross, query, keyval, up, down, halves, arrived, left,
    t_qkv, t_out, t_cross, t_query, t_keyval, t_up, t_down,
):
    core = info[1]
    loads = (
        pltpu.make_async_copy(
            mine.at[:, pl.ds(0, SHARE), :], halves.at[core], arrived.at[0]
        ),
        pltpu.make_async_copy(
            other.at[:, pl.ds(0, SHARE), :], halves.at[1 - core], arrived.at[1]
        ),
    )
    for load in loads:
        load.start()
    for load in loads:
        load.wait()
    stores = []

    def leave(source, target):
        store = pltpu.make_async_copy(source, target.at[0], left.at[len(stores)])
        store.start()
        stores.append(store)

    def block_of(half, at):
        pieces = []
        while True:
            share, inside = divmod(at, SHARE)
            count = min(SHARE - inside, D - sum(piece.shape[0] for piece in pieces))
            pieces.append(halves[half, share, inside : inside + count, :])
            at += count
            if sum(piece.shape[0] for piece in pieces) == D:
                return jnp.concatenate(pieces, axis=0).astype(F32)

    for half, members in enumerate(
        (((t_qkv, qkv, 9), (t_out, out, 3)), ((t_cross, cross, 3), (t_query, query, 3), (t_keyval, keyval, 6)))
    ):
        at = 0
        for held, target, count in members:
            for block in range(count):
                held[:, block * 128 : (block + 1) * 128] = block_of(half, at)
                at += D
            leave(held, target)
    for block in range(12):
        t_up[:, block * 128 : (block + 1) * 128] = block_of(0, HALF + block * D)
    leave(t_up, up)
    for block in range(12):
        t_down[block * 128 : (block + 1) * 128, :] = jnp.swapaxes(
            block_of(1, HALF + block * D), 0, 1
        )
    leave(t_down, down)
    for store in stores:
        store.wait()


def unpack_call(info, mine, other):
    shapes = ((D, 3 * D), (D, D), (D, D), (D, D), (D, 2 * D), (D, FF), (FF, D))
    return pl.pallas_call(
        unpack_kernel,
        out_shape=tuple(shape_of(F32, 1, *shape) for shape in shapes),
        in_specs=[pl.BlockSpec(memory_space=pltpu.SMEM)] + any_specs(2),
        out_specs=tuple(any_specs(len(shapes))),
        scratch_shapes=[
            pltpu.VMEM((2, 32, SHARE, 128), BF),
            pltpu.SemaphoreType.DMA((2,)),
            pltpu.SemaphoreType.DMA((len(shapes),)),
        ]
        + [pltpu.VMEM(shape, F32) for shape in shapes],
        compiler_params=params(),
        name="unpack",
    )(info, mine, other)


CHUNK = HALF // 4


def join_kernel(has_extra, keep_feed, got_feed, keep_mixing, got_mixing, *rest):
    extra = rest[0] if has_extra else None
    joined, held, total, arrived, left = rest[-5:]
    height = SHARE + (EXTRA if has_extra else 0)
    loads = []
    for part, (keep, got) in enumerate(((keep_mixing, got_mixing), (keep_feed, got_feed))):
        for piece in range(4):
            rows = pl.ds(piece * CHUNK, CHUNK)
            slot = part * 4 + piece
            for side, source in enumerate((keep, got)):
                load = pltpu.make_async_copy(
                    source.at[rows, :], held.at[side, pl.ds(slot * CHUNK, CHUNK), :],
                    arrived.at[side, slot],
                )
                load.start()
                loads.append(load)
    stores = []
    shares = CHUNK // SHARE
    for slot in range(8):
        loads[2 * slot].wait()
        loads[2 * slot + 1].wait()
        for at in range(shares):
            share = slot * shares + at
            rows = slice(share * SHARE, (share + 1) * SHARE)
            total[share, :SHARE, :] = held[0, rows, :] + held[1, rows, :]
            if has_extra:
                total[share, SHARE:, :] = extra[...]
        store = pltpu.make_async_copy(
            total.at[pl.ds(slot * shares, shares)], joined.at[pl.ds(slot * shares, shares)],
            left.at[slot],
        )
        store.start()
        stores.append(store)
    for store in stores:
        store.wait()


def join_call(keep_feed, got_feed, keep_mixing, got_mixing, extra, *after):
    has_extra = extra is not None
    height = SHARE + (EXTRA if has_extra else 0)
    return pl.pallas_call(
        functools.partial(join_kernel, has_extra),
        out_shape=shape_of(BF, 32, height, 128),
        in_specs=any_specs(4) + vmem_specs(int(has_extra)) + any_specs(len(after)),
        out_specs=any_specs(1)[0],
        scratch_shapes=[
            pltpu.VMEM((2, PACKED, 128), BF),
            pltpu.VMEM((32, height, 128), BF),
            pltpu.SemaphoreType.DMA((2, 8)),
            pltpu.SemaphoreType.DMA((8,)),
        ],
        compiler_params=params(),
        name="join",
    )(keep_feed, got_feed, keep_mixing, got_mixing, *((extra,) if has_extra else ()), *after)


def gate_kernel(*refs):
    del refs


def gate(value, *after):
    return pl.pallas_call(
        gate_kernel,
        out_shape=shape_of(value.dtype, *value.shape),
        in_specs=any_specs(1 + len(after)),
        out_specs=any_specs(1)[0],
        input_output_aliases={0: 0},
        name="gate",
    )(value, *after)


def batch_groups():
    return [[2 * chip + core for chip in range(32)] for core in range(2)]


def core_swap(value):
    count = lax.axis_size("batch")
    return lax.ppermute(value, "batch", [(i, i ^ 1) for i in range(count)])


def section_swap(value):
    return lax.ppermute(value, "section", [(0, 1), (1, 0)])


def across_chips(value):
    return lax.all_to_all(value, "batch", 0, 0, axis_index_groups=batch_groups(), tiled=True)


def copied(shard):
    return across_chips(jnp.broadcast_to(shard[None], (32,) + shard.shape)).reshape(-1, 128)


def share_sum(arrived):
    return jnp.sum(arrived.astype(F32), axis=0).astype(BF)


def body(
    inputs, cotangent, text, text_mask, segments, time_index, time_table,
    w_qkv, w_out, w_query, w_keyval, w_cross, w_up, w_down, w_ada, b_ada,
):
    section = lax.axis_index("section")
    place = lax.axis_index("batch")
    core, chip = place % 2, place // 2
    first = section == 0

    weights = (w_qkv, w_out, w_query, w_keyval, w_cross, w_up, w_down)
    shard = section_swap(shard_call(place.astype(jnp.int32).reshape(1), weights))
    packed = pack_call(weights, shard)
    mine = copied(shard)

    frames = segments.reshape(MICRO, FRAMES, PATCHES)[:, :, 0]
    mask_row = text_mask.reshape(MICRO, TEXT)
    mask_column = text_mask.reshape(-1, 1)
    info = jnp.concatenate(
        [
            jnp.stack([section, core]),
            lax.dynamic_index_in_dim(frames, section, 0, keepdims=False),
        ]
    ).astype(jnp.int32)
    time_onehot = (time_index[:, None] == jnp.arange(STEPS)[None, :]).astype(BF)
    time_rows = mm(time_onehot, time_table)
    mod = mm(jax.nn.silu(time_rows).astype(BF), w_ada[0]) + b_ada
    mod_pairs = mod.reshape(MICRO, VIDS, 6 * D)
    mod_own = lax.dynamic_index_in_dim(mod_pairs, section, 0, keepdims=False)
    mod_other = section_swap(lax.dynamic_index_in_dim(mod_pairs, 1 - section, 0, keepdims=False))
    mod_other = gate(mod_other, packed)
    mods = (jnp.where(first, mod_own, mod_other), jnp.where(first, mod_other, mod_own))

    mine = gate(mine, packed, *mods)
    sources = (packed, mine, core_swap(mine))

    given = inputs
    results, states = [], []
    for layer in range(2):
        kept = mix_forward_call(layer, info, given, mods[layer], text, mask_row, sources)
        given, hidden, projected = feed_forward_call(layer, info, mods[layer], kept[8], sources)
        results.append(given)
        states.append((kept[:8], kept[8], hidden, projected))

    def feed_back(layer, given, *after):
        kept, after_cross, hidden, projected = states[layer]
        return feed_back_call(
            layer, info, given, mods[layer], after_cross, hidden, projected, sources, *after
        )

    def mix_back(layer, d_after_cross, *after):
        return mix_back_call(
            layer, info, mods[layer], text, mask_column, d_after_cross, states[layer][0],
            sources, *after,
        )

    result_other = section_swap(jnp.where(first, results[1], results[0]))
    d_after_cross, keep_feed, send_feed, d_mod_feed = feed_back(1, cotangent)
    d_unused, sent, keep_mixing, send_mixing, d_text_one, d_mod_mixing = mix_back(
        1, d_after_cross, result_other
    )
    d_mod_one = jnp.concatenate([d_mod_mixing, d_mod_feed], axis=1)
    early = join_call(
        keep_feed, core_swap(send_feed), keep_mixing, core_swap(send_mixing), None
    )
    d_after_cross, keep_feed, send_feed, d_mod_feed = feed_back(0, sent, early)
    early = across_chips(early)
    d_first, given, keep_mixing, send_mixing, d_text_zero, d_mod_mixing = mix_back(0, d_after_cross)
    d_mod_zero = jnp.concatenate([d_mod_mixing, d_mod_feed], axis=1)
    def by_clip(own, other):
        return jnp.concatenate([jnp.where(first, own, other), jnp.where(first, other, own)])

    outputs = by_clip(jnp.where(first, results[0], results[1]), result_other)
    d_text_low = (d_text_zero + d_text_one).astype(BF)
    d_mod_low = [member.astype(BF).reshape(-1, D) for member in (d_mod_zero, d_mod_one)]
    packet = section_swap(
        jnp.concatenate([jnp.where(first, d_mod_low[1], d_mod_low[0]), d_text_low])
    )
    mod_rows = d_mod_low[0].shape[0]
    d_mod_clips = by_clip(
        jnp.where(first, d_mod_low[0], d_mod_low[1]), packet[:mod_rows]
    ).reshape(MICRO * VIDS, 6 * D)
    text_grad = by_clip(d_text_low, packet[mod_rows:]).astype(F32)
    digits = jnp.stack([time_index // 32, time_index % 32], axis=1).astype(BF)
    wide = jnp.concatenate(
        [d_mod_clips, time_rows.astype(BF), jnp.pad(digits, ((0, 0), (0, 126)))], axis=1
    ).reshape(MICRO * VIDS, 2, -1)
    wide_other = core_swap(lax.dynamic_index_in_dim(wide, 1 - core, 1, keepdims=False))
    wide_mine = lax.dynamic_index_in_dim(wide, core, 1, keepdims=False)
    extra = jnp.concatenate(
        [jnp.where(core == 0, wide_mine, wide_other), jnp.where(core == 0, wide_other, wide_mine)]
    ).reshape(EXTRA, 128)

    early = gate(early, given)
    late = across_chips(
        join_call(
            keep_feed, core_swap(send_feed), keep_mixing, core_swap(send_mixing), extra,
            early,
        )
    )
    early = share_sum(early)
    d_act_time = mm_nt(d_mod_clips, w_ada[0])
    unused, silu_back = jax.vjp(jax.nn.silu, time_rows)
    d_time_low = silu_back(d_act_time)[0].astype(BF)
    d_time_other = section_swap(d_time_low)
    d_time_sum = (d_time_low.astype(F32) + d_time_other.astype(F32)).astype(BF)
    d_time_swapped = core_swap(d_time_sum)
    d_time_chip = jnp.where(
        core == 0,
        jnp.concatenate([d_time_sum, d_time_swapped]),
        jnp.concatenate([d_time_swapped, d_time_sum]),
    ).reshape(TIMES, 128)
    late = gate(late, d_time_chip, early)
    last = share_sum(late[:, :SHARE])
    total = jnp.where(first, last, early).astype(F32) + section_swap(
        jnp.where(first, early, last)
    ).astype(F32)
    full = jnp.broadcast_to(
        jnp.concatenate([total.astype(BF), d_time_chip])[None], (32, SHARE + TIMES, 128)
    )
    given_other = section_swap(gate(jnp.where(first, sent, given), full))
    full = across_chips(full)
    d_input = by_clip(
        jnp.where(first, d_first, sent.astype(F32)), given_other.astype(F32)
    )
    columns = late[:, SHARE:].reshape(4 * 64, -1)
    columns_other = core_swap(columns)
    every = jnp.concatenate(
        [
            jnp.where(core == 0, columns, columns_other),
            jnp.where(core == 0, columns_other, columns),
        ],
        axis=1,
    )
    every_mod = every[:, : 6 * D]
    every_rows = every[:, 6 * D : 7 * D].astype(F32)
    every_digits = every[:, 7 * D : 7 * D + 2].astype(jnp.int32)
    every_index = every_digits[:, 0] * 32 + every_digits[:, 1]
    g_bias = jnp.sum(every_mod.astype(F32), axis=0)
    g_ada = mm_tn(jax.nn.silu(every_rows).astype(BF), every_mod)
    every_time = full[:, SHARE:].reshape(4 * 64, D)
    table_grad = mm_tn(
        (every_index[:, None] == jnp.arange(STEPS)[None, :]).astype(BF), every_time
    )
    full = gate(full, g_ada, g_bias, given_other)
    grads = unpack_call(info, full, core_swap(full))
    g_qkv, g_out, g_cross, g_query, g_keyval, g_up, g_down = grads
    return (
        outputs[None], d_input[None], text_grad, table_grad, g_qkv, g_out, g_query, g_keyval,
        g_cross, g_up, g_down, g_ada[None], g_bias[None],
    )


def solution(mesh):
    return jax.shard_map(
        body,
        mesh=mesh,
        in_specs=(
            P("batch", None),
            P("batch", None),
            P("batch", None),
            P("batch"),
            P("batch"),
            P("batch"),
            P(),
            P("section", None, None),
            P("section", None, None),
            P("section", None, None),
            P("section", None, None),
            P("section", None, None),
            P("section", None, None),
            P("section", None, None),
            P("section", None, None),
            P("section", None),
        ),
        out_specs=(
            P("section", "batch", None),
            P("section", "batch", None),
            P("batch", None),
            P(),
            P("section", None, None),
            P("section", None, None),
            P("section", None, None),
            P("section", None, None),
            P("section", None, None),
            P("section", None, None),
            P("section", None, None),
            P("section", None, None),
            P("section", None),
        ),
        check_vma=False,
    )
```

```python
import functools
import jax
import jax.numpy as jnp
from jax import lax
from jax.experimental import pallas as pl
from jax.experimental.pallas import tpu as pltpu
from jax.sharding import PartitionSpec as P

D = 384
HEADS = 6
HEAD = 64
FF = 1536
PATCHES = 128
FRAMES = 4
VIDS = 2
TXT = 64
MICRO = 2
STEPS = 1000
ROWS = FRAMES * PATCHES
TEXT = VIDS * TXT
BLOCKS = 24
PACKED = BLOCKS * D
HALF = PACKED // 2
SHARE = PACKED // 32
EXTRA = 88
TIMES = 24
MODS = 6 * VIDS
PAIRS = HEADS // 2
SCORE_SCALE = 0.125
NEGATIVE = -1000000000.0
EPSILON = 1e-06
F32 = jnp.float32
BF = jnp.bfloat16
VMEM_LIMIT = 56 * 1024 * 1024


def mm(left, right):
    return lax.dot_general(left, right, (((1,), (0,)), ((), ())), preferred_element_type=F32)


def mm_nt(left, right):
    return lax.dot_general(left, right, (((1,), (1,)), ((), ())), preferred_element_type=F32)


def mm_tn(left, right):
    return lax.dot_general(left, right, (((0,), (0,)), ((), ())), preferred_element_type=F32)


def frame(index):
    return pl.ds(index * PATCHES, PATCHES)


def normed(tensor):
    centre = tensor - jnp.sum(tensor, axis=-1, keepdims=True) * (1.0 / D)
    inverse = lax.rsqrt(jnp.sum(centre * centre, axis=-1, keepdims=True) * (1.0 / D) + EPSILON)
    return centre * inverse, inverse


def norm_back(hat, inverse, d_hat):
    first = jnp.sum(d_hat, axis=-1, keepdims=True) * (1.0 / D)
    second = jnp.sum(d_hat * hat, axis=-1, keepdims=True) * (1.0 / D)
    return inverse * (d_hat - first - hat * second)


def gelu_parts(hidden):
    square = hidden * hidden
    inner = hidden * (0.7978845608028654 + 0.035677408136300125 * square)
    tanh = jnp.tanh(inner)
    half = 0.5 * (1.0 + tanh)
    slope = half + 0.5 * hidden * (1.0 - tanh * tanh) * (
        0.7978845608028654 + 0.10703222440890037 * square
    )
    return hidden * half, slope


def gelu(hidden):
    inner = hidden * (0.7978845608028654 + 0.035677408136300125 * (hidden * hidden))
    return hidden * (0.5 + 0.5 * jnp.tanh(inner))


def half_masks():
    lane = lax.broadcasted_iota(jnp.int32, (1, 128), 1)
    low = (lane < HEAD).astype(F32)
    return low.astype(BF), (1.0 - low).astype(BF)


def stacked(pair, masks):
    return jnp.concatenate([pair * masks[0], pair * masks[1]], axis=0)


def folded(both):
    lane = lax.broadcasted_iota(jnp.int32, (PATCHES, 128), 1)
    return jnp.where(lane < HEAD, both[:PATCHES], both[PATCHES:])


def pair_attend(query, keys, values, allowed, masks):
    logits = mm_nt(stacked(query, masks), keys) * SCORE_SCALE
    if allowed is not None:
        logits = jnp.where(allowed, logits, NEGATIVE)
    raised = jnp.exp(logits - jnp.max(logits, axis=-1, keepdims=True))
    probs = raised * (1.0 / jnp.sum(raised, axis=-1, keepdims=True))
    return folded(mm(probs.astype(BF), values)).astype(BF)


def pair_back(query, keys, values, d_mixed, allowed, masks):
    both_query = stacked(query, masks)
    both_d = stacked(d_mixed, masks)
    logits = mm_nt(keys, both_query) * SCORE_SCALE
    if allowed is not None:
        logits = jnp.where(allowed, logits, NEGATIVE)
    raised = jnp.exp(logits - jnp.max(logits, axis=0, keepdims=True))
    probs = raised * (1.0 / jnp.sum(raised, axis=0, keepdims=True))
    d_probs = mm_nt(values, both_d)
    weighed = probs * d_probs
    d_scores = (
        SCORE_SCALE * (weighed - probs * jnp.sum(weighed, axis=0, keepdims=True))
    ).astype(BF)
    d_query = folded(mm_tn(d_scores, keys))
    d_keys = mm(d_scores, both_query)
    d_values = mm(probs.astype(BF), both_d)
    return d_query, d_keys, d_values


def head_maps():
    feature = lax.broadcasted_iota(jnp.int32, (D, 128), 0) // HEAD
    lane = lax.broadcasted_iota(jnp.int32, (D, 128), 1)
    gather = (feature == lane).astype(F32).astype(BF)
    feature = lax.broadcasted_iota(jnp.int32, (128, D), 1) // HEAD
    lane = lax.broadcasted_iota(jnp.int32, (128, D), 0)
    return gather, (feature == lane).astype(F32).astype(BF)


def temporal_probs(query, keys, same, gather):
    products = jnp.concatenate([(query * key).astype(BF) for key in keys], axis=0)
    scores = mm(products, gather) * SCORE_SCALE
    logits = [
        jnp.where(same[other], scores[other * PATCHES : (other + 1) * PATCHES], NEGATIVE)
        for other in range(FRAMES)
    ]
    top = functools.reduce(jnp.maximum, logits)
    raised = [jnp.exp(member - top) for member in logits]
    scale = 1.0 / functools.reduce(jnp.add, raised)
    return [member * scale for member in raised]


def spread(members, expand):
    wide = mm(jnp.concatenate([member.astype(BF) for member in members], axis=0), expand)
    return [wide[other * PATCHES : (other + 1) * PATCHES] for other in range(FRAMES)]


def vmem_specs(count):
    return [pl.BlockSpec(memory_space=pltpu.VMEM)] * count


def any_specs(count):
    return [pl.BlockSpec(memory_space=pl.ANY)] * count


def params():
    return pltpu.CompilerParams(vmem_limit_bytes=VMEM_LIMIT)


def cost(micros):
    return pl.CostEstimate(flops=int(micros * 1e9), bytes_accessed=1 << 20, transcendentals=0)


def shape_of(dtype, *shape):
    return jax.ShapeDtypeStruct(shape, dtype)


class Weights:
    def __init__(self, info, layer, sources, held, arrived, pieces, shift):
        self.own, self.mine, self.other = sources
        self.done = False
        self.held, self.arrived, self.pieces = held, arrived, pieces
        is_own = info[0] == layer
        for slot, (start, count) in enumerate(pieces):
            half = start // HALF
            into = held.at[pl.ds(start, count), :]
            inside = start - half * HALF + shift

            def begin(source, at, into=into, slot=slot, count=count):
                pltpu.make_async_copy(
                    source.at[pl.ds(at, count), :], into, arrived.at[slot]
                ).start()

            pl.when(is_own)(functools.partial(begin, self.own, half * PACKED + inside))
            pl.when(jnp.logical_not(is_own) & (info[1] == half))(
                functools.partial(begin, self.mine, inside)
            )
            pl.when(jnp.logical_not(is_own) & (info[1] != half))(
                functools.partial(begin, self.other, inside)
            )

    def wait(self, slot):
        if self.done:
            return
        start, count = self.pieces[slot]
        rows = pl.ds(start, count)
        pltpu.make_async_copy(
            self.own.at[rows, :], self.held.at[rows, :], self.arrived.at[slot]
        ).wait()

    def columns(self, block, count):
        return jnp.concatenate(
            [self.held[(block + at) * D : (block + at + 1) * D, :] for at in range(count)], axis=1
        )


class Gradients:
    def __init__(self, info, kept, keep, send, left):
        self.info, self.kept, self.keep, self.send, self.left = info, kept, keep, send, left

    def put(self, block, fresh):
        for offset in range(fresh.shape[1] // 128):
            at = (block + offset) * D
            if not isinstance(at, int):
                at = pl.multiple_of(at, D)
            self.kept[pl.ds(at, D), :] = fresh[:, offset * 128 : (offset + 1) * 128].astype(BF)

    def copy(self, half, target):
        return pltpu.make_async_copy(
            self.kept.at[pl.ds(half * HALF, HALF), :], target, self.left.at[half]
        )

    def begin(self, half):
        pl.when(self.info[1] == half)(lambda: self.copy(half, self.keep).start())
        pl.when(self.info[1] != half)(lambda: self.copy(half, self.send).start())

    def finish(self):
        for half in range(2):
            self.copy(half, self.keep).wait()


MIXING_PIECES = ((0, 9 * D), (9 * D, 3 * D), (12 * D, 3 * D), (15 * D, 9 * D))
FEED_PIECES = ((0, 12 * D), (12 * D, 12 * D))
QKV, OUT, CROSS, QUERY, KEYVAL = 0, 9, 12, 15, 18


def weight_scratch(pieces):
    return [pltpu.VMEM((PACKED, 128), BF), pltpu.SemaphoreType.DMA((len(pieces),))]


def fill_packed(weights, held, after_part):
    w_qkv, w_out, w_query, w_keyval, w_cross, w_up, w_down = weights
    for half, members in enumerate(
        (((w_qkv, 9), (w_out, 3)), ((w_cross, 3), (w_query, 3), (w_keyval, 6)))
    ):
        at = half * PACKED
        for source, count in members:
            for block in range(count):
                held[at : at + D, :] = source[0, :, block * 128 : (block + 1) * 128]
                at += D
        after_part(half * PACKED)
    for block in range(12):
        at = HALF + block * D
        held[at : at + D, :] = w_up[0, :, block * 128 : (block + 1) * 128]
    after_part(HALF)
    for block in range(3):
        at = PACKED + HALF + block * FF
        held[at : at + FF, :] = w_down[0, :, block * 128 : (block + 1) * 128]
    after_part(PACKED + HALF)


def shard_kernel(place, *refs):
    weights, (shard, held) = refs[:7], refs[7:]
    fill_packed(weights, held, lambda start: None)
    start = (place[0] % 2) * PACKED + (place[0] // 2) * SHARE
    shard[...] = held[pl.ds(pl.multiple_of(start, SHARE), SHARE), :]


def shard_call(place, weights):
    return pl.pallas_call(
        shard_kernel,
        out_shape=shape_of(BF, SHARE, 128),
        in_specs=[pl.BlockSpec(memory_space=pltpu.SMEM)] + vmem_specs(len(weights)),
        out_specs=vmem_specs(1)[0],
        scratch_shapes=[pltpu.VMEM((2 * PACKED, 128), BF)],
        compiler_params=params(),
        name="shard",
    )(place, *weights)


def pack_kernel(*refs):
    weights, (after, packed, held, left) = refs[:7], refs[7:]
    copies = []

    def leave(start):
        rows = pl.ds(start, HALF)
        made = pltpu.make_async_copy(held.at[rows, :], packed.at[rows, :], left.at[len(copies)])
        made.start()
        copies.append(made)

    fill_packed(weights, held, leave)
    for made in copies:
        made.wait()


def pack_call(weights, after):
    return pl.pallas_call(
        pack_kernel,
        out_shape=shape_of(BF, 2 * PACKED, 128),
        in_specs=vmem_specs(len(weights)) + any_specs(1),
        out_specs=any_specs(1)[0],
        scratch_shapes=[pltpu.VMEM((2 * PACKED, 128), BF), pltpu.SemaphoreType.DMA((4,))],
        compiler_params=params(),
        name="pack",
    )(*weights, after)


def video_group(info, mod):
    def group(index, which):
        return mod[pl.ds(info[2 + index], 1), which * D : (which + 1) * D]

    return group


def mix_forward(layer, weights, info, given, mod, text, mask_row, kept, normed_rows):
    (
        x_kept, qkv, mixed, attended, after_attend, cross_query, text_kv, cross_mixed, after_cross
    ) = kept[:9]
    clip = info[0]
    masks = half_masks()
    group = video_group(info, mod)
    for index in range(FRAMES):
        rows = frame(index)
        if layer == 0:
            x_kept[rows, :] = given[pl.ds(clip * ROWS + index * PATCHES, PATCHES), :]
        x = x_kept[rows, :]
        hat, unused = normed(x.astype(F32))
        normed_rows[rows, :] = (hat * (1.0 + group(index, 1)) + group(index, 0)).astype(BF)
    weights.wait(0)
    for part in range(3):
        qkv[:, part * D : (part + 1) * D] = mm(
            normed_rows[...], weights.columns(QKV + 3 * part, 3)
        ).astype(BF)

    def spatial(index, carry):
        rows = frame(index)
        for pair in range(PAIRS):
            mixed[rows, pair * 128 : (pair + 1) * 128] = pair_attend(
                qkv[rows, pair * 128 : (pair + 1) * 128],
                qkv[rows, D + pair * 128 : D + (pair + 1) * 128],
                qkv[rows, 2 * D + pair * 128 : 2 * D + (pair + 1) * 128],
                None,
                masks,
            )
        return carry

    def temporal(index, carry):
        gather, expand = head_maps()
        rows = frame(index)
        query = qkv[rows, :D].astype(F32)
        keys = [qkv[frame(at), D : 2 * D].astype(F32) for at in range(FRAMES)]
        same = [info[2 + at] == info[2 + index] for at in range(FRAMES)]
        wide = spread(temporal_probs(query, keys, same, gather), expand)
        total = sum(wide[at] * qkv[frame(at), 2 * D :].astype(F32) for at in range(FRAMES))
        mixed[rows, :] = total.astype(BF)
        return carry

    lax.fori_loop(0, FRAMES, spatial if layer == 0 else temporal, 0, unroll=True)
    weights.wait(1)
    projection = mm(mixed[...], weights.columns(OUT, 3))
    for index in range(FRAMES):
        rows = frame(index)
        piece = projection[index * PATCHES : (index + 1) * PATCHES]
        attended[rows, :] = piece.astype(BF)
        state = x_kept[rows, :].astype(F32) + group(index, 2) * piece
        after_attend[rows, :] = state
        normed_rows[rows, :] = normed(state)[0].astype(BF)
    weights.wait(2)
    weights.wait(3)
    cross_query[...] = mm(normed_rows[...], weights.columns(QUERY, 3)).astype(BF)
    text_rows = text[pl.ds(clip * TEXT, TEXT), :]
    text_kv[...] = mm(text_rows, weights.columns(KEYVAL, 6)).astype(BF)
    owner = lax.broadcasted_iota(jnp.int32, (1, TEXT), 1) // TXT
    real = mask_row[pl.ds(clip, 1), :] == 1

    def cross(index, carry):
        rows = frame(index)
        allowed = real & (owner == info[2 + index])
        for pair in range(PAIRS):
            cross_mixed[rows, pair * 128 : (pair + 1) * 128] = pair_attend(
                cross_query[rows, pair * 128 : (pair + 1) * 128],
                text_kv[:, pair * 128 : (pair + 1) * 128],
                text_kv[:, D + pair * 128 : D + (pair + 1) * 128],
                allowed,
                masks,
            )
        return carry

    lax.fori_loop(0, FRAMES, cross, 0, unroll=True)
    projection = mm(cross_mixed[...], weights.columns(CROSS, 3))
    for index in range(FRAMES):
        rows = frame(index)
        after_cross[rows, :] = (
            after_attend[rows, :] + projection[index * PATCHES : (index + 1) * PATCHES]
        )


def feed_forward(layer, weights, info, mod, kept, result, normed_rows, activated):
    after_cross, hidden, projected = kept[8:]
    held = weights.held
    group = video_group(info, mod)
    for index in range(FRAMES):
        rows = frame(index)
        hat, unused = normed(after_cross[rows, :])
        normed_rows[rows, :] = (hat * (1.0 + group(index, 4)) + group(index, 3)).astype(BF)
    weights.wait(0)
    for chunk in range(FF // 256):
        columns = slice(chunk * 256, (chunk + 1) * 256)
        raw = mm(normed_rows[...], weights.columns(2 * chunk, 2))
        hidden[:, columns] = raw.astype(BF)
        activated[:, columns] = gelu(raw).astype(BF)
    weights.wait(1)
    down = jnp.concatenate(
        [held[HALF + block * FF : HALF + (block + 1) * FF, :] for block in range(3)], axis=1
    )
    projection = mm(activated[...], down)
    for index in range(FRAMES):
        rows = frame(index)
        piece = projection[index * PATCHES : (index + 1) * PATCHES]
        projected[rows, :] = piece.astype(BF)
        result[rows, :] = (after_cross[rows, :] + group(index, 5) * piece).astype(BF)


def column_sum(tensor):
    return jnp.sum(tensor, axis=0, keepdims=True)


def add_by_video(totals, info, index, terms):
    for video in range(VIDS):
        for slot, term in enumerate(terms):
            if term is not None:
                totals[video][slot] = totals[video][slot] + jnp.where(
                    info[2 + index] == video, term, 0.0
                )


def no_totals():
    return [[jnp.zeros((1, D), F32) for unused in range(3)] for unused in range(VIDS)]


def put_totals(d_mod, totals, group):
    for member in range(VIDS):
        for slot in range(3):
            row = member * 6 + group + slot
            d_mod[row : row + 1, :] = totals[member][slot]


def feed_back(layer, weights, info, given, mod, kept, d_after_cross, grads, d_mod, work):
    after_cross, hidden, projected = kept[8:]
    normed_turned, d_turned, d_low, d_active, d_hidden = work
    held = weights.held
    clip = info[0]
    totals = no_totals()
    group = video_group(info, mod)

    def incoming(index):
        if layer == 1:
            return given[pl.ds(clip * ROWS + index * PATCHES, PATCHES), :].astype(F32)
        return given[frame(index), :].astype(F32)

    for index in range(FRAMES):
        rows = frame(index)
        grad = incoming(index)
        low = (grad * group(index, 5)).astype(BF)
        d_low[rows, :] = low
        d_turned[:, rows] = jnp.swapaxes(low, 0, 1)
        d_gate = column_sum(grad * projected[rows, :].astype(F32))
        add_by_video(totals, info, index, (None, None, d_gate))
        hat, unused = normed(after_cross[rows, :])
        normed_turned[:, rows] = jnp.swapaxes(
            (hat * (1.0 + group(index, 4)) + group(index, 3)).astype(BF), 0, 1
        )
    weights.wait(1)
    weights.wait(0)

    def feed(chunk, carry):
        columns = pl.ds(pl.multiple_of(chunk * 256, 256), 256)
        down = jnp.concatenate(
            [
                held[pl.ds(pl.multiple_of(HALF + block * FF + chunk * 256, 256), 256), :]
                for block in range(3)
            ],
            axis=1,
        )
        d_active[...] = mm_nt(d_low[...], down)
        for piece in range(8):
            rows = pl.ds(piece * 64, 64)
            active, slope = gelu_parts(hidden[rows, columns].astype(F32))
            d_hidden[rows, columns] = (d_active[rows, :] * slope).astype(BF)
            d_active[rows, :] = active
        grads.put(2 * chunk, mm(normed_turned[...], d_hidden[:, columns]))
        grads.put(12 + 2 * chunk, mm(d_turned[...], d_active[...].astype(BF)))
        return carry

    lax.fori_loop(0, FF // 256, feed, 0, unroll=True)
    grads.begin(0)
    grads.begin(1)
    d_normed = mm_nt(d_hidden[...], weights.columns(0, 12))
    for index in range(FRAMES):
        rows = frame(index)
        grad = incoming(index)
        piece = d_normed[index * PATCHES : (index + 1) * PATCHES]
        hat, inverse = normed(after_cross[rows, :])
        add_by_video(totals, info, index, (column_sum(piece), column_sum(piece * hat), None))
        d_after_cross[rows, :] = grad + norm_back(hat, inverse, piece * (1.0 + group(index, 4)))
    put_totals(d_mod, totals, 3)


def mix_back(
    layer, weights, info, mod, text, mask_column, d_after_cross, kept, d_input, d_sent, grads,
    d_text, d_mod, work,
):
    (
        x_kept, qkv, mixed, attended, after_attend, cross_query, text_kv, cross_mixed
    ) = kept[:8]
    low, turned, d_heads, d_query, d_text_kv, d_qkv, d_attend, d_keys, d_values = work
    clip = info[0]
    totals = no_totals()
    masks = half_masks()
    group = video_group(info, mod)

    for index in range(FRAMES):
        rows = frame(index)
        low[rows, :] = d_after_cross[rows, :].astype(BF)
        turned[:, rows] = jnp.swapaxes(cross_mixed[rows, :], 0, 1)
    grads.put(CROSS, mm(turned[...], low[...]))
    weights.wait(2)
    weights.wait(3)
    d_heads[...] = mm_nt(low[...], weights.columns(CROSS, 3)).astype(BF)
    owner = lax.broadcasted_iota(jnp.int32, (TEXT, 1), 0) // TXT
    real = mask_column[pl.ds(clip * TEXT, TEXT), :] == 1
    d_keys[...] = jnp.zeros_like(d_keys)
    d_values[...] = jnp.zeros_like(d_values)

    def cross(index, carry):
        rows = frame(index)
        allowed = real & (owner == info[2 + index])
        for pair in range(PAIRS):
            columns = slice(pair * 128, (pair + 1) * 128)
            late = slice(D + pair * 128, D + (pair + 1) * 128)
            one, two, three = pair_back(
                cross_query[rows, columns], text_kv[:, columns], text_kv[:, late],
                d_heads[rows, columns], allowed, masks,
            )
            d_query[rows, columns] = one.astype(BF)
            d_keys[: TEXT, columns] += two
            d_values[: TEXT, columns] += three
        return carry

    lax.fori_loop(0, FRAMES, cross, 0, unroll=True)
    d_text_kv[:, :D] = d_keys[: TEXT, :].astype(BF)
    d_text_kv[:, D:] = d_values[: TEXT, :].astype(BF)
    text_turned = jnp.swapaxes(text[pl.ds(clip * TEXT, TEXT), :], 0, 1)
    grads.put(KEYVAL, mm(text_turned, d_text_kv[...]))
    d_text[...] = mm_nt(d_text_kv[...], weights.columns(KEYVAL, 6))
    for index in range(FRAMES):
        rows = frame(index)
        hat, unused = normed(after_attend[rows, :])
        turned[:, rows] = jnp.swapaxes(hat.astype(BF), 0, 1)
    grads.put(QUERY, mm(turned[...], d_query[...]))
    grads.begin(1)
    d_normed = mm_nt(d_query[...], weights.columns(QUERY, 3))
    for index in range(FRAMES):
        rows = frame(index)
        piece = d_normed[index * PATCHES : (index + 1) * PATCHES]
        hat, inverse = normed(after_attend[rows, :])
        total = d_after_cross[rows, :] + norm_back(hat, inverse, piece)
        d_attend[rows, :] = total
        low[rows, :] = (total * group(index, 2)).astype(BF)
        add_by_video(
            totals, info, index, (None, None, column_sum(total * attended[rows, :].astype(F32)))
        )
        turned[:, rows] = jnp.swapaxes(mixed[rows, :], 0, 1)
    grads.put(OUT, mm(turned[...], low[...]))
    weights.wait(1)
    d_heads[...] = mm_nt(low[...], weights.columns(OUT, 3)).astype(BF)

    if layer == 0:
        def one_frame(index, carry):
            rows = frame(index)
            for pair in range(PAIRS):
                columns = slice(pair * 128, (pair + 1) * 128)
                second = slice(D + pair * 128, D + (pair + 1) * 128)
                third = slice(2 * D + pair * 128, 2 * D + (pair + 1) * 128)
                one, two, three = pair_back(
                    qkv[rows, columns], qkv[rows, second], qkv[rows, third],
                    d_heads[rows, columns], None, masks,
                )
                d_qkv[rows, columns] = one.astype(BF)
                d_qkv[rows, second] = two.astype(BF)
                d_qkv[rows, third] = three.astype(BF)
            return carry

        lax.fori_loop(0, FRAMES, one_frame, 0, unroll=True)

    else:
        gather, expand = head_maps()
        d_keys[...] = jnp.zeros_like(d_keys)
        d_values[...] = jnp.zeros_like(d_values)

        def one_frame(index, carry):
            rows = frame(index)
            query = qkv[rows, :D].astype(F32)
            d_mixed = d_heads[rows, :].astype(F32)
            keys = [qkv[frame(at), D : 2 * D].astype(F32) for at in range(FRAMES)]
            same = [info[2 + at] == info[2 + index] for at in range(FRAMES)]
            probs = temporal_probs(query, keys, same, gather)
            products = jnp.concatenate(
                [
                    (d_mixed * qkv[frame(at), 2 * D :].astype(F32)).astype(BF)
                    for at in range(FRAMES)
                ],
                axis=0,
            )
            d_probs = mm(products, gather)
            weighed = [
                probs[at] * d_probs[at * PATCHES : (at + 1) * PATCHES]
                for at in range(FRAMES)
            ]
            total = functools.reduce(jnp.add, weighed)
            d_scores = [
                SCORE_SCALE * (weighed[at] - probs[at] * total) for at in range(FRAMES)
            ]
            wide_probs = spread(probs, expand)
            wide_scores = spread(d_scores, expand)
            d_one = jnp.zeros((PATCHES, D), F32)
            for at in range(FRAMES):
                d_one = d_one + wide_scores[at] * keys[at]
                d_keys[frame(at), :] += wide_scores[at] * query
                d_values[frame(at), :] += wide_probs[at] * d_mixed
            d_qkv[rows, :D] = d_one.astype(BF)
            return carry

        lax.fori_loop(0, FRAMES, one_frame, 0, unroll=True)
        d_qkv[:, D : 2 * D] = d_keys[...].astype(BF)
        d_qkv[:, 2 * D :] = d_values[...].astype(BF)

    for index in range(FRAMES):
        rows = frame(index)
        hat, unused = normed(x_kept[rows, :].astype(F32))
        turned[:, rows] = jnp.swapaxes(
            (hat * (1.0 + group(index, 1)) + group(index, 0)).astype(BF), 0, 1
        )
    for part in range(3):
        grads.put(3 * part, mm(turned[...], d_qkv[:, part * D : (part + 1) * D]))
    grads.begin(0)
    weights.wait(0)
    d_normed = mm_nt(d_qkv[...], weights.columns(QKV, 9))
    for index in range(FRAMES):
        rows = frame(index)
        piece = d_normed[index * PATCHES : (index + 1) * PATCHES]
        hat, inverse = normed(x_kept[rows, :].astype(F32))
        add_by_video(totals, info, index, (column_sum(piece), column_sum(piece * hat), None))
        total = d_attend[rows, :] + norm_back(hat, inverse, piece * (1.0 + group(index, 1)))
        d_sent[rows, :] = total.astype(BF)
        if d_input is not None:
            d_input[rows, :] = total
    put_totals(d_mod, totals, 0)


KEPT = (
    (BF, ROWS, D), (BF, ROWS, 3 * D), (BF, ROWS, D), (BF, ROWS, D), (F32, ROWS, D), (BF, ROWS, D),
    (BF, TEXT, 2 * D), (BF, ROWS, D), (F32, ROWS, D), (BF, ROWS, FF), (BF, ROWS, D),
)
FEED_WORK = (
    (BF, D, ROWS), (BF, D, ROWS), (BF, ROWS, D), (F32, ROWS, 256), (BF, ROWS, FF)
)
MIX_WORK = (
    (BF, ROWS, D), (BF, D, ROWS), (BF, ROWS, D), (BF, ROWS, D), (BF, TEXT, 2 * D),
    (BF, ROWS, 3 * D), (F32, ROWS, D), (F32, ROWS, D), (F32, ROWS, D),
)


def scratch(shapes):
    return [pltpu.VMEM(tuple(shape[1:]), shape[0]) for shape in shapes]


def grad_scratch():
    return [pltpu.VMEM((PACKED, 128), BF), pltpu.SemaphoreType.DMA((2,))]


def both_weights(info, layer, sources, mixing_refs, feed_refs):
    return (
        Weights(info, layer, sources, *mixing_refs, MIXING_PIECES, 0),
        Weights(info, layer, sources, *feed_refs, FEED_PIECES, HALF),
    )


def first_kernel(
    info, inputs, cotangent, mod_zero, mod_one, text, mask_row, mask_column, own, mine, other, *rest
):
    rest = iter(rest)
    take = lambda count: [next(rest) for unused in range(count)]
    result_zero, result_one, sent, d_text, d_mod = take(5)
    keep_feed, send_feed, keep_mixing, send_mixing = take(4)
    left_kept = take(11)
    kept_zero, kept_one = take(11), take(10)
    feed_work, mix_work = take(5), take(9)
    normed_rows, activated, d_after_cross = take(3)
    sources = (own, mine, other)
    mixing_zero, feed_zero = both_weights(info, 0, sources, take(2), take(2))
    mixing_one, feed_one = both_weights(info, 1, sources, take(2), take(2))
    feed_grads = Gradients(info, *take(1), keep_feed, send_feed, *take(1))
    mixing_grads = Gradients(info, *take(1), keep_mixing, send_mixing, *take(1))
    leaving = take(1)[0]
    mix_forward(0, mixing_zero, info, inputs, mod_zero, text, mask_row, kept_zero, normed_rows)
    feed_forward(0, feed_zero, info, mod_zero, kept_zero, result_zero, normed_rows, activated)
    copies = [
        pltpu.make_async_copy(held, target, leaving.at[slot])
        for slot, (held, target) in enumerate(zip(kept_zero, left_kept))
    ]
    for copy in copies:
        copy.start()
    kept_one = [result_zero] + kept_one
    mix_forward(1, mixing_one, info, None, mod_one, text, mask_row, kept_one, normed_rows)
    feed_forward(1, feed_one, info, mod_one, kept_one, result_one, normed_rows, activated)
    feed_one.done = mixing_one.done = True
    feed_back(
        1, feed_one, info, cotangent, mod_one, kept_one, d_after_cross, feed_grads, d_mod,
        feed_work,
    )
    mix_back(
        1, mixing_one, info, mod_one, text, mask_column, d_after_cross, kept_one, None, sent,
        mixing_grads, d_text, d_mod, mix_work,
    )
    feed_grads.finish()
    mixing_grads.finish()
    for copy in copies:
        copy.wait()


def first_call(info, inputs, cotangent, mods, text, mask_row, mask_column, sources):
    return pl.pallas_call(
        first_kernel,
        out_shape=(
            shape_of(BF, ROWS, D), shape_of(BF, ROWS, D), shape_of(BF, ROWS, D),
            shape_of(F32, TEXT, D), shape_of(F32, MODS, D),
        )
        + (shape_of(BF, HALF, 128),) * 4
        + tuple(shape_of(*shape) for shape in KEPT),
        in_specs=[pl.BlockSpec(memory_space=pltpu.SMEM)] + vmem_specs(7) + any_specs(3),
        out_specs=tuple(vmem_specs(5) + any_specs(15)),
        scratch_shapes=scratch(KEPT) + scratch(KEPT[1:]) + scratch(FEED_WORK) + scratch(MIX_WORK)
        + scratch(((BF, ROWS, D), (BF, ROWS, FF), (F32, ROWS, D)))
        + weight_scratch(MIXING_PIECES) + weight_scratch(FEED_PIECES)
        + weight_scratch(MIXING_PIECES) + weight_scratch(FEED_PIECES)
        + grad_scratch() + grad_scratch() + [pltpu.SemaphoreType.DMA((11,))],
        compiler_params=params(),
        name="first",
    )(info, inputs, cotangent, *mods, text, mask_row, mask_column, *sources)


def second_kernel(info, given, mod, text, mask_column, d_text_one, own, mine, other, *rest):
    rest = iter(rest)
    take = lambda count: [next(rest) for unused in range(count)]
    held_kept = take(11)
    unused_after = take(2)
    d_input, d_sent, d_text_low, d_mod = take(4)
    keep_feed, send_feed, keep_mixing, send_mixing = take(4)
    kept = take(11)
    feed_work, mix_work = take(5), take(9)
    d_after_cross, d_text = take(2)
    arrived = take(1)[0]
    order = (8, 10, 9, 7, 5, 6, 4, 3, 2, 1, 0)
    copies = {
        slot: pltpu.make_async_copy(held_kept[slot], kept[slot], arrived.at[slot]) for slot in order
    }
    for slot in order[:2]:
        copies[slot].start()
    feed = Weights(info, 0, (own, mine, other), *take(2), FEED_PIECES, HALF)
    for slot in order[2:]:
        copies[slot].start()
    mixing = Weights(info, 0, (own, mine, other), *take(2), MIXING_PIECES, 0)
    feed_grads = Gradients(info, *take(1), keep_feed, send_feed, *take(1))
    mixing_grads = Gradients(info, *take(1), keep_mixing, send_mixing, *take(1))
    for slot in order[:3]:
        copies[slot].wait()
    feed_back(
        0, feed, info, given, mod, kept, d_after_cross, feed_grads, d_mod, feed_work
    )
    for slot in order[3:]:
        copies[slot].wait()
    mix_back(
        0, mixing, info, mod, text, mask_column, d_after_cross, kept, d_input, d_sent,
        mixing_grads, d_text, d_mod, mix_work,
    )
    d_text_low[...] = (d_text[...] + d_text_one[...]).astype(BF)
    feed_grads.finish()
    mixing_grads.finish()


def second_call(info, given, mod, text, mask_column, d_text_one, sources, kept, *after):
    return pl.pallas_call(
        second_kernel,
        out_shape=(
            shape_of(F32, ROWS, D), shape_of(BF, ROWS, D), shape_of(BF, TEXT, D),
            shape_of(F32, MODS, D),
        )
        + (shape_of(BF, HALF, 128),) * 4,
        in_specs=[pl.BlockSpec(memory_space=pltpu.SMEM)] + vmem_specs(5) + any_specs(16),
        out_specs=tuple(vmem_specs(4) + any_specs(4)),
        scratch_shapes=scratch(KEPT) + scratch(FEED_WORK) + scratch(MIX_WORK)
        + scratch(((F32, ROWS, D), (F32, TEXT, D))) + [pltpu.SemaphoreType.DMA((11,))]
        + weight_scratch(FEED_PIECES) + weight_scratch(MIXING_PIECES)
        + grad_scratch() + grad_scratch(),
        compiler_params=params(),
        name="second",
    )(info, given, mod, text, mask_column, d_text_one, *sources, *kept, *after)


def unpack_kernel(
    info, mine, other, qkv, out, cross, query, keyval, up, down, halves, arrived, left,
    t_qkv, t_out, t_cross, t_query, t_keyval, t_up, t_down,
):
    core = info[1]
    loads = []
    for part in (1, 0):
        shares = pl.ds(16 * part, 16)
        for side, (source, half) in enumerate(((mine, core), (other, 1 - core))):
            load = pltpu.make_async_copy(
                source.at[shares, pl.ds(0, SHARE), :], halves.at[half, shares],
                arrived.at[part, side],
            )
            load.start()
            loads.append(load)
    stores = []

    def leave(source, target):
        store = pltpu.make_async_copy(source, target.at[0], left.at[len(stores)])
        store.start()
        stores.append(store)

    def block_of(half, at):
        pieces = []
        while True:
            share, inside = divmod(at, SHARE)
            count = min(SHARE - inside, D - sum(piece.shape[0] for piece in pieces))
            pieces.append(halves[half, share, inside : inside + count, :])
            at += count
            if sum(piece.shape[0] for piece in pieces) == D:
                return jnp.concatenate(pieces, axis=0).astype(F32)

    for load in loads[:2]:
        load.wait()
    for block in range(12):
        t_up[:, block * 128 : (block + 1) * 128] = block_of(0, HALF + block * D)
    leave(t_up, up)
    for block in range(12):
        t_down[block * 128 : (block + 1) * 128, :] = jnp.swapaxes(
            block_of(1, HALF + block * D), 0, 1
        )
    leave(t_down, down)
    for load in loads[2:]:
        load.wait()
    for half, members in enumerate(
        (((t_qkv, qkv, 9), (t_out, out, 3)), ((t_cross, cross, 3), (t_query, query, 3), (t_keyval, keyval, 6)))
    ):
        at = 0
        for held, target, count in members:
            for block in range(count):
                held[:, block * 128 : (block + 1) * 128] = block_of(half, at)
                at += D
            leave(held, target)
    for store in stores:
        store.wait()


def unpack_call(info, mine, other):
    shapes = ((D, 3 * D), (D, D), (D, D), (D, D), (D, 2 * D), (D, FF), (FF, D))
    return pl.pallas_call(
        unpack_kernel,
        out_shape=tuple(shape_of(F32, 1, *shape) for shape in shapes),
        in_specs=[pl.BlockSpec(memory_space=pltpu.SMEM)] + any_specs(2),
        out_specs=tuple(any_specs(len(shapes))),
        scratch_shapes=[
            pltpu.VMEM((2, 32, SHARE, 128), BF),
            pltpu.SemaphoreType.DMA((2, 2)),
            pltpu.SemaphoreType.DMA((len(shapes),)),
        ]
        + [pltpu.VMEM(shape, F32) for shape in shapes],
        compiler_params=params(),
        name="unpack",
    )(info, mine, other)


CHUNK = HALF // 4


def join_kernel(has_extra, keep_feed, got_feed, keep_mixing, got_mixing, *rest):
    extra = rest[0] if has_extra else None
    joined, held, total, arrived, left = rest[-5:]
    height = SHARE + (EXTRA if has_extra else 0)
    loads = []
    for part, (keep, got) in enumerate(((keep_mixing, got_mixing), (keep_feed, got_feed))):
        for piece in range(4):
            rows = pl.ds(piece * CHUNK, CHUNK)
            slot = part * 4 + piece
            for side, source in enumerate((keep, got)):
                load = pltpu.make_async_copy(
                    source.at[rows, :], held.at[side, pl.ds(slot * CHUNK, CHUNK), :],
                    arrived.at[side, slot],
                )
                load.start()
                loads.append(load)
    stores = []
    shares = CHUNK // SHARE
    for slot in range(8):
        loads[2 * slot].wait()
        loads[2 * slot + 1].wait()
        for at in range(shares):
            share = slot * shares + at
            rows = slice(share * SHARE, (share + 1) * SHARE)
            total[share, :SHARE, :] = held[0, rows, :] + held[1, rows, :]
            if has_extra:
                total[share, SHARE:, :] = extra[...]
        store = pltpu.make_async_copy(
            total.at[pl.ds(slot * shares, shares)], joined.at[pl.ds(slot * shares, shares)],
            left.at[slot],
        )
        store.start()
        stores.append(store)
    for store in stores:
        store.wait()


def join_call(keep_feed, got_feed, keep_mixing, got_mixing, extra, *after):
    has_extra = extra is not None
    height = SHARE + (EXTRA if has_extra else 0)
    return pl.pallas_call(
        functools.partial(join_kernel, has_extra),
        out_shape=shape_of(BF, 32, height, 128),
        in_specs=any_specs(4) + vmem_specs(int(has_extra)) + any_specs(len(after)),
        out_specs=any_specs(1)[0],
        scratch_shapes=[
            pltpu.VMEM((2, PACKED, 128), BF),
            pltpu.VMEM((32, height, 128), BF),
            pltpu.SemaphoreType.DMA((2, 8)),
            pltpu.SemaphoreType.DMA((8,)),
        ],
        compiler_params=params(),
        name="join",
    )(keep_feed, got_feed, keep_mixing, got_mixing, *((extra,) if has_extra else ()), *after)


def gate_kernel(*refs):
    del refs


def gate(value, *after):
    return pl.pallas_call(
        gate_kernel,
        out_shape=shape_of(value.dtype, *value.shape),
        in_specs=any_specs(1 + len(after)),
        out_specs=any_specs(1)[0],
        input_output_aliases={0: 0},
        name="gate",
    )(value, *after)


def batch_groups():
    return [[2 * chip + core for chip in range(32)] for core in range(2)]


def core_swap(value):
    count = lax.axis_size("batch")
    return lax.ppermute(value, "batch", [(i, i ^ 1) for i in range(count)])


def section_swap(value):
    return lax.ppermute(value, "section", [(0, 1), (1, 0)])


def across_chips(value):
    return lax.all_to_all(value, "batch", 0, 0, axis_index_groups=batch_groups(), tiled=True)


def copied(shard):
    return across_chips(jnp.broadcast_to(shard[None], (32,) + shard.shape)).reshape(-1, 128)


def share_sum(arrived):
    return jnp.sum(arrived.astype(F32), axis=0).astype(BF)


def body(
    inputs, cotangent, text, text_mask, segments, time_index, time_table,
    w_qkv, w_out, w_query, w_keyval, w_cross, w_up, w_down, w_ada, b_ada,
):
    section = lax.axis_index("section")
    place = lax.axis_index("batch")
    core, chip = place % 2, place // 2
    first = section == 0

    weights = (w_qkv, w_out, w_query, w_keyval, w_cross, w_up, w_down)
    shard = section_swap(shard_call(place.astype(jnp.int32).reshape(1), weights))
    packed = pack_call(weights, shard)
    mine = copied(shard)

    frames = segments.reshape(MICRO, FRAMES, PATCHES)[:, :, 0]
    mask_row = text_mask.reshape(MICRO, TEXT)
    mask_column = text_mask.reshape(-1, 1)
    info = jnp.concatenate(
        [
            jnp.stack([section, core]),
            lax.dynamic_index_in_dim(frames, section, 0, keepdims=False),
        ]
    ).astype(jnp.int32)
    time_onehot = (time_index[:, None] == jnp.arange(STEPS)[None, :]).astype(BF)
    time_rows = mm(time_onehot, time_table)
    mod = mm(jax.nn.silu(time_rows).astype(BF), w_ada[0]) + b_ada
    mod_pairs = mod.reshape(MICRO, VIDS, 6 * D)
    mod_own = lax.dynamic_index_in_dim(mod_pairs, section, 0, keepdims=False)
    mod_other = section_swap(lax.dynamic_index_in_dim(mod_pairs, 1 - section, 0, keepdims=False))
    mod_other = gate(mod_other, packed)
    mods = (jnp.where(first, mod_own, mod_other), jnp.where(first, mod_other, mod_own))

    mine = gate(mine, packed, *mods)
    sources = (packed, mine, core_swap(mine))

    results = [None, None]
    (
        results[0], results[1], sent, d_text_one, d_mod_one,
        keep_feed, send_feed, keep_mixing, send_mixing, *kept,
    ) = first_call(info, inputs, cotangent, mods, text, mask_row, mask_column, sources)
    result_other = section_swap(jnp.where(first, results[1], results[0]))
    early = join_call(
        keep_feed, core_swap(send_feed), keep_mixing, core_swap(send_mixing), None
    )
    (
        d_first, given, d_text_low, d_mod_zero, keep_feed, send_feed, keep_mixing, send_mixing,
    ) = second_call(info, sent, mods[0], text, mask_column, d_text_one, sources, kept, early, result_other)
    early = across_chips(early)

    def by_clip(own, other):
        return jnp.concatenate([jnp.where(first, own, other), jnp.where(first, other, own)])

    d_mod_low = [member.astype(BF) for member in (d_mod_zero, d_mod_one)]
    packet = section_swap(
        jnp.concatenate([jnp.where(first, d_mod_low[1], d_mod_low[0]), d_text_low])
    )
    mod_rows = d_mod_low[0].shape[0]
    d_mod_clips = by_clip(
        jnp.where(first, d_mod_low[0], d_mod_low[1]), packet[:mod_rows]
    ).reshape(MICRO * VIDS, 6 * D)
    text_grad = by_clip(d_text_low, packet[mod_rows:]).astype(F32)
    digits = jnp.stack([time_index // 32, time_index % 32], axis=1).astype(BF)
    wide = jnp.concatenate(
        [d_mod_clips, time_rows.astype(BF), jnp.pad(digits, ((0, 0), (0, 126)))], axis=1
    ).reshape(MICRO * VIDS, 2, -1)
    wide_other = core_swap(lax.dynamic_index_in_dim(wide, 1 - core, 1, keepdims=False))
    wide_mine = lax.dynamic_index_in_dim(wide, core, 1, keepdims=False)
    extra = jnp.concatenate(
        [jnp.where(core == 0, wide_mine, wide_other), jnp.where(core == 0, wide_other, wide_mine)]
    ).reshape(EXTRA, 128)

    early = gate(early, given)
    late = across_chips(
        join_call(
            keep_feed, core_swap(send_feed), keep_mixing, core_swap(send_mixing), extra,
            early,
        )
    )
    early = share_sum(early)
    d_act_time = mm_nt(d_mod_clips, w_ada[0])
    unused, silu_back = jax.vjp(jax.nn.silu, time_rows)
    d_time_low = silu_back(d_act_time)[0].astype(BF)
    d_time_swapped = core_swap(d_time_low)
    d_time_own = jnp.where(
        core == 0,
        jnp.concatenate([d_time_low, d_time_swapped]),
        jnp.concatenate([d_time_swapped, d_time_low]),
    ).reshape(TIMES, 128)
    late = gate(late, d_time_own, early)
    last = share_sum(late[:, :SHARE])
    total = (
        jnp.concatenate([jnp.where(first, last, early), d_time_own]).astype(F32)
        + section_swap(jnp.concatenate([jnp.where(first, early, last), d_time_own])).astype(F32)
    ).astype(BF)
    full = jnp.broadcast_to(total[None], (32, SHARE + TIMES, 128))
    given_other = section_swap(gate(jnp.where(first, sent, given), full))
    full = across_chips(full)
    outputs = by_clip(jnp.where(first, results[0], results[1]), result_other)
    d_input = by_clip(
        jnp.where(first, d_first, sent.astype(F32)), given_other.astype(F32)
    )
    columns = late[:, SHARE:].reshape(4 * 64, -1)
    columns_other = core_swap(columns)
    every = jnp.concatenate(
        [
            jnp.where(core == 0, columns, columns_other),
            jnp.where(core == 0, columns_other, columns),
        ],
        axis=1,
    )
    every_mod = every[:, : 6 * D]
    every_rows = every[:, 6 * D : 7 * D].astype(F32)
    every_digits = every[:, 7 * D : 7 * D + 2].astype(jnp.int32)
    every_index = every_digits[:, 0] * 32 + every_digits[:, 1]
    g_bias = jnp.sum(every_mod.astype(F32), axis=0)
    g_ada = mm_tn(jax.nn.silu(every_rows).astype(BF), every_mod)
    every_time = full[:, SHARE:].reshape(4 * 64, D)
    full = gate(full, g_ada, g_bias, given_other)
    full_other = core_swap(full)
    table_grad = mm_tn(
        (every_index[:, None] == jnp.arange(STEPS)[None, :]).astype(BF), every_time
    )
    grads = unpack_call(info, full, full_other)
    g_qkv, g_out, g_cross, g_query, g_keyval, g_up, g_down = grads
    return (
        outputs[None], d_input[None], text_grad, table_grad, g_qkv, g_out, g_query, g_keyval,
        g_cross, g_up, g_down, g_ada[None], g_bias[None],
    )


def solution(mesh):
    return jax.shard_map(
        body,
        mesh=mesh,
        in_specs=(
            P("batch", None),
            P("batch", None),
            P("batch", None),
            P("batch"),
            P("batch"),
            P("batch"),
            P(),
            P("section", None, None),
            P("section", None, None),
            P("section", None, None),
            P("section", None, None),
            P("section", None, None),
            P("section", None, None),
            P("section", None, None),
            P("section", None, None),
            P("section", None),
        ),
        out_specs=(
            P("section", "batch", None),
            P("section", "batch", None),
            P("batch", None),
            P(),
            P("section", None, None),
            P("section", None, None),
            P("section", None, None),
            P("section", None, None),
            P("section", None, None),
            P("section", None, None),
            P("section", None, None),
            P("section", None, None),
            P("section", None),
        ),
        check_vma=False,
    )
```

```python
import functools
import jax
import jax.numpy as jnp
from jax import lax
from jax.experimental import pallas as pl
from jax.experimental.pallas import tpu as pltpu
from jax.sharding import PartitionSpec as P

D = 384
HEADS = 6
HEAD = 64
FF = 1536
PATCHES = 128
FRAMES = 4
VIDS = 2
TXT = 64
MICRO = 2
STEPS = 1000
ROWS = FRAMES * PATCHES
TEXT = VIDS * TXT
BLOCKS = 24
PACKED = BLOCKS * D
HALF = PACKED // 2
SHARE = PACKED // 32
EXTRA = 88
TIMES = 24
MODS = 6 * VIDS
PAIRS = HEADS // 2
SCORE_SCALE = 0.125
NEGATIVE = -1000000000.0
EPSILON = 1e-06
F32 = jnp.float32
BF = jnp.bfloat16
VMEM_LIMIT = 56 * 1024 * 1024


def mm(left, right):
    return lax.dot_general(left, right, (((1,), (0,)), ((), ())), preferred_element_type=F32)


def mm_nt(left, right):
    return lax.dot_general(left, right, (((1,), (1,)), ((), ())), preferred_element_type=F32)


def mm_tn(left, right):
    return lax.dot_general(left, right, (((0,), (0,)), ((), ())), preferred_element_type=F32)


def frame(index):
    return pl.ds(index * PATCHES, PATCHES)


def normed(tensor):
    centre = tensor - jnp.sum(tensor, axis=-1, keepdims=True) * (1.0 / D)
    inverse = lax.rsqrt(jnp.sum(centre * centre, axis=-1, keepdims=True) * (1.0 / D) + EPSILON)
    return centre * inverse, inverse


def norm_back(hat, inverse, d_hat):
    first = jnp.sum(d_hat, axis=-1, keepdims=True) * (1.0 / D)
    second = jnp.sum(d_hat * hat, axis=-1, keepdims=True) * (1.0 / D)
    return inverse * (d_hat - first - hat * second)


def gelu_parts(hidden):
    square = hidden * hidden
    inner = hidden * (0.7978845608028654 + 0.035677408136300125 * square)
    tanh = jnp.tanh(inner)
    half = 0.5 * (1.0 + tanh)
    slope = half + 0.5 * hidden * (1.0 - tanh * tanh) * (
        0.7978845608028654 + 0.10703222440890037 * square
    )
    return hidden * half, slope


def gelu(hidden):
    inner = hidden * (0.7978845608028654 + 0.035677408136300125 * (hidden * hidden))
    return hidden * (0.5 + 0.5 * jnp.tanh(inner))


def half_masks():
    lane = lax.broadcasted_iota(jnp.int32, (1, 128), 1)
    low = (lane < HEAD).astype(F32)
    return low.astype(BF), (1.0 - low).astype(BF)


def stacked(pair, masks):
    return jnp.concatenate([pair * masks[0], pair * masks[1]], axis=0)


def folded(both):
    lane = lax.broadcasted_iota(jnp.int32, (PATCHES, 128), 1)
    return jnp.where(lane < HEAD, both[:PATCHES], both[PATCHES:])


def pair_attend(query, keys, values, allowed, masks):
    logits = mm_nt(stacked(query, masks), keys) * SCORE_SCALE
    if allowed is not None:
        logits = jnp.where(allowed, logits, NEGATIVE)
    raised = jnp.exp(logits - jnp.max(logits, axis=-1, keepdims=True))
    probs = raised * (1.0 / jnp.sum(raised, axis=-1, keepdims=True))
    return folded(mm(probs.astype(BF), values)).astype(BF)


def pair_back(query, keys, values, d_mixed, allowed, masks):
    both_query = stacked(query, masks)
    both_d = stacked(d_mixed, masks)
    logits = mm_nt(keys, both_query) * SCORE_SCALE
    if allowed is not None:
        logits = jnp.where(allowed, logits, NEGATIVE)
    raised = jnp.exp(logits - jnp.max(logits, axis=0, keepdims=True))
    probs = raised * (1.0 / jnp.sum(raised, axis=0, keepdims=True))
    d_probs = mm_nt(values, both_d)
    weighed = probs * d_probs
    d_scores = (
        SCORE_SCALE * (weighed - probs * jnp.sum(weighed, axis=0, keepdims=True))
    ).astype(BF)
    d_query = folded(mm_tn(d_scores, keys))
    d_keys = mm(d_scores, both_query)
    d_values = mm(probs.astype(BF), both_d)
    return d_query, d_keys, d_values


def head_maps():
    feature = lax.broadcasted_iota(jnp.int32, (D, 128), 0) // HEAD
    lane = lax.broadcasted_iota(jnp.int32, (D, 128), 1)
    gather = (feature == lane).astype(F32).astype(BF)
    feature = lax.broadcasted_iota(jnp.int32, (128, D), 1) // HEAD
    lane = lax.broadcasted_iota(jnp.int32, (128, D), 0)
    return gather, (feature == lane).astype(F32).astype(BF)


def temporal_probs(query, keys, same, gather):
    products = jnp.concatenate([(query * key).astype(BF) for key in keys], axis=0)
    scores = mm(products, gather) * SCORE_SCALE
    logits = [
        jnp.where(same[other], scores[other * PATCHES : (other + 1) * PATCHES], NEGATIVE)
        for other in range(FRAMES)
    ]
    top = functools.reduce(jnp.maximum, logits)
    raised = [jnp.exp(member - top) for member in logits]
    scale = 1.0 / functools.reduce(jnp.add, raised)
    return [member * scale for member in raised]


def spread(members, expand):
    wide = mm(jnp.concatenate([member.astype(BF) for member in members], axis=0), expand)
    return [wide[other * PATCHES : (other + 1) * PATCHES] for other in range(FRAMES)]


def vmem_specs(count):
    return [pl.BlockSpec(memory_space=pltpu.VMEM)] * count


def any_specs(count):
    return [pl.BlockSpec(memory_space=pl.ANY)] * count


def params():
    return pltpu.CompilerParams(vmem_limit_bytes=VMEM_LIMIT)


def cost(micros):
    return pl.CostEstimate(flops=int(micros * 1e9), bytes_accessed=1 << 20, transcendentals=0)


def shape_of(dtype, *shape):
    return jax.ShapeDtypeStruct(shape, dtype)


class Weights:
    def __init__(self, info, layer, sources, held, arrived, pieces, shift):
        self.own, self.mine, self.other = sources
        self.done = False
        self.held, self.arrived, self.pieces = held, arrived, pieces
        is_own = info[0] == layer
        for slot, (start, count) in enumerate(pieces):
            half = start // HALF
            into = held.at[pl.ds(start, count), :]
            inside = start - half * HALF + shift

            def begin(source, at, into=into, slot=slot, count=count):
                pltpu.make_async_copy(
                    source.at[pl.ds(at, count), :], into, arrived.at[slot]
                ).start()

            pl.when(is_own)(functools.partial(begin, self.own, half * PACKED + inside))
            pl.when(jnp.logical_not(is_own) & (info[1] == half))(
                functools.partial(begin, self.mine, inside)
            )
            pl.when(jnp.logical_not(is_own) & (info[1] != half))(
                functools.partial(begin, self.other, inside)
            )

    def wait(self, slot):
        if self.done:
            return
        start, count = self.pieces[slot]
        rows = pl.ds(start, count)
        pltpu.make_async_copy(
            self.own.at[rows, :], self.held.at[rows, :], self.arrived.at[slot]
        ).wait()

    def columns(self, block, count):
        return jnp.concatenate(
            [self.held[(block + at) * D : (block + at + 1) * D, :] for at in range(count)], axis=1
        )


class Gradients:
    def __init__(self, info, kept, keep, send, left):
        self.info, self.kept, self.keep, self.send, self.left = info, kept, keep, send, left

    def put(self, block, fresh):
        for offset in range(fresh.shape[1] // 128):
            at = (block + offset) * D
            if not isinstance(at, int):
                at = pl.multiple_of(at, D)
            self.kept[pl.ds(at, D), :] = fresh[:, offset * 128 : (offset + 1) * 128].astype(BF)

    def copy(self, half, target):
        return pltpu.make_async_copy(
            self.kept.at[pl.ds(half * HALF, HALF), :], target, self.left.at[half]
        )

    def begin(self, half):
        pl.when(self.info[1] == half)(lambda: self.copy(half, self.keep).start())
        pl.when(self.info[1] != half)(lambda: self.copy(half, self.send).start())

    def finish(self):
        for half in range(2):
            self.copy(half, self.keep).wait()


MIXING_PIECES = ((0, 9 * D), (9 * D, 3 * D), (12 * D, 3 * D), (15 * D, 9 * D))
FEED_PIECES = ((0, 12 * D), (12 * D, 12 * D))
QKV, OUT, CROSS, QUERY, KEYVAL = 0, 9, 12, 15, 18


def weight_scratch(pieces):
    return [pltpu.VMEM((PACKED, 128), BF), pltpu.SemaphoreType.DMA((len(pieces),))]


def fill_packed(weights, held, after_part):
    w_qkv, w_out, w_query, w_keyval, w_cross, w_up, w_down = weights
    for half, members in enumerate(
        (((w_qkv, 9), (w_out, 3)), ((w_cross, 3), (w_query, 3), (w_keyval, 6)))
    ):
        at = half * PACKED
        for source, count in members:
            for block in range(count):
                held[at : at + D, :] = source[0, :, block * 128 : (block + 1) * 128]
                at += D
        after_part(half * PACKED)
    for block in range(12):
        at = HALF + block * D
        held[at : at + D, :] = w_up[0, :, block * 128 : (block + 1) * 128]
    after_part(HALF)
    for block in range(3):
        at = PACKED + HALF + block * FF
        held[at : at + FF, :] = w_down[0, :, block * 128 : (block + 1) * 128]
    after_part(PACKED + HALF)


UNIT = 96


def shard_kernel(place, w_qkv, w_out, w_query, w_keyval, w_cross, w_up, w_down, shard, arrived):
    halves = (
        [(w_qkv, 0, b) for b in range(9)] + [(w_out, 0, b) for b in range(3)]
        + [(w_up, 0, b) for b in range(12)],
        [(w_cross, 0, b) for b in range(3)] + [(w_query, 0, b) for b in range(3)]
        + [(w_keyval, 0, b) for b in range(6)]
        + [(w_down, D * (b % 4), b // 4) for b in range(12)],
    )
    core, chip = place[0] % 2, place[0] // 2

    def copy(source, row, column, slot):
        return pltpu.make_async_copy(
            source.at[0, pl.ds(pl.multiple_of(row, 16), UNIT), pl.ds(column * 128, 128)],
            shard.at[pl.ds(slot * UNIT, UNIT), :],
            arrived.at[slot],
        )

    for slot in range(SHARE // UNIT):
        unit = chip * (SHARE // UNIT) + slot
        block, inside = unit // (D // UNIT), (unit % (D // UNIT)) * UNIT
        for half in range(2):
            for at, (source, row, column) in enumerate(halves[half]):

                def begin(source=source, row=row, column=column, slot=slot, inside=inside):
                    copy(source, row + inside, column, slot).start()

                pl.when((core == half) & (block == at))(begin)
    for slot in range(SHARE // UNIT):
        copy(w_qkv, 0, 0, slot).wait()


def shard_call(place, weights):
    return pl.pallas_call(
        shard_kernel,
        out_shape=shape_of(BF, SHARE, 128),
        in_specs=[pl.BlockSpec(memory_space=pltpu.SMEM)] + any_specs(len(weights)),
        out_specs=vmem_specs(1)[0],
        scratch_shapes=[pltpu.SemaphoreType.DMA((SHARE // UNIT,))],
        compiler_params=params(),
        name="shard",
    )(place, *weights)


def pack_kernel(*refs):
    weights, (after, packed, held, left) = refs[:7], refs[7:]
    copies = []

    def leave(start):
        rows = pl.ds(start, HALF)
        made = pltpu.make_async_copy(held.at[rows, :], packed.at[rows, :], left.at[len(copies)])
        made.start()
        copies.append(made)

    fill_packed(weights, held, leave)
    for made in copies:
        made.wait()


def pack_call(weights, after):
    return pl.pallas_call(
        pack_kernel,
        out_shape=shape_of(BF, 2 * PACKED, 128),
        in_specs=vmem_specs(len(weights)) + any_specs(1),
        out_specs=any_specs(1)[0],
        scratch_shapes=[pltpu.VMEM((2 * PACKED, 128), BF), pltpu.SemaphoreType.DMA((4,))],
        compiler_params=params(),
        name="pack",
    )(*weights, after)


def video_group(info, mod):
    def group(index, which):
        return mod[pl.ds(info[2 + index], 1), which * D : (which + 1) * D]

    return group


def mix_forward(layer, weights, info, given, mod, text, mask_row, kept, normed_rows):
    (
        x_kept, qkv, mixed, attended, after_attend, cross_query, text_kv, cross_mixed, after_cross
    ) = kept[:9]
    clip = info[0]
    masks = half_masks()
    group = video_group(info, mod)
    for index in range(FRAMES):
        rows = frame(index)
        if layer == 0:
            x_kept[rows, :] = given[pl.ds(clip * ROWS + index * PATCHES, PATCHES), :]
        x = x_kept[rows, :]
        hat, unused = normed(x.astype(F32))
        normed_rows[rows, :] = (hat * (1.0 + group(index, 1)) + group(index, 0)).astype(BF)
    weights.wait(0)
    for part in range(3):
        qkv[:, part * D : (part + 1) * D] = mm(
            normed_rows[...], weights.columns(QKV + 3 * part, 3)
        ).astype(BF)

    def spatial(index, carry):
        rows = frame(index)
        for pair in range(PAIRS):
            mixed[rows, pair * 128 : (pair + 1) * 128] = pair_attend(
                qkv[rows, pair * 128 : (pair + 1) * 128],
                qkv[rows, D + pair * 128 : D + (pair + 1) * 128],
                qkv[rows, 2 * D + pair * 128 : 2 * D + (pair + 1) * 128],
                None,
                masks,
            )
        return carry

    def temporal(index, carry):
        gather, expand = head_maps()
        rows = frame(index)
        query = qkv[rows, :D].astype(F32)
        keys = [qkv[frame(at), D : 2 * D].astype(F32) for at in range(FRAMES)]
        same = [info[2 + at] == info[2 + index] for at in range(FRAMES)]
        wide = spread(temporal_probs(query, keys, same, gather), expand)
        total = sum(wide[at] * qkv[frame(at), 2 * D :].astype(F32) for at in range(FRAMES))
        mixed[rows, :] = total.astype(BF)
        return carry

    lax.fori_loop(0, FRAMES, spatial if layer == 0 else temporal, 0, unroll=True)
    weights.wait(1)
    projection = mm(mixed[...], weights.columns(OUT, 3))
    for index in range(FRAMES):
        rows = frame(index)
        piece = projection[index * PATCHES : (index + 1) * PATCHES]
        attended[rows, :] = piece.astype(BF)
        state = x_kept[rows, :].astype(F32) + group(index, 2) * piece
        after_attend[rows, :] = state
        normed_rows[rows, :] = normed(state)[0].astype(BF)
    weights.wait(2)
    weights.wait(3)
    cross_query[...] = mm(normed_rows[...], weights.columns(QUERY, 3)).astype(BF)
    text_rows = text[pl.ds(clip * TEXT, TEXT), :]
    text_kv[...] = mm(text_rows, weights.columns(KEYVAL, 6)).astype(BF)
    owner = lax.broadcasted_iota(jnp.int32, (1, TEXT), 1) // TXT
    real = mask_row[pl.ds(clip, 1), :] == 1

    def cross(index, carry):
        rows = frame(index)
        allowed = real & (owner == info[2 + index])
        for pair in range(PAIRS):
            cross_mixed[rows, pair * 128 : (pair + 1) * 128] = pair_attend(
                cross_query[rows, pair * 128 : (pair + 1) * 128],
                text_kv[:, pair * 128 : (pair + 1) * 128],
                text_kv[:, D + pair * 128 : D + (pair + 1) * 128],
                allowed,
                masks,
            )
        return carry

    lax.fori_loop(0, FRAMES, cross, 0, unroll=True)
    projection = mm(cross_mixed[...], weights.columns(CROSS, 3))
    for index in range(FRAMES):
        rows = frame(index)
        after_cross[rows, :] = (
            after_attend[rows, :] + projection[index * PATCHES : (index + 1) * PATCHES]
        )


def feed_forward(layer, weights, info, mod, kept, result, normed_rows, activated):
    after_cross, hidden, projected = kept[8:]
    held = weights.held
    group = video_group(info, mod)
    for index in range(FRAMES):
        rows = frame(index)
        hat, unused = normed(after_cross[rows, :])
        normed_rows[rows, :] = (hat * (1.0 + group(index, 4)) + group(index, 3)).astype(BF)
    weights.wait(0)
    for chunk in range(FF // 256):
        columns = slice(chunk * 256, (chunk + 1) * 256)
        raw = mm(normed_rows[...], weights.columns(2 * chunk, 2))
        hidden[:, columns] = raw.astype(BF)
        activated[:, columns] = gelu(raw).astype(BF)
    weights.wait(1)
    down = jnp.concatenate(
        [held[HALF + block * FF : HALF + (block + 1) * FF, :] for block in range(3)], axis=1
    )
    projection = mm(activated[...], down)
    for index in range(FRAMES):
        rows = frame(index)
        piece = projection[index * PATCHES : (index + 1) * PATCHES]
        projected[rows, :] = piece.astype(BF)
        result[rows, :] = (after_cross[rows, :] + group(index, 5) * piece).astype(BF)


def column_sum(tensor):
    return jnp.sum(tensor, axis=0, keepdims=True)


def add_by_video(totals, info, index, terms):
    for video in range(VIDS):
        for slot, term in enumerate(terms):
            if term is not None:
                totals[video][slot] = totals[video][slot] + jnp.where(
                    info[2 + index] == video, term, 0.0
                )


def no_totals():
    return [[jnp.zeros((1, D), F32) for unused in range(3)] for unused in range(VIDS)]


def put_totals(d_mod, totals, group):
    for member in range(VIDS):
        for slot in range(3):
            row = member * 6 + group + slot
            d_mod[row : row + 1, :] = totals[member][slot]


def feed_back(layer, weights, info, given, mod, kept, d_after_cross, grads, d_mod, work):
    after_cross, hidden, projected = kept[8:]
    normed_turned, d_turned, d_low, d_active, d_hidden = work
    held = weights.held
    clip = info[0]
    totals = no_totals()
    group = video_group(info, mod)

    def incoming(index):
        if layer == 1:
            return given[pl.ds(clip * ROWS + index * PATCHES, PATCHES), :].astype(F32)
        return given[frame(index), :].astype(F32)

    for index in range(FRAMES):
        rows = frame(index)
        grad = incoming(index)
        low = (grad * group(index, 5)).astype(BF)
        d_low[rows, :] = low
        d_turned[:, rows] = jnp.swapaxes(low, 0, 1)
        d_gate = column_sum(grad * projected[rows, :].astype(F32))
        add_by_video(totals, info, index, (None, None, d_gate))
        hat, unused = normed(after_cross[rows, :])
        normed_turned[:, rows] = jnp.swapaxes(
            (hat * (1.0 + group(index, 4)) + group(index, 3)).astype(BF), 0, 1
        )
    weights.wait(1)
    weights.wait(0)

    def feed(chunk, carry):
        columns = pl.ds(pl.multiple_of(chunk * 256, 256), 256)
        down = jnp.concatenate(
            [
                held[pl.ds(pl.multiple_of(HALF + block * FF + chunk * 256, 256), 256), :]
                for block in range(3)
            ],
            axis=1,
        )
        d_active[...] = mm_nt(d_low[...], down)
        for piece in range(8):
            rows = pl.ds(piece * 64, 64)
            active, slope = gelu_parts(hidden[rows, columns].astype(F32))
            d_hidden[rows, columns] = (d_active[rows, :] * slope).astype(BF)
            d_active[rows, :] = active
        grads.put(2 * chunk, mm(normed_turned[...], d_hidden[:, columns]))
        grads.put(12 + 2 * chunk, mm(d_turned[...], d_active[...].astype(BF)))
        return carry

    lax.fori_loop(0, FF // 256, feed, 0, unroll=True)
    grads.begin(0)
    grads.begin(1)
    d_normed = mm_nt(d_hidden[...], weights.columns(0, 12))
    for index in range(FRAMES):
        rows = frame(index)
        grad = incoming(index)
        piece = d_normed[index * PATCHES : (index + 1) * PATCHES]
        hat, inverse = normed(after_cross[rows, :])
        add_by_video(totals, info, index, (column_sum(piece), column_sum(piece * hat), None))
        d_after_cross[rows, :] = grad + norm_back(hat, inverse, piece * (1.0 + group(index, 4)))
    put_totals(d_mod, totals, 3)


def mix_back(
    layer, weights, info, mod, text, mask_column, d_after_cross, kept, d_input, d_sent, grads,
    d_text, d_mod, work,
):
    (
        x_kept, qkv, mixed, attended, after_attend, cross_query, text_kv, cross_mixed
    ) = kept[:8]
    low, turned, d_heads, d_query, d_text_kv, d_qkv, d_attend, d_keys, d_values = work
    clip = info[0]
    totals = no_totals()
    masks = half_masks()
    group = video_group(info, mod)

    for index in range(FRAMES):
        rows = frame(index)
        low[rows, :] = d_after_cross[rows, :].astype(BF)
        turned[:, rows] = jnp.swapaxes(cross_mixed[rows, :], 0, 1)
    grads.put(CROSS, mm(turned[...], low[...]))
    weights.wait(2)
    weights.wait(3)
    d_heads[...] = mm_nt(low[...], weights.columns(CROSS, 3)).astype(BF)
    owner = lax.broadcasted_iota(jnp.int32, (TEXT, 1), 0) // TXT
    real = mask_column[pl.ds(clip * TEXT, TEXT), :] == 1
    d_keys[...] = jnp.zeros_like(d_keys)
    d_values[...] = jnp.zeros_like(d_values)

    def cross(index, carry):
        rows = frame(index)
        allowed = real & (owner == info[2 + index])
        for pair in range(PAIRS):
            columns = slice(pair * 128, (pair + 1) * 128)
            late = slice(D + pair * 128, D + (pair + 1) * 128)
            one, two, three = pair_back(
                cross_query[rows, columns], text_kv[:, columns], text_kv[:, late],
                d_heads[rows, columns], allowed, masks,
            )
            d_query[rows, columns] = one.astype(BF)
            d_keys[: TEXT, columns] += two
            d_values[: TEXT, columns] += three
        return carry

    lax.fori_loop(0, FRAMES, cross, 0, unroll=True)
    d_text_kv[:, :D] = d_keys[: TEXT, :].astype(BF)
    d_text_kv[:, D:] = d_values[: TEXT, :].astype(BF)
    text_turned = jnp.swapaxes(text[pl.ds(clip * TEXT, TEXT), :], 0, 1)
    grads.put(KEYVAL, mm(text_turned, d_text_kv[...]))
    d_text[...] = mm_nt(d_text_kv[...], weights.columns(KEYVAL, 6))
    for index in range(FRAMES):
        rows = frame(index)
        hat, unused = normed(after_attend[rows, :])
        turned[:, rows] = jnp.swapaxes(hat.astype(BF), 0, 1)
    grads.put(QUERY, mm(turned[...], d_query[...]))
    grads.begin(1)
    d_normed = mm_nt(d_query[...], weights.columns(QUERY, 3))
    for index in range(FRAMES):
        rows = frame(index)
        piece = d_normed[index * PATCHES : (index + 1) * PATCHES]
        hat, inverse = normed(after_attend[rows, :])
        total = d_after_cross[rows, :] + norm_back(hat, inverse, piece)
        d_attend[rows, :] = total
        low[rows, :] = (total * group(index, 2)).astype(BF)
        add_by_video(
            totals, info, index, (None, None, column_sum(total * attended[rows, :].astype(F32)))
        )
        turned[:, rows] = jnp.swapaxes(mixed[rows, :], 0, 1)
    grads.put(OUT, mm(turned[...], low[...]))
    weights.wait(1)
    d_heads[...] = mm_nt(low[...], weights.columns(OUT, 3)).astype(BF)

    if layer == 0:
        def one_frame(index, carry):
            rows = frame(index)
            for pair in range(PAIRS):
                columns = slice(pair * 128, (pair + 1) * 128)
                second = slice(D + pair * 128, D + (pair + 1) * 128)
                third = slice(2 * D + pair * 128, 2 * D + (pair + 1) * 128)
                one, two, three = pair_back(
                    qkv[rows, columns], qkv[rows, second], qkv[rows, third],
                    d_heads[rows, columns], None, masks,
                )
                d_qkv[rows, columns] = one.astype(BF)
                d_qkv[rows, second] = two.astype(BF)
                d_qkv[rows, third] = three.astype(BF)
            return carry

        lax.fori_loop(0, FRAMES, one_frame, 0, unroll=True)

    else:
        gather, expand = head_maps()
        d_keys[...] = jnp.zeros_like(d_keys)
        d_values[...] = jnp.zeros_like(d_values)

        def one_frame(index, carry):
            rows = frame(index)
            query = qkv[rows, :D].astype(F32)
            d_mixed = d_heads[rows, :].astype(F32)
            keys = [qkv[frame(at), D : 2 * D].astype(F32) for at in range(FRAMES)]
            same = [info[2 + at] == info[2 + index] for at in range(FRAMES)]
            probs = temporal_probs(query, keys, same, gather)
            products = jnp.concatenate(
                [
                    (d_mixed * qkv[frame(at), 2 * D :].astype(F32)).astype(BF)
                    for at in range(FRAMES)
                ],
                axis=0,
            )
            d_probs = mm(products, gather)
            weighed = [
                probs[at] * d_probs[at * PATCHES : (at + 1) * PATCHES]
                for at in range(FRAMES)
            ]
            total = functools.reduce(jnp.add, weighed)
            d_scores = [
                SCORE_SCALE * (weighed[at] - probs[at] * total) for at in range(FRAMES)
            ]
            wide_probs = spread(probs, expand)
            wide_scores = spread(d_scores, expand)
            d_one = jnp.zeros((PATCHES, D), F32)
            for at in range(FRAMES):
                d_one = d_one + wide_scores[at] * keys[at]
                d_keys[frame(at), :] += wide_scores[at] * query
                d_values[frame(at), :] += wide_probs[at] * d_mixed
            d_qkv[rows, :D] = d_one.astype(BF)
            return carry

        lax.fori_loop(0, FRAMES, one_frame, 0, unroll=True)
        d_qkv[:, D : 2 * D] = d_keys[...].astype(BF)
        d_qkv[:, 2 * D :] = d_values[...].astype(BF)

    for index in range(FRAMES):
        rows = frame(index)
        hat, unused = normed(x_kept[rows, :].astype(F32))
        turned[:, rows] = jnp.swapaxes(
            (hat * (1.0 + group(index, 1)) + group(index, 0)).astype(BF), 0, 1
        )
    for part in range(3):
        grads.put(3 * part, mm(turned[...], d_qkv[:, part * D : (part + 1) * D]))
    grads.begin(0)
    weights.wait(0)
    d_normed = mm_nt(d_qkv[...], weights.columns(QKV, 9))
    for index in range(FRAMES):
        rows = frame(index)
        piece = d_normed[index * PATCHES : (index + 1) * PATCHES]
        hat, inverse = normed(x_kept[rows, :].astype(F32))
        add_by_video(totals, info, index, (column_sum(piece), column_sum(piece * hat), None))
        total = d_attend[rows, :] + norm_back(hat, inverse, piece * (1.0 + group(index, 1)))
        d_sent[rows, :] = total.astype(BF)
        if d_input is not None:
            d_input[rows, :] = total
    put_totals(d_mod, totals, 0)


KEPT = (
    (BF, ROWS, D), (BF, ROWS, 3 * D), (BF, ROWS, D), (BF, ROWS, D), (F32, ROWS, D), (BF, ROWS, D),
    (BF, TEXT, 2 * D), (BF, ROWS, D), (F32, ROWS, D), (BF, ROWS, FF), (BF, ROWS, D),
)
FEED_WORK = (
    (BF, D, ROWS), (BF, D, ROWS), (BF, ROWS, D), (F32, ROWS, 256), (BF, ROWS, FF)
)
MIX_WORK = (
    (BF, ROWS, D), (BF, D, ROWS), (BF, ROWS, D), (BF, ROWS, D), (BF, TEXT, 2 * D),
    (BF, ROWS, 3 * D), (F32, ROWS, D), (F32, ROWS, D), (F32, ROWS, D),
)


def scratch(shapes):
    return [pltpu.VMEM(tuple(shape[1:]), shape[0]) for shape in shapes]


def grad_scratch():
    return [pltpu.VMEM((PACKED, 128), BF), pltpu.SemaphoreType.DMA((2,))]


def both_weights(info, layer, sources, mixing_refs, feed_refs):
    return (
        Weights(info, layer, sources, *mixing_refs, MIXING_PIECES, 0),
        Weights(info, layer, sources, *feed_refs, FEED_PIECES, HALF),
    )


def first_kernel(
    info, inputs, cotangent, mod_zero, mod_one, text, mask_row, mask_column, own, mine, other, *rest
):
    rest = iter(rest)
    take = lambda count: [next(rest) for unused in range(count)]
    result_zero, result_one, sent, d_text, d_mod = take(5)
    keep_feed, send_feed, keep_mixing, send_mixing = take(4)
    left_kept = take(11)
    kept_zero, kept_one = take(11), take(10)
    feed_work, mix_work = take(5), take(9)
    normed_rows, activated, d_after_cross = take(3)
    sources = (own, mine, other)
    mixing_zero, feed_zero = both_weights(info, 0, sources, take(2), take(2))
    mixing_one, feed_one = both_weights(info, 1, sources, take(2), take(2))
    feed_grads = Gradients(info, *take(1), keep_feed, send_feed, *take(1))
    mixing_grads = Gradients(info, *take(1), keep_mixing, send_mixing, *take(1))
    leaving = take(1)[0]
    mix_forward(0, mixing_zero, info, inputs, mod_zero, text, mask_row, kept_zero, normed_rows)
    feed_forward(0, feed_zero, info, mod_zero, kept_zero, result_zero, normed_rows, activated)
    copies = [
        pltpu.make_async_copy(held, target, leaving.at[slot])
        for slot, (held, target) in enumerate(zip(kept_zero, left_kept))
    ]
    for copy in copies:
        copy.start()
    kept_one = [result_zero] + kept_one
    mix_forward(1, mixing_one, info, None, mod_one, text, mask_row, kept_one, normed_rows)
    feed_forward(1, feed_one, info, mod_one, kept_one, result_one, normed_rows, activated)
    feed_one.done = mixing_one.done = True
    feed_back(
        1, feed_one, info, cotangent, mod_one, kept_one, d_after_cross, feed_grads, d_mod,
        feed_work,
    )
    mix_back(
        1, mixing_one, info, mod_one, text, mask_column, d_after_cross, kept_one, None, sent,
        mixing_grads, d_text, d_mod, mix_work,
    )
    feed_grads.finish()
    mixing_grads.finish()
    for copy in copies:
        copy.wait()


def first_call(info, inputs, cotangent, mods, text, mask_row, mask_column, sources):
    return pl.pallas_call(
        first_kernel,
        out_shape=(
            shape_of(BF, ROWS, D), shape_of(BF, ROWS, D), shape_of(BF, ROWS, D),
            shape_of(F32, TEXT, D), shape_of(F32, MODS, D),
        )
        + (shape_of(BF, HALF, 128),) * 4
        + tuple(shape_of(*shape) for shape in KEPT),
        in_specs=[pl.BlockSpec(memory_space=pltpu.SMEM)] + vmem_specs(7) + any_specs(3),
        out_specs=tuple(vmem_specs(5) + any_specs(15)),
        scratch_shapes=scratch(KEPT) + scratch(KEPT[1:]) + scratch(FEED_WORK) + scratch(MIX_WORK)
        + scratch(((BF, ROWS, D), (BF, ROWS, FF), (F32, ROWS, D)))
        + weight_scratch(MIXING_PIECES) + weight_scratch(FEED_PIECES)
        + weight_scratch(MIXING_PIECES) + weight_scratch(FEED_PIECES)
        + grad_scratch() + grad_scratch() + [pltpu.SemaphoreType.DMA((11,))],
        compiler_params=params(),
        name="first",
    )(info, inputs, cotangent, *mods, text, mask_row, mask_column, *sources)


def second_kernel(info, given, mod, text, mask_column, d_text_one, own, mine, other, *rest):
    rest = iter(rest)
    take = lambda count: [next(rest) for unused in range(count)]
    held_kept = take(11)
    unused_after = take(2)
    d_input, d_sent, d_text_low, d_mod = take(4)
    keep_feed, send_feed, keep_mixing, send_mixing = take(4)
    kept = take(11)
    feed_work, mix_work = take(5), take(9)
    d_after_cross, d_text = take(2)
    arrived = take(1)[0]
    order = (8, 10, 9, 7, 5, 6, 4, 3, 2, 1, 0)
    copies = {
        slot: pltpu.make_async_copy(held_kept[slot], kept[slot], arrived.at[slot]) for slot in order
    }
    for slot in order[:2]:
        copies[slot].start()
    feed = Weights(info, 0, (own, mine, other), *take(2), FEED_PIECES, HALF)
    for slot in order[2:]:
        copies[slot].start()
    mixing = Weights(info, 0, (own, mine, other), *take(2), MIXING_PIECES, 0)
    feed_grads = Gradients(info, *take(1), keep_feed, send_feed, *take(1))
    mixing_grads = Gradients(info, *take(1), keep_mixing, send_mixing, *take(1))
    for slot in order[:3]:
        copies[slot].wait()
    feed_back(
        0, feed, info, given, mod, kept, d_after_cross, feed_grads, d_mod, feed_work
    )
    for slot in order[3:]:
        copies[slot].wait()
    mix_back(
        0, mixing, info, mod, text, mask_column, d_after_cross, kept, d_input, d_sent,
        mixing_grads, d_text, d_mod, mix_work,
    )
    d_text_low[...] = (d_text[...] + d_text_one[...]).astype(BF)
    feed_grads.finish()
    mixing_grads.finish()


def second_call(info, given, mod, text, mask_column, d_text_one, sources, kept, *after):
    return pl.pallas_call(
        second_kernel,
        out_shape=(
            shape_of(F32, ROWS, D), shape_of(BF, ROWS, D), shape_of(BF, TEXT, D),
            shape_of(F32, MODS, D),
        )
        + (shape_of(BF, HALF, 128),) * 4,
        in_specs=[pl.BlockSpec(memory_space=pltpu.SMEM)] + vmem_specs(5) + any_specs(16),
        out_specs=tuple(vmem_specs(4) + any_specs(4)),
        scratch_shapes=scratch(KEPT) + scratch(FEED_WORK) + scratch(MIX_WORK)
        + scratch(((F32, ROWS, D), (F32, TEXT, D))) + [pltpu.SemaphoreType.DMA((11,))]
        + weight_scratch(FEED_PIECES) + weight_scratch(MIXING_PIECES)
        + grad_scratch() + grad_scratch(),
        compiler_params=params(),
        name="second",
    )(info, given, mod, text, mask_column, d_text_one, *sources, *kept, *after)


def unpack_kernel(
    info, mine, other, qkv, out, cross, query, keyval, up, down, halves, arrived, left,
    t_qkv, t_out, t_cross, t_query, t_keyval, t_up, t_down,
):
    core = info[1]
    loads = []
    for part in (1, 0):
        shares = pl.ds(16 * part, 16)
        for side, (source, half) in enumerate(((mine, core), (other, 1 - core))):
            load = pltpu.make_async_copy(
                source.at[shares, pl.ds(0, SHARE), :], halves.at[half, shares],
                arrived.at[part, side],
            )
            load.start()
            loads.append(load)
    stores = []

    def leave(source, target):
        store = pltpu.make_async_copy(source, target.at[0], left.at[len(stores)])
        store.start()
        stores.append(store)

    def block_of(half, at):
        pieces = []
        while True:
            share, inside = divmod(at, SHARE)
            count = min(SHARE - inside, D - sum(piece.shape[0] for piece in pieces))
            pieces.append(halves[half, share, inside : inside + count, :])
            at += count
            if sum(piece.shape[0] for piece in pieces) == D:
                return jnp.concatenate(pieces, axis=0).astype(F32)

    for load in loads[:2]:
        load.wait()
    for block in range(12):
        t_up[:, block * 128 : (block + 1) * 128] = block_of(0, HALF + block * D)
    leave(t_up, up)
    for block in range(12):
        t_down[block * 128 : (block + 1) * 128, :] = jnp.swapaxes(
            block_of(1, HALF + block * D), 0, 1
        )
    leave(t_down, down)
    for load in loads[2:]:
        load.wait()
    for half, members in enumerate(
        (((t_qkv, qkv, 9), (t_out, out, 3)), ((t_cross, cross, 3), (t_query, query, 3), (t_keyval, keyval, 6)))
    ):
        at = 0
        for held, target, count in members:
            for block in range(count):
                held[:, block * 128 : (block + 1) * 128] = block_of(half, at)
                at += D
            leave(held, target)
    for store in stores:
        store.wait()


def unpack_call(info, mine, other):
    shapes = ((D, 3 * D), (D, D), (D, D), (D, D), (D, 2 * D), (D, FF), (FF, D))
    return pl.pallas_call(
        unpack_kernel,
        out_shape=tuple(shape_of(F32, 1, *shape) for shape in shapes),
        in_specs=[pl.BlockSpec(memory_space=pltpu.SMEM)] + any_specs(2),
        out_specs=tuple(any_specs(len(shapes))),
        scratch_shapes=[
            pltpu.VMEM((2, 32, SHARE, 128), BF),
            pltpu.SemaphoreType.DMA((2, 2)),
            pltpu.SemaphoreType.DMA((len(shapes),)),
        ]
        + [pltpu.VMEM(shape, F32) for shape in shapes],
        compiler_params=params(),
        name="unpack",
    )(info, mine, other)


CHUNK = HALF // 4


def join_kernel(has_extra, keep_feed, got_feed, keep_mixing, got_mixing, *rest):
    extra = rest[0] if has_extra else None
    joined, held, total, arrived, left = rest[-5:]
    height = SHARE + (EXTRA if has_extra else 0)
    loads = []
    for part, (keep, got) in enumerate(((keep_mixing, got_mixing), (keep_feed, got_feed))):
        for piece in range(4):
            rows = pl.ds(piece * CHUNK, CHUNK)
            slot = part * 4 + piece
            for side, source in enumerate((keep, got)):
                load = pltpu.make_async_copy(
                    source.at[rows, :], held.at[side, pl.ds(slot * CHUNK, CHUNK), :],
                    arrived.at[side, slot],
                )
                load.start()
                loads.append(load)
    stores = []
    shares = CHUNK // SHARE
    for slot in range(8):
        loads[2 * slot].wait()
        loads[2 * slot + 1].wait()
        for at in range(shares):
            share = slot * shares + at
            rows = slice(share * SHARE, (share + 1) * SHARE)
            total[share, :SHARE, :] = held[0, rows, :] + held[1, rows, :]
            if has_extra:
                total[share, SHARE:, :] = extra[...]
        store = pltpu.make_async_copy(
            total.at[pl.ds(slot * shares, shares)], joined.at[pl.ds(slot * shares, shares)],
            left.at[slot],
        )
        store.start()
        stores.append(store)
    for store in stores:
        store.wait()


def join_call(keep_feed, got_feed, keep_mixing, got_mixing, extra, *after):
    has_extra = extra is not None
    height = SHARE + (EXTRA if has_extra else 0)
    return pl.pallas_call(
        functools.partial(join_kernel, has_extra),
        out_shape=shape_of(BF, 32, height, 128),
        in_specs=any_specs(4) + vmem_specs(int(has_extra)) + any_specs(len(after)),
        out_specs=any_specs(1)[0],
        scratch_shapes=[
            pltpu.VMEM((2, PACKED, 128), BF),
            pltpu.VMEM((32, height, 128), BF),
            pltpu.SemaphoreType.DMA((2, 8)),
            pltpu.SemaphoreType.DMA((8,)),
        ],
        compiler_params=params(),
        name="join",
    )(keep_feed, got_feed, keep_mixing, got_mixing, *((extra,) if has_extra else ()), *after)


def gate_kernel(*refs):
    del refs


def gate(value, *after):
    return pl.pallas_call(
        gate_kernel,
        out_shape=shape_of(value.dtype, *value.shape),
        in_specs=any_specs(1 + len(after)),
        out_specs=any_specs(1)[0],
        input_output_aliases={0: 0},
        name="gate",
    )(value, *after)


def batch_groups():
    return [[2 * chip + core for chip in range(32)] for core in range(2)]


def core_swap(value):
    count = lax.axis_size("batch")
    return lax.ppermute(value, "batch", [(i, i ^ 1) for i in range(count)])


def section_swap(value):
    return lax.ppermute(value, "section", [(0, 1), (1, 0)])


def across_chips(value):
    return lax.all_to_all(value, "batch", 0, 0, axis_index_groups=batch_groups(), tiled=True)


def copied(shard):
    return across_chips(jnp.broadcast_to(shard[None], (32,) + shard.shape)).reshape(-1, 128)


def share_sum(arrived):
    return jnp.sum(arrived.astype(F32), axis=0).astype(BF)


def body(
    inputs, cotangent, text, text_mask, segments, time_index, time_table,
    w_qkv, w_out, w_query, w_keyval, w_cross, w_up, w_down, w_ada, b_ada,
):
    section = lax.axis_index("section")
    place = lax.axis_index("batch")
    core, chip = place % 2, place // 2
    first = section == 0

    weights = (w_qkv, w_out, w_query, w_keyval, w_cross, w_up, w_down)
    shard = section_swap(shard_call(place.astype(jnp.int32).reshape(1), weights))
    packed = pack_call(weights, shard)
    mine = copied(shard)

    frames = segments.reshape(MICRO, FRAMES, PATCHES)[:, :, 0]
    mask_row = text_mask.reshape(MICRO, TEXT)
    mask_column = text_mask.reshape(-1, 1)
    info = jnp.concatenate(
        [
            jnp.stack([section, core]),
            lax.dynamic_index_in_dim(frames, section, 0, keepdims=False),
        ]
    ).astype(jnp.int32)
    time_onehot = (time_index[:, None] == jnp.arange(STEPS)[None, :]).astype(BF)
    time_rows = mm(time_onehot, time_table)
    mod = mm(jax.nn.silu(time_rows).astype(BF), w_ada[0]) + b_ada
    mod_pairs = mod.reshape(MICRO, VIDS, 6 * D)
    mod_own = lax.dynamic_index_in_dim(mod_pairs, section, 0, keepdims=False)
    mod_other = section_swap(lax.dynamic_index_in_dim(mod_pairs, 1 - section, 0, keepdims=False))
    mod_other = gate(mod_other, packed)
    mods = (jnp.where(first, mod_own, mod_other), jnp.where(first, mod_other, mod_own))

    mine = gate(mine, packed, *mods)
    sources = (packed, mine, core_swap(mine))

    results = [None, None]
    (
        results[0], results[1], sent, d_text_one, d_mod_one,
        keep_feed, send_feed, keep_mixing, send_mixing, *kept,
    ) = first_call(info, inputs, cotangent, mods, text, mask_row, mask_column, sources)
    result_other = section_swap(jnp.where(first, results[1], results[0]))
    early = join_call(
        keep_feed, core_swap(send_feed), keep_mixing, core_swap(send_mixing), None
    )
    (
        d_first, given, d_text_low, d_mod_zero, keep_feed, send_feed, keep_mixing, send_mixing,
    ) = second_call(info, sent, mods[0], text, mask_column, d_text_one, sources, kept, early, result_other)
    early = across_chips(early)

    def by_clip(own, other):
        return jnp.concatenate([jnp.where(first, own, other), jnp.where(first, other, own)])

    d_mod_low = [member.astype(BF) for member in (d_mod_zero, d_mod_one)]
    packet = section_swap(
        jnp.concatenate([jnp.where(first, d_mod_low[1], d_mod_low[0]), d_text_low])
    )
    mod_rows = d_mod_low[0].shape[0]
    d_mod_clips = by_clip(
        jnp.where(first, d_mod_low[0], d_mod_low[1]), packet[:mod_rows]
    ).reshape(MICRO * VIDS, 6 * D)
    text_grad = by_clip(d_text_low, packet[mod_rows:]).astype(F32)
    digits = jnp.stack([time_index // 32, time_index % 32], axis=1).astype(BF)
    wide = jnp.concatenate(
        [d_mod_clips, time_rows.astype(BF), jnp.pad(digits, ((0, 0), (0, 126)))], axis=1
    ).reshape(MICRO * VIDS, 2, -1)
    wide_other = core_swap(lax.dynamic_index_in_dim(wide, 1 - core, 1, keepdims=False))
    wide_mine = lax.dynamic_index_in_dim(wide, core, 1, keepdims=False)
    extra = jnp.concatenate(
        [jnp.where(core == 0, wide_mine, wide_other), jnp.where(core == 0, wide_other, wide_mine)]
    ).reshape(EXTRA, 128)

    early = gate(early, given)
    late = across_chips(
        join_call(
            keep_feed, core_swap(send_feed), keep_mixing, core_swap(send_mixing), extra,
            early,
        )
    )
    early = share_sum(early)
    d_act_time = mm_nt(d_mod_clips, w_ada[0])
    unused, silu_back = jax.vjp(jax.nn.silu, time_rows)
    d_time_low = silu_back(d_act_time)[0].astype(BF)
    d_time_swapped = core_swap(d_time_low)
    d_time_own = jnp.where(
        core == 0,
        jnp.concatenate([d_time_low, d_time_swapped]),
        jnp.concatenate([d_time_swapped, d_time_low]),
    ).reshape(TIMES, 128)
    late = gate(late, d_time_own, early)
    last = share_sum(late[:, :SHARE])
    total = (
        jnp.concatenate([jnp.where(first, last, early), d_time_own]).astype(F32)
        + section_swap(jnp.concatenate([jnp.where(first, early, last), d_time_own])).astype(F32)
    ).astype(BF)
    full = jnp.broadcast_to(total[None], (32, SHARE + TIMES, 128))
    given_other = section_swap(gate(jnp.where(first, sent, given), full))
    full = across_chips(full)
    outputs = by_clip(jnp.where(first, results[0], results[1]), result_other)
    d_input = by_clip(
        jnp.where(first, d_first, sent.astype(F32)), given_other.astype(F32)
    )
    columns = late[:, SHARE:].reshape(4 * 64, -1)
    columns_other = core_swap(columns)
    every = jnp.concatenate(
        [
            jnp.where(core == 0, columns, columns_other),
            jnp.where(core == 0, columns_other, columns),
        ],
        axis=1,
    )
    every_mod = every[:, : 6 * D]
    every_rows = every[:, 6 * D : 7 * D].astype(F32)
    every_digits = every[:, 7 * D : 7 * D + 2].astype(jnp.int32)
    every_index = every_digits[:, 0] * 32 + every_digits[:, 1]
    g_bias = jnp.sum(every_mod.astype(F32), axis=0)
    g_ada = mm_tn(jax.nn.silu(every_rows).astype(BF), every_mod)
    every_time = full[:, SHARE:].reshape(4 * 64, D)
    full = gate(full, g_ada, g_bias, given_other, outputs)
    full_other = core_swap(full)
    table_grad = mm_tn(
        (every_index[:, None] == jnp.arange(STEPS)[None, :]).astype(BF), every_time
    )
    grads = unpack_call(info, full, full_other)
    g_qkv, g_out, g_cross, g_query, g_keyval, g_up, g_down = grads
    return (
        outputs[None], d_input[None], text_grad, table_grad, g_qkv, g_out, g_query, g_keyval,
        g_cross, g_up, g_down, g_ada[None], g_bias[None],
    )


def solution(mesh):
    return jax.shard_map(
        body,
        mesh=mesh,
        in_specs=(
            P("batch", None),
            P("batch", None),
            P("batch", None),
            P("batch"),
            P("batch"),
            P("batch"),
            P(),
            P("section", None, None),
            P("section", None, None),
            P("section", None, None),
            P("section", None, None),
            P("section", None, None),
            P("section", None, None),
            P("section", None, None),
            P("section", None, None),
            P("section", None),
        ),
        out_specs=(
            P("section", "batch", None),
            P("section", "batch", None),
            P("batch", None),
            P(),
            P("section", None, None),
            P("section", None, None),
            P("section", None, None),
            P("section", None, None),
            P("section", None, None),
            P("section", None, None),
            P("section", None, None),
            P("section", None, None),
            P("section", None),
        ),
        check_vma=False,
    )
```

```python
import functools
import jax
import jax.numpy as jnp
from jax import lax
from jax.experimental import pallas as pl
from jax.experimental.pallas import tpu as pltpu
from jax.sharding import PartitionSpec as P

D = 384
HEADS = 6
HEAD = 64
FF = 1536
PATCHES = 128
FRAMES = 4
VIDS = 2
TXT = 64
MICRO = 2
STEPS = 1000
ROWS = FRAMES * PATCHES
TEXT = VIDS * TXT
BLOCKS = 24
PACKED = BLOCKS * D
HALF = PACKED // 2
SHARE = PACKED // 32
EXTRA = 88
TIMES = 24
MODS = 6 * VIDS
PAIRS = HEADS // 2
SCORE_SCALE = 0.125
NEGATIVE = -1000000000.0
EPSILON = 1e-06
F32 = jnp.float32
BF = jnp.bfloat16
VMEM_LIMIT = 56 * 1024 * 1024


def mm(left, right):
    return lax.dot_general(left, right, (((1,), (0,)), ((), ())), preferred_element_type=F32)


def mm_nt(left, right):
    return lax.dot_general(left, right, (((1,), (1,)), ((), ())), preferred_element_type=F32)


def mm_tn(left, right):
    return lax.dot_general(left, right, (((0,), (0,)), ((), ())), preferred_element_type=F32)


def frame(index):
    return pl.ds(index * PATCHES, PATCHES)


def normed(tensor):
    centre = tensor - jnp.sum(tensor, axis=-1, keepdims=True) * (1.0 / D)
    inverse = lax.rsqrt(jnp.sum(centre * centre, axis=-1, keepdims=True) * (1.0 / D) + EPSILON)
    return centre * inverse, inverse


def norm_back(hat, inverse, d_hat):
    first = jnp.sum(d_hat, axis=-1, keepdims=True) * (1.0 / D)
    second = jnp.sum(d_hat * hat, axis=-1, keepdims=True) * (1.0 / D)
    return inverse * (d_hat - first - hat * second)


def gelu_parts(hidden):
    square = hidden * hidden
    inner = hidden * (0.7978845608028654 + 0.035677408136300125 * square)
    tanh = jnp.tanh(inner)
    half = 0.5 * (1.0 + tanh)
    slope = half + 0.5 * hidden * (1.0 - tanh * tanh) * (
        0.7978845608028654 + 0.10703222440890037 * square
    )
    return hidden * half, slope


def gelu(hidden):
    inner = hidden * (0.7978845608028654 + 0.035677408136300125 * (hidden * hidden))
    return hidden * (0.5 + 0.5 * jnp.tanh(inner))


def half_masks():
    lane = lax.broadcasted_iota(jnp.int32, (1, 128), 1)
    low = (lane < HEAD).astype(F32)
    return low.astype(BF), (1.0 - low).astype(BF)


def stacked(pair, masks):
    return jnp.concatenate([pair * masks[0], pair * masks[1]], axis=0)


def folded(both):
    lane = lax.broadcasted_iota(jnp.int32, (PATCHES, 128), 1)
    return jnp.where(lane < HEAD, both[:PATCHES], both[PATCHES:])


def pair_attend(query, keys, values, allowed, masks):
    logits = mm_nt(stacked(query, masks), keys) * SCORE_SCALE
    if allowed is not None:
        logits = jnp.where(allowed, logits, NEGATIVE)
    raised = jnp.exp(logits - jnp.max(logits, axis=-1, keepdims=True))
    probs = raised * (1.0 / jnp.sum(raised, axis=-1, keepdims=True))
    return folded(mm(probs.astype(BF), values)).astype(BF)


def pair_back(query, keys, values, d_mixed, allowed, masks):
    both_query = stacked(query, masks)
    both_d = stacked(d_mixed, masks)
    logits = mm_nt(keys, both_query) * SCORE_SCALE
    if allowed is not None:
        logits = jnp.where(allowed, logits, NEGATIVE)
    raised = jnp.exp(logits - jnp.max(logits, axis=0, keepdims=True))
    probs = raised * (1.0 / jnp.sum(raised, axis=0, keepdims=True))
    d_probs = mm_nt(values, both_d)
    weighed = probs * d_probs
    d_scores = (
        SCORE_SCALE * (weighed - probs * jnp.sum(weighed, axis=0, keepdims=True))
    ).astype(BF)
    d_query = folded(mm_tn(d_scores, keys))
    d_keys = mm(d_scores, both_query)
    d_values = mm(probs.astype(BF), both_d)
    return d_query, d_keys, d_values


def head_maps():
    feature = lax.broadcasted_iota(jnp.int32, (D, 128), 0) // HEAD
    lane = lax.broadcasted_iota(jnp.int32, (D, 128), 1)
    gather = (feature == lane).astype(F32).astype(BF)
    feature = lax.broadcasted_iota(jnp.int32, (128, D), 1) // HEAD
    lane = lax.broadcasted_iota(jnp.int32, (128, D), 0)
    return gather, (feature == lane).astype(F32).astype(BF)


def temporal_probs(query, keys, same, gather):
    products = jnp.concatenate([(query * key).astype(BF) for key in keys], axis=0)
    scores = mm(products, gather) * SCORE_SCALE
    logits = [
        jnp.where(same[other], scores[other * PATCHES : (other + 1) * PATCHES], NEGATIVE)
        for other in range(FRAMES)
    ]
    top = functools.reduce(jnp.maximum, logits)
    raised = [jnp.exp(member - top) for member in logits]
    scale = 1.0 / functools.reduce(jnp.add, raised)
    return [member * scale for member in raised]


def spread(members, expand):
    wide = mm(jnp.concatenate([member.astype(BF) for member in members], axis=0), expand)
    return [wide[other * PATCHES : (other + 1) * PATCHES] for other in range(FRAMES)]


def vmem_specs(count):
    return [pl.BlockSpec(memory_space=pltpu.VMEM)] * count


def any_specs(count):
    return [pl.BlockSpec(memory_space=pl.ANY)] * count


def params():
    return pltpu.CompilerParams(vmem_limit_bytes=VMEM_LIMIT)


def cost(micros):
    return pl.CostEstimate(flops=int(micros * 1e9), bytes_accessed=1 << 20, transcendentals=0)


def shape_of(dtype, *shape):
    return jax.ShapeDtypeStruct(shape, dtype)


class Weights:
    def __init__(self, info, layer, sources, held, arrived, pieces, shift):
        self.own, self.mine, self.other = sources
        self.done = False
        self.held, self.arrived, self.pieces = held, arrived, pieces
        is_own = info[0] == layer
        for slot, (start, count) in enumerate(pieces):
            half = start // HALF
            into = held.at[pl.ds(start, count), :]
            inside = start - half * HALF + shift

            def begin(source, at, into=into, slot=slot, count=count):
                pltpu.make_async_copy(
                    source.at[pl.ds(at, count), :], into, arrived.at[slot]
                ).start()

            pl.when(is_own)(functools.partial(begin, self.own, half * PACKED + inside))
            pl.when(jnp.logical_not(is_own) & (info[1] == half))(
                functools.partial(begin, self.mine, inside)
            )
            pl.when(jnp.logical_not(is_own) & (info[1] != half))(
                functools.partial(begin, self.other, inside)
            )

    def wait(self, slot):
        if self.done:
            return
        start, count = self.pieces[slot]
        rows = pl.ds(start, count)
        pltpu.make_async_copy(
            self.own.at[rows, :], self.held.at[rows, :], self.arrived.at[slot]
        ).wait()

    def columns(self, block, count):
        return jnp.concatenate(
            [self.held[(block + at) * D : (block + at + 1) * D, :] for at in range(count)], axis=1
        )


class Gradients:
    def __init__(self, info, kept, keep, send, left):
        self.info, self.kept, self.keep, self.send, self.left = info, kept, keep, send, left

    def put(self, block, fresh):
        for offset in range(fresh.shape[1] // 128):
            at = (block + offset) * D
            if not isinstance(at, int):
                at = pl.multiple_of(at, D)
            self.kept[pl.ds(at, D), :] = fresh[:, offset * 128 : (offset + 1) * 128].astype(BF)

    def copy(self, half, target):
        return pltpu.make_async_copy(
            self.kept.at[pl.ds(half * HALF, HALF), :], target, self.left.at[half]
        )

    def begin(self, half):
        pl.when(self.info[1] == half)(lambda: self.copy(half, self.keep).start())
        pl.when(self.info[1] != half)(lambda: self.copy(half, self.send).start())

    def finish(self):
        for half in range(2):
            self.copy(half, self.keep).wait()


MIXING_PIECES = ((0, 9 * D), (9 * D, 3 * D), (12 * D, 3 * D), (15 * D, 9 * D))
FEED_PIECES = ((0, 12 * D), (12 * D, 12 * D))
QKV, OUT, CROSS, QUERY, KEYVAL = 0, 9, 12, 15, 18


def weight_scratch(pieces):
    return [pltpu.VMEM((PACKED, 128), BF), pltpu.SemaphoreType.DMA((len(pieces),))]


def fill_packed(weights, held, after_part):
    w_qkv, w_out, w_query, w_keyval, w_cross, w_up, w_down = weights
    for half, members in enumerate(
        (((w_qkv, 9), (w_out, 3)), ((w_cross, 3), (w_query, 3), (w_keyval, 6)))
    ):
        at = half * PACKED
        for source, count in members:
            for block in range(count):
                held[at : at + D, :] = source[0, :, block * 128 : (block + 1) * 128]
                at += D
        after_part(half * PACKED)
    for block in range(12):
        at = HALF + block * D
        held[at : at + D, :] = w_up[0, :, block * 128 : (block + 1) * 128]
    after_part(HALF)
    for block in range(3):
        at = PACKED + HALF + block * FF
        held[at : at + FF, :] = w_down[0, :, block * 128 : (block + 1) * 128]
    after_part(PACKED + HALF)


UNIT = 96


def shard_kernel(place, w_qkv, w_out, w_query, w_keyval, w_cross, w_up, w_down, shard, arrived):
    halves = (
        [(w_qkv, 0, b) for b in range(9)] + [(w_out, 0, b) for b in range(3)]
        + [(w_up, 0, b) for b in range(12)],
        [(w_cross, 0, b) for b in range(3)] + [(w_query, 0, b) for b in range(3)]
        + [(w_keyval, 0, b) for b in range(6)]
        + [(w_down, D * (b % 4), b // 4) for b in range(12)],
    )
    core, chip = place[0] % 2, place[0] // 2

    def copy(source, row, column, slot):
        return pltpu.make_async_copy(
            source.at[0, pl.ds(pl.multiple_of(row, 16), UNIT), pl.ds(column * 128, 128)],
            shard.at[pl.ds(slot * UNIT, UNIT), :],
            arrived.at[slot],
        )

    for slot in range(SHARE // UNIT):
        unit = chip * (SHARE // UNIT) + slot
        block, inside = unit // (D // UNIT), (unit % (D // UNIT)) * UNIT
        for half in range(2):
            for at, (source, row, column) in enumerate(halves[half]):

                def begin(source=source, row=row, column=column, slot=slot, inside=inside):
                    copy(source, row + inside, column, slot).start()

                pl.when((core == half) & (block == at))(begin)
    for slot in range(SHARE // UNIT):
        copy(w_qkv, 0, 0, slot).wait()


def shard_call(place, weights):
    return pl.pallas_call(
        shard_kernel,
        out_shape=shape_of(BF, SHARE, 128),
        in_specs=[pl.BlockSpec(memory_space=pltpu.SMEM)] + any_specs(len(weights)),
        out_specs=vmem_specs(1)[0],
        scratch_shapes=[pltpu.SemaphoreType.DMA((SHARE // UNIT,))],
        compiler_params=params(),
        name="shard",
    )(place, *weights)


def pack_kernel(*refs):
    weights, (after, packed, held, left) = refs[:7], refs[7:]
    copies = []

    def leave(start):
        rows = pl.ds(start, HALF)
        made = pltpu.make_async_copy(held.at[rows, :], packed.at[rows, :], left.at[len(copies)])
        made.start()
        copies.append(made)

    fill_packed(weights, held, leave)
    for made in copies:
        made.wait()


def pack_call(weights, after):
    return pl.pallas_call(
        pack_kernel,
        out_shape=shape_of(BF, 2 * PACKED, 128),
        in_specs=vmem_specs(len(weights)) + any_specs(1),
        out_specs=any_specs(1)[0],
        scratch_shapes=[pltpu.VMEM((2 * PACKED, 128), BF), pltpu.SemaphoreType.DMA((4,))],
        compiler_params=params(),
        name="pack",
    )(*weights, after)


def video_group(info, mod):
    def group(index, which):
        return mod[pl.ds(info[2 + index], 1), which * D : (which + 1) * D]

    return group


def mix_forward(layer, weights, info, given, mod, text, mask_row, kept, normed_rows):
    (
        x_kept, qkv, mixed, attended, after_attend, cross_query, text_kv, cross_mixed, after_cross
    ) = kept[:9]
    clip = info[0]
    masks = half_masks()
    group = video_group(info, mod)
    for index in range(FRAMES):
        rows = frame(index)
        if layer == 0:
            x_kept[rows, :] = given[pl.ds(clip * ROWS + index * PATCHES, PATCHES), :]
        x = x_kept[rows, :]
        hat, unused = normed(x.astype(F32))
        normed_rows[rows, :] = (hat * (1.0 + group(index, 1)) + group(index, 0)).astype(BF)
    weights.wait(0)
    for part in range(3):
        qkv[:, part * D : (part + 1) * D] = mm(
            normed_rows[...], weights.columns(QKV + 3 * part, 3)
        ).astype(BF)

    def spatial(index, carry):
        rows = frame(index)
        for pair in range(PAIRS):
            mixed[rows, pair * 128 : (pair + 1) * 128] = pair_attend(
                qkv[rows, pair * 128 : (pair + 1) * 128],
                qkv[rows, D + pair * 128 : D + (pair + 1) * 128],
                qkv[rows, 2 * D + pair * 128 : 2 * D + (pair + 1) * 128],
                None,
                masks,
            )
        return carry

    def temporal(index, carry):
        gather, expand = head_maps()
        rows = frame(index)
        query = qkv[rows, :D].astype(F32)
        keys = [qkv[frame(at), D : 2 * D].astype(F32) for at in range(FRAMES)]
        same = [info[2 + at] == info[2 + index] for at in range(FRAMES)]
        wide = spread(temporal_probs(query, keys, same, gather), expand)
        total = sum(wide[at] * qkv[frame(at), 2 * D :].astype(F32) for at in range(FRAMES))
        mixed[rows, :] = total.astype(BF)
        return carry

    lax.fori_loop(0, FRAMES, spatial if layer == 0 else temporal, 0, unroll=True)
    weights.wait(1)
    projection = mm(mixed[...], weights.columns(OUT, 3))
    for index in range(FRAMES):
        rows = frame(index)
        piece = projection[index * PATCHES : (index + 1) * PATCHES]
        attended[rows, :] = piece.astype(BF)
        state = x_kept[rows, :].astype(F32) + group(index, 2) * piece
        after_attend[rows, :] = state
        normed_rows[rows, :] = normed(state)[0].astype(BF)
    weights.wait(2)
    weights.wait(3)
    cross_query[...] = mm(normed_rows[...], weights.columns(QUERY, 3)).astype(BF)
    text_rows = text[pl.ds(clip * TEXT, TEXT), :]
    text_kv[...] = mm(text_rows, weights.columns(KEYVAL, 6)).astype(BF)
    owner = lax.broadcasted_iota(jnp.int32, (1, TEXT), 1) // TXT
    real = mask_row[pl.ds(clip, 1), :] == 1

    def cross(index, carry):
        rows = frame(index)
        allowed = real & (owner == info[2 + index])
        for pair in range(PAIRS):
            cross_mixed[rows, pair * 128 : (pair + 1) * 128] = pair_attend(
                cross_query[rows, pair * 128 : (pair + 1) * 128],
                text_kv[:, pair * 128 : (pair + 1) * 128],
                text_kv[:, D + pair * 128 : D + (pair + 1) * 128],
                allowed,
                masks,
            )
        return carry

    lax.fori_loop(0, FRAMES, cross, 0, unroll=True)
    projection = mm(cross_mixed[...], weights.columns(CROSS, 3))
    for index in range(FRAMES):
        rows = frame(index)
        after_cross[rows, :] = (
            after_attend[rows, :] + projection[index * PATCHES : (index + 1) * PATCHES]
        )


def feed_forward(layer, weights, info, mod, kept, result, normed_rows, activated):
    after_cross, hidden, projected = kept[8:]
    held = weights.held
    group = video_group(info, mod)
    for index in range(FRAMES):
        rows = frame(index)
        hat, unused = normed(after_cross[rows, :])
        normed_rows[rows, :] = (hat * (1.0 + group(index, 4)) + group(index, 3)).astype(BF)
    weights.wait(0)
    for chunk in range(FF // 256):
        columns = slice(chunk * 256, (chunk + 1) * 256)
        raw = mm(normed_rows[...], weights.columns(2 * chunk, 2))
        hidden[:, columns] = raw.astype(BF)
        activated[:, columns] = gelu(raw).astype(BF)
    weights.wait(1)
    down = jnp.concatenate(
        [held[HALF + block * FF : HALF + (block + 1) * FF, :] for block in range(3)], axis=1
    )
    projection = mm(activated[...], down)
    for index in range(FRAMES):
        rows = frame(index)
        piece = projection[index * PATCHES : (index + 1) * PATCHES]
        projected[rows, :] = piece.astype(BF)
        result[rows, :] = (after_cross[rows, :] + group(index, 5) * piece).astype(BF)


def column_sum(tensor):
    return jnp.sum(tensor, axis=0, keepdims=True)


def add_by_video(totals, info, index, terms):
    for video in range(VIDS):
        for slot, term in enumerate(terms):
            if term is not None:
                totals[video][slot] = totals[video][slot] + jnp.where(
                    info[2 + index] == video, term, 0.0
                )


def no_totals():
    return [[jnp.zeros((1, D), F32) for unused in range(3)] for unused in range(VIDS)]


def put_totals(d_mod, totals, group):
    for member in range(VIDS):
        for slot in range(3):
            row = member * 6 + group + slot
            d_mod[row : row + 1, :] = totals[member][slot]


def feed_back(layer, weights, info, given, mod, kept, d_after_cross, grads, d_mod, work):
    after_cross, hidden, projected = kept[8:]
    normed_turned, d_turned, d_low, d_active, d_hidden = work
    held = weights.held
    clip = info[0]
    totals = no_totals()
    group = video_group(info, mod)

    def incoming(index):
        if layer == 1:
            return given[pl.ds(clip * ROWS + index * PATCHES, PATCHES), :].astype(F32)
        return given[frame(index), :].astype(F32)

    for index in range(FRAMES):
        rows = frame(index)
        grad = incoming(index)
        low = (grad * group(index, 5)).astype(BF)
        d_low[rows, :] = low
        d_turned[:, rows] = jnp.swapaxes(low, 0, 1)
        d_gate = column_sum(grad * projected[rows, :].astype(F32))
        add_by_video(totals, info, index, (None, None, d_gate))
        hat, unused = normed(after_cross[rows, :])
        normed_turned[:, rows] = jnp.swapaxes(
            (hat * (1.0 + group(index, 4)) + group(index, 3)).astype(BF), 0, 1
        )
    weights.wait(1)
    weights.wait(0)

    def feed(chunk, carry):
        columns = pl.ds(pl.multiple_of(chunk * 256, 256), 256)
        down = jnp.concatenate(
            [
                held[pl.ds(pl.multiple_of(HALF + block * FF + chunk * 256, 256), 256), :]
                for block in range(3)
            ],
            axis=1,
        )
        d_active[...] = mm_nt(d_low[...], down)
        for piece in range(8):
            rows = pl.ds(piece * 64, 64)
            active, slope = gelu_parts(hidden[rows, columns].astype(F32))
            d_hidden[rows, columns] = (d_active[rows, :] * slope).astype(BF)
            d_active[rows, :] = active
        grads.put(2 * chunk, mm(normed_turned[...], d_hidden[:, columns]))
        grads.put(12 + 2 * chunk, mm(d_turned[...], d_active[...].astype(BF)))
        return carry

    lax.fori_loop(0, FF // 256, feed, 0, unroll=True)
    grads.begin(0)
    grads.begin(1)
    d_normed = mm_nt(d_hidden[...], weights.columns(0, 12))
    for index in range(FRAMES):
        rows = frame(index)
        grad = incoming(index)
        piece = d_normed[index * PATCHES : (index + 1) * PATCHES]
        hat, inverse = normed(after_cross[rows, :])
        add_by_video(totals, info, index, (column_sum(piece), column_sum(piece * hat), None))
        d_after_cross[rows, :] = grad + norm_back(hat, inverse, piece * (1.0 + group(index, 4)))
    put_totals(d_mod, totals, 3)


def mix_back(
    layer, weights, info, mod, text, mask_column, d_after_cross, kept, d_input, d_sent, grads,
    d_text, d_mod, work,
):
    (
        x_kept, qkv, mixed, attended, after_attend, cross_query, text_kv, cross_mixed
    ) = kept[:8]
    low, turned, d_heads, d_query, d_text_kv, d_qkv, d_attend, d_keys, d_values = work
    clip = info[0]
    totals = no_totals()
    masks = half_masks()
    group = video_group(info, mod)

    for index in range(FRAMES):
        rows = frame(index)
        low[rows, :] = d_after_cross[rows, :].astype(BF)
        turned[:, rows] = jnp.swapaxes(cross_mixed[rows, :], 0, 1)
    grads.put(CROSS, mm(turned[...], low[...]))
    weights.wait(2)
    weights.wait(3)
    d_heads[...] = mm_nt(low[...], weights.columns(CROSS, 3)).astype(BF)
    owner = lax.broadcasted_iota(jnp.int32, (TEXT, 1), 0) // TXT
    real = mask_column[pl.ds(clip * TEXT, TEXT), :] == 1
    d_keys[...] = jnp.zeros_like(d_keys)
    d_values[...] = jnp.zeros_like(d_values)

    def cross(index, carry):
        rows = frame(index)
        allowed = real & (owner == info[2 + index])
        for pair in range(PAIRS):
            columns = slice(pair * 128, (pair + 1) * 128)
            late = slice(D + pair * 128, D + (pair + 1) * 128)
            one, two, three = pair_back(
                cross_query[rows, columns], text_kv[:, columns], text_kv[:, late],
                d_heads[rows, columns], allowed, masks,
            )
            d_query[rows, columns] = one.astype(BF)
            d_keys[: TEXT, columns] += two
            d_values[: TEXT, columns] += three
        return carry

    lax.fori_loop(0, FRAMES, cross, 0, unroll=True)
    d_text_kv[:, :D] = d_keys[: TEXT, :].astype(BF)
    d_text_kv[:, D:] = d_values[: TEXT, :].astype(BF)
    text_turned = jnp.swapaxes(text[pl.ds(clip * TEXT, TEXT), :], 0, 1)
    grads.put(KEYVAL, mm(text_turned, d_text_kv[...]))
    d_text[...] = mm_nt(d_text_kv[...], weights.columns(KEYVAL, 6))
    for index in range(FRAMES):
        rows = frame(index)
        hat, unused = normed(after_attend[rows, :])
        turned[:, rows] = jnp.swapaxes(hat.astype(BF), 0, 1)
    grads.put(QUERY, mm(turned[...], d_query[...]))
    grads.begin(1)
    d_normed = mm_nt(d_query[...], weights.columns(QUERY, 3))
    for index in range(FRAMES):
        rows = frame(index)
        piece = d_normed[index * PATCHES : (index + 1) * PATCHES]
        hat, inverse = normed(after_attend[rows, :])
        total = d_after_cross[rows, :] + norm_back(hat, inverse, piece)
        d_attend[rows, :] = total
        low[rows, :] = (total * group(index, 2)).astype(BF)
        add_by_video(
            totals, info, index, (None, None, column_sum(total * attended[rows, :].astype(F32)))
        )
        turned[:, rows] = jnp.swapaxes(mixed[rows, :], 0, 1)
    grads.put(OUT, mm(turned[...], low[...]))
    weights.wait(1)
    d_heads[...] = mm_nt(low[...], weights.columns(OUT, 3)).astype(BF)

    if layer == 0:
        def one_frame(index, carry):
            rows = frame(index)
            for pair in range(PAIRS):
                columns = slice(pair * 128, (pair + 1) * 128)
                second = slice(D + pair * 128, D + (pair + 1) * 128)
                third = slice(2 * D + pair * 128, 2 * D + (pair + 1) * 128)
                one, two, three = pair_back(
                    qkv[rows, columns], qkv[rows, second], qkv[rows, third],
                    d_heads[rows, columns], None, masks,
                )
                d_qkv[rows, columns] = one.astype(BF)
                d_qkv[rows, second] = two.astype(BF)
                d_qkv[rows, third] = three.astype(BF)
            return carry

        lax.fori_loop(0, FRAMES, one_frame, 0, unroll=True)

    else:
        gather, expand = head_maps()
        d_keys[...] = jnp.zeros_like(d_keys)
        d_values[...] = jnp.zeros_like(d_values)

        def one_frame(index, carry):
            rows = frame(index)
            query = qkv[rows, :D].astype(F32)
            d_mixed = d_heads[rows, :].astype(F32)
            keys = [qkv[frame(at), D : 2 * D].astype(F32) for at in range(FRAMES)]
            same = [info[2 + at] == info[2 + index] for at in range(FRAMES)]
            probs = temporal_probs(query, keys, same, gather)
            products = jnp.concatenate(
                [
                    (d_mixed * qkv[frame(at), 2 * D :].astype(F32)).astype(BF)
                    for at in range(FRAMES)
                ],
                axis=0,
            )
            d_probs = mm(products, gather)
            weighed = [
                probs[at] * d_probs[at * PATCHES : (at + 1) * PATCHES]
                for at in range(FRAMES)
            ]
            total = functools.reduce(jnp.add, weighed)
            d_scores = [
                SCORE_SCALE * (weighed[at] - probs[at] * total) for at in range(FRAMES)
            ]
            wide_probs = spread(probs, expand)
            wide_scores = spread(d_scores, expand)
            d_one = jnp.zeros((PATCHES, D), F32)
            for at in range(FRAMES):
                d_one = d_one + wide_scores[at] * keys[at]
                d_keys[frame(at), :] += wide_scores[at] * query
                d_values[frame(at), :] += wide_probs[at] * d_mixed
            d_qkv[rows, :D] = d_one.astype(BF)
            return carry

        lax.fori_loop(0, FRAMES, one_frame, 0, unroll=True)
        d_qkv[:, D : 2 * D] = d_keys[...].astype(BF)
        d_qkv[:, 2 * D :] = d_values[...].astype(BF)

    for index in range(FRAMES):
        rows = frame(index)
        hat, unused = normed(x_kept[rows, :].astype(F32))
        turned[:, rows] = jnp.swapaxes(
            (hat * (1.0 + group(index, 1)) + group(index, 0)).astype(BF), 0, 1
        )
    for part in range(3):
        grads.put(3 * part, mm(turned[...], d_qkv[:, part * D : (part + 1) * D]))
    grads.begin(0)
    weights.wait(0)
    d_normed = mm_nt(d_qkv[...], weights.columns(QKV, 9))
    for index in range(FRAMES):
        rows = frame(index)
        piece = d_normed[index * PATCHES : (index + 1) * PATCHES]
        hat, inverse = normed(x_kept[rows, :].astype(F32))
        add_by_video(totals, info, index, (column_sum(piece), column_sum(piece * hat), None))
        total = d_attend[rows, :] + norm_back(hat, inverse, piece * (1.0 + group(index, 1)))
        d_sent[rows, :] = total.astype(BF)
        if d_input is not None:
            d_input[rows, :] = total
    put_totals(d_mod, totals, 0)


KEPT = (
    (BF, ROWS, D), (BF, ROWS, 3 * D), (BF, ROWS, D), (BF, ROWS, D), (F32, ROWS, D), (BF, ROWS, D),
    (BF, TEXT, 2 * D), (BF, ROWS, D), (F32, ROWS, D), (BF, ROWS, FF), (BF, ROWS, D),
)
FEED_WORK = (
    (BF, D, ROWS), (BF, D, ROWS), (BF, ROWS, D), (F32, ROWS, 256), (BF, ROWS, FF)
)
MIX_WORK = (
    (BF, ROWS, D), (BF, D, ROWS), (BF, ROWS, D), (BF, ROWS, D), (BF, TEXT, 2 * D),
    (BF, ROWS, 3 * D), (F32, ROWS, D), (F32, ROWS, D), (F32, ROWS, D),
)


def scratch(shapes):
    return [pltpu.VMEM(tuple(shape[1:]), shape[0]) for shape in shapes]


def grad_scratch():
    return [pltpu.VMEM((PACKED, 128), BF), pltpu.SemaphoreType.DMA((2,))]


def both_weights(info, layer, sources, mixing_refs, feed_refs):
    return (
        Weights(info, layer, sources, *mixing_refs, MIXING_PIECES, 0),
        Weights(info, layer, sources, *feed_refs, FEED_PIECES, HALF),
    )


def first_kernel(
    info, inputs, cotangent, mod_zero, mod_one, text, mask_row, mask_column, own, mine, other, *rest
):
    rest = iter(rest)
    take = lambda count: [next(rest) for unused in range(count)]
    result_zero, result_one, sent, d_text, d_mod = take(5)
    keep_feed, send_feed, keep_mixing, send_mixing = take(4)
    left_kept = take(11)
    kept_zero, kept_one = take(11), take(10)
    feed_work, mix_work = take(5), take(9)
    normed_rows, activated, d_after_cross = take(3)
    sources = (own, mine, other)
    mixing_zero, feed_zero = both_weights(info, 0, sources, take(2), take(2))
    mixing_one, feed_one = both_weights(info, 1, sources, take(2), take(2))
    feed_grads = Gradients(info, *take(1), keep_feed, send_feed, *take(1))
    mixing_grads = Gradients(info, *take(1), keep_mixing, send_mixing, *take(1))
    leaving = take(1)[0]
    mix_forward(0, mixing_zero, info, inputs, mod_zero, text, mask_row, kept_zero, normed_rows)
    feed_forward(0, feed_zero, info, mod_zero, kept_zero, result_zero, normed_rows, activated)
    copies = [
        pltpu.make_async_copy(held, target, leaving.at[slot])
        for slot, (held, target) in enumerate(zip(kept_zero, left_kept))
    ]
    for copy in copies:
        copy.start()
    kept_one = [result_zero] + kept_one
    mix_forward(1, mixing_one, info, None, mod_one, text, mask_row, kept_one, normed_rows)
    feed_forward(1, feed_one, info, mod_one, kept_one, result_one, normed_rows, activated)
    feed_one.done = mixing_one.done = True
    feed_back(
        1, feed_one, info, cotangent, mod_one, kept_one, d_after_cross, feed_grads, d_mod,
        feed_work,
    )
    mix_back(
        1, mixing_one, info, mod_one, text, mask_column, d_after_cross, kept_one, None, sent,
        mixing_grads, d_text, d_mod, mix_work,
    )
    feed_grads.finish()
    mixing_grads.finish()
    for copy in copies:
        copy.wait()


def first_call(info, inputs, cotangent, mods, text, mask_row, mask_column, sources):
    return pl.pallas_call(
        first_kernel,
        out_shape=(
            shape_of(BF, ROWS, D), shape_of(BF, ROWS, D), shape_of(BF, ROWS, D),
            shape_of(F32, TEXT, D), shape_of(F32, MODS, D),
        )
        + (shape_of(BF, HALF, 128),) * 4
        + tuple(shape_of(*shape) for shape in KEPT),
        in_specs=[pl.BlockSpec(memory_space=pltpu.SMEM)] + vmem_specs(7) + any_specs(3),
        out_specs=tuple(vmem_specs(5) + any_specs(15)),
        scratch_shapes=scratch(KEPT) + scratch(KEPT[1:]) + scratch(FEED_WORK) + scratch(MIX_WORK)
        + scratch(((BF, ROWS, D), (BF, ROWS, FF), (F32, ROWS, D)))
        + weight_scratch(MIXING_PIECES) + weight_scratch(FEED_PIECES)
        + weight_scratch(MIXING_PIECES) + weight_scratch(FEED_PIECES)
        + grad_scratch() + grad_scratch() + [pltpu.SemaphoreType.DMA((11,))],
        compiler_params=params(),
        name="first",
    )(info, inputs, cotangent, *mods, text, mask_row, mask_column, *sources)


def second_kernel(info, given, mod, text, mask_column, d_text_one, own, mine, other, *rest):
    rest = iter(rest)
    take = lambda count: [next(rest) for unused in range(count)]
    held_kept = take(11)
    unused_after = take(2)
    d_input, d_sent, d_text_low, d_mod = take(4)
    keep_feed, send_feed, keep_mixing, send_mixing = take(4)
    kept = take(11)
    feed_work, mix_work = take(5), take(9)
    d_after_cross, d_text = take(2)
    arrived = take(1)[0]
    order = (8, 10, 9, 7, 5, 6, 4, 3, 2, 1, 0)
    copies = {
        slot: pltpu.make_async_copy(held_kept[slot], kept[slot], arrived.at[slot]) for slot in order
    }
    for slot in order[:2]:
        copies[slot].start()
    feed = Weights(info, 0, (own, mine, other), *take(2), FEED_PIECES, HALF)
    for slot in order[2:]:
        copies[slot].start()
    mixing = Weights(info, 0, (own, mine, other), *take(2), MIXING_PIECES, 0)
    feed_grads = Gradients(info, *take(1), keep_feed, send_feed, *take(1))
    mixing_grads = Gradients(info, *take(1), keep_mixing, send_mixing, *take(1))
    for slot in order[:3]:
        copies[slot].wait()
    feed_back(
        0, feed, info, given, mod, kept, d_after_cross, feed_grads, d_mod, feed_work
    )
    for slot in order[3:]:
        copies[slot].wait()
    mix_back(
        0, mixing, info, mod, text, mask_column, d_after_cross, kept, d_input, d_sent,
        mixing_grads, d_text, d_mod, mix_work,
    )
    d_text_low[...] = (d_text[...] + d_text_one[...]).astype(BF)
    feed_grads.finish()
    mixing_grads.finish()


def second_call(info, given, mod, text, mask_column, d_text_one, sources, kept, *after):
    return pl.pallas_call(
        second_kernel,
        out_shape=(
            shape_of(F32, ROWS, D), shape_of(BF, ROWS, D), shape_of(BF, TEXT, D),
            shape_of(F32, MODS, D),
        )
        + (shape_of(BF, HALF, 128),) * 4,
        in_specs=[pl.BlockSpec(memory_space=pltpu.SMEM)] + vmem_specs(5) + any_specs(16),
        out_specs=tuple(vmem_specs(4) + any_specs(4)),
        scratch_shapes=scratch(KEPT) + scratch(FEED_WORK) + scratch(MIX_WORK)
        + scratch(((F32, ROWS, D), (F32, TEXT, D))) + [pltpu.SemaphoreType.DMA((11,))]
        + weight_scratch(FEED_PIECES) + weight_scratch(MIXING_PIECES)
        + grad_scratch() + grad_scratch(),
        compiler_params=params(),
        name="second",
    )(info, given, mod, text, mask_column, d_text_one, *sources, *kept, *after)


def unpack_kernel(
    info, mine, other, qkv, out, cross, query, keyval, up, down, halves, arrived, left,
    t_qkv, t_out, t_cross, t_query, t_keyval, t_up, t_down,
):
    core = info[1]
    loads = []
    for part in (1, 0):
        shares = pl.ds(16 * part, 16)
        for side, (source, half) in enumerate(((mine, core), (other, 1 - core))):
            load = pltpu.make_async_copy(
                source.at[shares, pl.ds(0, SHARE), :], halves.at[half, shares],
                arrived.at[part, side],
            )
            load.start()
            loads.append(load)
    stores = []

    def leave(source, target):
        store = pltpu.make_async_copy(source, target.at[0], left.at[len(stores)])
        store.start()
        stores.append(store)

    def block_of(half, at):
        pieces = []
        while True:
            share, inside = divmod(at, SHARE)
            count = min(SHARE - inside, D - sum(piece.shape[0] for piece in pieces))
            pieces.append(halves[half, share, inside : inside + count, :])
            at += count
            if sum(piece.shape[0] for piece in pieces) == D:
                return jnp.concatenate(pieces, axis=0).astype(F32)

    for load in loads[:2]:
        load.wait()
    for block in range(12):
        t_up[:, block * 128 : (block + 1) * 128] = block_of(0, HALF + block * D)
    leave(t_up, up)
    for block in range(12):
        t_down[block * 128 : (block + 1) * 128, :] = jnp.swapaxes(
            block_of(1, HALF + block * D), 0, 1
        )
    leave(t_down, down)
    for load in loads[2:]:
        load.wait()
    for half, members in enumerate(
        (((t_qkv, qkv, 9), (t_out, out, 3)), ((t_cross, cross, 3), (t_query, query, 3), (t_keyval, keyval, 6)))
    ):
        at = 0
        for held, target, count in members:
            for block in range(count):
                held[:, block * 128 : (block + 1) * 128] = block_of(half, at)
                at += D
            leave(held, target)
    for store in stores:
        store.wait()


def unpack_call(info, mine, other):
    shapes = ((D, 3 * D), (D, D), (D, D), (D, D), (D, 2 * D), (D, FF), (FF, D))
    return pl.pallas_call(
        unpack_kernel,
        out_shape=tuple(shape_of(F32, 1, *shape) for shape in shapes),
        in_specs=[pl.BlockSpec(memory_space=pltpu.SMEM)] + any_specs(2),
        out_specs=tuple(any_specs(len(shapes))),
        scratch_shapes=[
            pltpu.VMEM((2, 32, SHARE, 128), BF),
            pltpu.SemaphoreType.DMA((2, 2)),
            pltpu.SemaphoreType.DMA((len(shapes),)),
        ]
        + [pltpu.VMEM(shape, F32) for shape in shapes],
        compiler_params=params(),
        name="unpack",
    )(info, mine, other)


CHUNK = HALF // 4


def join_kernel(has_extra, keep_feed, got_feed, keep_mixing, got_mixing, *rest):
    extra = rest[0] if has_extra else None
    joined, held, total, arrived, left = rest[-5:]
    height = SHARE + (EXTRA if has_extra else 0)
    loads = []
    for part, (keep, got) in enumerate(((keep_mixing, got_mixing), (keep_feed, got_feed))):
        for piece in range(4):
            rows = pl.ds(piece * CHUNK, CHUNK)
            slot = part * 4 + piece
            for side, source in enumerate((keep, got)):
                load = pltpu.make_async_copy(
                    source.at[rows, :], held.at[side, pl.ds(slot * CHUNK, CHUNK), :],
                    arrived.at[side, slot],
                )
                load.start()
                loads.append(load)
    stores = []
    shares = CHUNK // SHARE
    for slot in range(8):
        loads[2 * slot].wait()
        loads[2 * slot + 1].wait()
        for at in range(shares):
            share = slot * shares + at
            rows = slice(share * SHARE, (share + 1) * SHARE)
            total[share, :SHARE, :] = held[0, rows, :] + held[1, rows, :]
            if has_extra:
                total[share, SHARE:, :] = extra[...]
        store = pltpu.make_async_copy(
            total.at[pl.ds(slot * shares, shares)], joined.at[pl.ds(slot * shares, shares)],
            left.at[slot],
        )
        store.start()
        stores.append(store)
    for store in stores:
        store.wait()


def join_call(keep_feed, got_feed, keep_mixing, got_mixing, extra, *after):
    has_extra = extra is not None
    height = SHARE + (EXTRA if has_extra else 0)
    return pl.pallas_call(
        functools.partial(join_kernel, has_extra),
        out_shape=shape_of(BF, 32, height, 128),
        in_specs=any_specs(4) + vmem_specs(int(has_extra)) + any_specs(len(after)),
        out_specs=any_specs(1)[0],
        scratch_shapes=[
            pltpu.VMEM((2, PACKED, 128), BF),
            pltpu.VMEM((32, height, 128), BF),
            pltpu.SemaphoreType.DMA((2, 8)),
            pltpu.SemaphoreType.DMA((8,)),
        ],
        compiler_params=params(),
        name="join",
    )(keep_feed, got_feed, keep_mixing, got_mixing, *((extra,) if has_extra else ()), *after)


def gate_kernel(*refs):
    del refs


def gate(value, *after):
    return pl.pallas_call(
        gate_kernel,
        out_shape=shape_of(value.dtype, *value.shape),
        in_specs=any_specs(1 + len(after)),
        out_specs=any_specs(1)[0],
        input_output_aliases={0: 0},
        name="gate",
    )(value, *after)


def batch_groups():
    return [[2 * chip + core for chip in range(32)] for core in range(2)]


def core_swap(value):
    count = lax.axis_size("batch")
    return lax.ppermute(value, "batch", [(i, i ^ 1) for i in range(count)])


def section_swap(value):
    return lax.ppermute(value, "section", [(0, 1), (1, 0)])


def across_chips(value):
    return lax.all_to_all(value, "batch", 0, 0, axis_index_groups=batch_groups(), tiled=True)


def copied(shard):
    return across_chips(jnp.broadcast_to(shard[None], (32,) + shard.shape)).reshape(-1, 128)


def share_sum(arrived):
    return jnp.sum(arrived.astype(F32), axis=0).astype(BF)


def body(
    inputs, cotangent, text, text_mask, segments, time_index, time_table,
    w_qkv, w_out, w_query, w_keyval, w_cross, w_up, w_down, w_ada, b_ada,
):
    section = lax.axis_index("section")
    place = lax.axis_index("batch")
    core, chip = place % 2, place // 2
    first = section == 0

    weights = (w_qkv, w_out, w_query, w_keyval, w_cross, w_up, w_down)
    shard = section_swap(shard_call(place.astype(jnp.int32).reshape(1), weights))
    packed = pack_call(weights, shard)
    mine = copied(shard)

    frames = segments.reshape(MICRO, FRAMES, PATCHES)[:, :, 0]
    mask_row = text_mask.reshape(MICRO, TEXT)
    mask_column = text_mask.reshape(-1, 1)
    info = jnp.concatenate(
        [
            jnp.stack([section, core]),
            lax.dynamic_index_in_dim(frames, section, 0, keepdims=False),
        ]
    ).astype(jnp.int32)
    time_onehot = (time_index[:, None] == jnp.arange(STEPS)[None, :]).astype(BF)
    time_rows = mm(time_onehot, time_table)
    mod = mm(jax.nn.silu(time_rows).astype(BF), w_ada[0]) + b_ada
    mod_pairs = mod.reshape(MICRO, VIDS, 6 * D)
    mod_own = lax.dynamic_index_in_dim(mod_pairs, section, 0, keepdims=False)
    mod_other = section_swap(lax.dynamic_index_in_dim(mod_pairs, 1 - section, 0, keepdims=False))
    mod_other = gate(mod_other, packed)
    mods = (jnp.where(first, mod_own, mod_other), jnp.where(first, mod_other, mod_own))

    mine = gate(mine, packed, *mods)
    sources = (packed, mine, core_swap(mine))

    results = [None, None]
    (
        results[0], results[1], sent, d_text_one, d_mod_one,
        keep_feed, send_feed, keep_mixing, send_mixing, *kept,
    ) = first_call(info, inputs, cotangent, mods, text, mask_row, mask_column, sources)
    result_other = section_swap(jnp.where(first, results[1], results[0]))
    early = join_call(
        keep_feed, core_swap(send_feed), keep_mixing, core_swap(send_mixing), None
    )
    (
        d_first, given, d_text_low, d_mod_zero, keep_feed, send_feed, keep_mixing, send_mixing,
    ) = second_call(info, sent, mods[0], text, mask_column, d_text_one, sources, kept, early, result_other)
    early = across_chips(early)

    def by_clip(own, other):
        return jnp.concatenate([jnp.where(first, own, other), jnp.where(first, other, own)])

    d_mod_low = [member.astype(BF) for member in (d_mod_zero, d_mod_one)]
    packet = section_swap(
        jnp.concatenate([jnp.where(first, d_mod_low[1], d_mod_low[0]), d_text_low])
    )
    mod_rows = d_mod_low[0].shape[0]
    d_mod_clips = by_clip(
        jnp.where(first, d_mod_low[0], d_mod_low[1]), packet[:mod_rows]
    ).reshape(MICRO * VIDS, 6 * D)
    text_grad = by_clip(d_text_low, packet[mod_rows:]).astype(F32)
    digits = jnp.stack([time_index // 32, time_index % 32], axis=1).astype(BF)
    extra = jnp.concatenate(
        [d_mod_clips, time_rows.astype(BF), jnp.pad(digits, ((0, 0), (0, 126)))], axis=1
    ).reshape(EXTRA, 128)

    early = gate(early, given)
    late = across_chips(
        join_call(
            keep_feed, core_swap(send_feed), keep_mixing, core_swap(send_mixing), extra,
            early,
        )
    )
    early = share_sum(early)
    d_act_time = mm_nt(d_mod_clips, w_ada[0])
    unused, silu_back = jax.vjp(jax.nn.silu, time_rows)
    d_time_low = silu_back(d_act_time)[0].astype(BF)
    d_time_swapped = core_swap(d_time_low)
    d_time_own = jnp.where(
        core == 0,
        jnp.concatenate([d_time_low, d_time_swapped]),
        jnp.concatenate([d_time_swapped, d_time_low]),
    ).reshape(TIMES, 128)
    late = gate(late, d_time_own, early)
    last = share_sum(late[:, :SHARE])
    total = (
        jnp.concatenate([jnp.where(first, last, early), d_time_own]).astype(F32)
        + section_swap(jnp.concatenate([jnp.where(first, early, last), d_time_own])).astype(F32)
    ).astype(BF)
    full = jnp.broadcast_to(total[None], (32, SHARE + TIMES, 128))
    given_other = section_swap(gate(jnp.where(first, sent, given), full))
    full = across_chips(full)
    outputs = by_clip(jnp.where(first, results[0], results[1]), result_other)
    d_input = by_clip(
        jnp.where(first, d_first, sent.astype(F32)), given_other.astype(F32)
    )
    columns = late[:, SHARE:].reshape(4 * 32, -1)
    columns_other = core_swap(columns)
    every = jnp.concatenate([columns, columns_other])
    every_mod = every[:, : 6 * D]
    every_rows = every[:, 6 * D : 7 * D].astype(F32)

    def index_of(rows):
        pair = rows[:, 7 * D : 7 * D + 2].astype(jnp.int32)
        return (pair[:, 0] * 32 + pair[:, 1]).reshape(32, 4)

    index_mine, index_other = index_of(columns), index_of(columns_other)
    every_index = jnp.concatenate(
        [
            jnp.where(core == 0, index_mine, index_other),
            jnp.where(core == 0, index_other, index_mine),
        ],
        axis=1,
    ).reshape(-1)
    g_bias = jnp.sum(every_mod.astype(F32), axis=0)
    g_ada = mm_tn(jax.nn.silu(every_rows).astype(BF), every_mod)
    every_time = full[:, SHARE:].reshape(4 * 64, D)
    full = gate(full, g_ada, g_bias, given_other, outputs)
    full_other = core_swap(full)
    table_grad = mm_tn(
        (every_index[:, None] == jnp.arange(STEPS)[None, :]).astype(BF), every_time
    )
    grads = unpack_call(info, full, full_other)
    g_qkv, g_out, g_cross, g_query, g_keyval, g_up, g_down = grads
    return (
        outputs[None], d_input[None], text_grad, table_grad, g_qkv, g_out, g_query, g_keyval,
        g_cross, g_up, g_down, g_ada[None], g_bias[None],
    )


def solution(mesh):
    return jax.shard_map(
        body,
        mesh=mesh,
        in_specs=(
            P("batch", None),
            P("batch", None),
            P("batch", None),
            P("batch"),
            P("batch"),
            P("batch"),
            P(),
            P("section", None, None),
            P("section", None, None),
            P("section", None, None),
            P("section", None, None),
            P("section", None, None),
            P("section", None, None),
            P("section", None, None),
            P("section", None, None),
            P("section", None),
        ),
        out_specs=(
            P("section", "batch", None),
            P("section", "batch", None),
            P("batch", None),
            P(),
            P("section", None, None),
            P("section", None, None),
            P("section", None, None),
            P("section", None, None),
            P("section", None, None),
            P("section", None, None),
            P("section", None, None),
            P("section", None, None),
            P("section", None),
        ),
        check_vma=False,
    )
```
